128 devices in a mesh: ctx: 4 (over y_lo, core), fsdp: 32 (over z, x, y_hi).
Axes of the slice: x: 4, y: 4 (y_hi: 2, y_lo: 2; y = y_hi * 2 + y_lo), z: 4, core: 2. Of those that a mesh axis runs over, the one named last changes fastest.
Arguments:
- tokens: bfloat16 [32, 2, 4, 128, 896], P('fsdp', None, 'ctx'), may hold values from -6 to 6
- attn_gain: bfloat16 [896], P('fsdp'), may hold values from 0.5 to 1.5
- qkv_weight: bfloat16 [896, 1152], P('fsdp'), may hold values from -0.1875 to 0.1875
- qk_bias: bfloat16 [1024], P('fsdp'), may hold values from -3 to 3
- value_bias: bfloat16 [128], P('fsdp'), may hold values from -3 to 3
- out_weight: bfloat16 [896, 896], P('fsdp'), may hold values from -0.75 to 0.75
- mlp_gain: bfloat16 [896], P('fsdp'), may hold values from 0.5 to 1.5
- gate_weight: bfloat16 [896, 4864], P('fsdp'), may hold values from -0.1875 to 0.1875
- up_weight: bfloat16 [896, 4864], P('fsdp'), may hold values from -0.1875 to 0.1875
- down_weight: bfloat16 [4864, 896], P('fsdp'), may hold values from -0.078125 to 0.078125
- cotangent: bfloat16 [32, 2, 4, 128, 896], P('fsdp', None, 'ctx'), may hold values from -6 to 6
Outputs:
- mixed: bfloat16 [32, 2, 4, 128, 896], P('fsdp', None, 'ctx')
- token_grad: float32 [32, 2, 4, 128, 896], P('fsdp', None, 'ctx')
- attn_gain_grad: float32 [896], P('fsdp')
- qkv_weight_grad: float32 [896, 1152], P('fsdp')
- qk_bias_grad: float32 [1024], P('fsdp')
- value_bias_grad: float32 [128], P('fsdp')
- out_weight_grad: float32 [896, 896], P('fsdp')
- mlp_gain_grad: float32 [896], P('fsdp')
- gate_weight_grad: float32 [896, 4864], P('fsdp')
- up_weight_grad: float32 [896, 4864], P('fsdp')
- down_weight_grad: float32 [4864, 896], P('fsdp')
The draws below stay inside these ranges and needn't reach their ends.
All inputs are finite; a program needn't handle non-finite values.
Results may differ from the reference program's by a relative error of at most 0.04.
Values may be sent and summed in bfloat16 or wider, within the bound.
No kernel may reach another device: no remote copies, remote signals or barrier semaphores. Data moves between devices by JAX's collectives and lax.ppermute only.
A program may use at most 192 MiB of HBM per device.

```python
import jax
import jax.numpy as jnp
from jax import lax

D = 896
H = 14
KVH = 2
HD = 64
FF = 4864
BLK = 128
QW = 896
KW = 128
QKVW = 1152
SEQS = 32
N_CTX = 4


def block_scale(rng, dims, cuts, least, high):
    level = 1.0
    for position, blocks in cuts:
        heights = jax.random.uniform(jax.random.fold_in(jax.random.fold_in(rng, 6), position), (blocks,), jnp.float32, least / len(cuts), high / len(cuts))
        level = level * jnp.repeat(jnp.exp(heights), dims[position] // blocks).reshape((-1,) + (1,) * (len(dims) - 1 - position))
    return level


def noise(stream_key, dims, spread, most, shards=(), held_as=jnp.bfloat16):
    level = block_scale(stream_key, dims, shards, -0.22, 0.18) if shards else 1.0
    values = jax.random.normal(stream_key, dims, jnp.float32) * spread * level
    return jnp.minimum(jnp.maximum(values, -most), most).astype(held_as)


def setup_inputs(seed: int = 0) -> dict:
    keys = jax.random.split(jax.random.key(seed), 12)
    return {
        "tokens": noise(keys[0], (SEQS, 2, N_CTX, BLK, D), 1.0, 6.0, ((0, 32), (2, 4))),
        "attn_gain": jnp.clip(1.0 + 0.1 * jax.random.normal(keys[1], (D,), jnp.float32), 0.5, 1.5).astype(jnp.bfloat16),
        "qkv_weight": noise(keys[2], (D, QKVW), D ** -0.5, 0.1875, ((0, 32),)),
        "qk_bias": noise(keys[3], (QW + KW,), 0.5, 3.0, ((0, 32),)),
        "value_bias": noise(keys[4], (KW,), 0.5, 3.0, ((0, 32),)),
        "out_weight": noise(keys[5], (QW, D), (D // 16) ** -0.5, 0.75, ((0, 32),)),
        "mlp_gain": jnp.clip(1.0 + 0.1 * jax.random.normal(keys[6], (D,), jnp.float32), 0.5, 1.5).astype(jnp.bfloat16),
        "gate_weight": noise(keys[7], (D, FF), D ** -0.5, 0.1875, ((0, 32),)),
        "up_weight": noise(keys[8], (D, FF), D ** -0.5, 0.1875, ((0, 32),)),
        "down_weight": noise(keys[9], (FF, D), FF ** -0.5, 0.078125, ((0, 32),)),
        "cotangent": noise(keys[10], (SEQS, 2, N_CTX, BLK, D), 1.0, 6.0, ((0, 32), (2, 4))),
    }


EPSILON = 1e-06
THETA = 1000000.0
HIGHEST = lax.Precision.HIGHEST

@jax.custom_vjp
def low(v):
    return lax.optimization_barrier(v.astype(jnp.bfloat16)).astype(jnp.float32)

@jax.custom_vjp
def low_back(v):
    return v

def low_keep(v):
    return (low(v), None)

def low_pass(kept, grad):
    return (grad,)

def back_keep(v):
    return (v, None)

def back_low(kept, grad):
    return (low(grad),)
low.defvjp(low_keep, low_pass)
low_back.defvjp(back_keep, back_low)

def natural_order(blocks):
    return jnp.concatenate([blocks[0], blocks[1][::-1]], axis=0).reshape(-1, blocks.shape[-1])

def mirror_order(flat):
    pieces = flat.reshape(2 * N_CTX, BLK, flat.shape[-1])
    return jnp.stack([pieces[:N_CTX], pieces[N_CTX:][::-1]])

def rms_norm(values, gain):
    return values * lax.rsqrt(lax.optimization_barrier(jnp.mean(values * values, axis=-1, keepdims=True)) + EPSILON) * gain

def angles(positions):
    freqs = THETA ** (-(jnp.arange(HD // 2, dtype=jnp.float32) * 2.0 / HD))
    return positions.astype(jnp.float32)[:, None] * freqs[None, :]

def rotate(values, turns):
    half = values.shape[-1] // 2
    cosine = jnp.cos(turns)[:, None, :]
    sine = jnp.sin(turns)[:, None, :]
    first = values[..., :half]
    second = values[..., half:]
    return jnp.concatenate([first * cosine - second * sine, second * cosine + first * sine], axis=-1)

def layer(inputs, attn_gain, qkv_weight, qk_bias, value_bias, out_weight, mlp_gain, gate_weight, up_weight, down_weight):
    length = inputs.shape[0]
    q_width = H * HD
    k_width = KVH * HD
    normed_in = low(rms_norm(inputs, attn_gain))
    bias_full = jnp.concatenate([qk_bias, value_bias], axis=0)
    projected = low_back(jnp.dot(normed_in, qkv_weight, precision=HIGHEST) + bias_full)
    positions = jnp.arange(length, dtype=jnp.int32)
    turns = angles(positions)
    query = low(rotate(projected[:, :q_width].reshape(length, H, HD), turns))
    key_rows = low(rotate(projected[:, q_width:q_width + k_width].reshape(length, KVH, HD), turns))
    value_rows = low(projected[:, q_width + k_width:].reshape(length, KVH, HD))
    grouped = query.reshape(length, KVH, H // KVH, HD)
    scores = low_back(jnp.einsum('qgrd,kgd->grqk', grouped, key_rows, precision=HIGHEST) * HD ** (-0.5))
    causal = positions[:, None] >= positions[None, :]
    scores = jnp.where(causal, scores, -1e+30)
    softmax_out = jax.nn.softmax(scores, axis=-1)
    attn = jnp.einsum('grqk,kgd->qgrd', low(softmax_out), value_rows, precision=HIGHEST).reshape(length, q_width)
    attn = low(low_back(attn))
    hidden = inputs + low_back(jnp.dot(attn, out_weight, precision=HIGHEST))
    normed_mid = low(rms_norm(hidden, mlp_gain))
    gate = low_back(jnp.dot(normed_mid, gate_weight, precision=HIGHEST))
    up_rows = low_back(jnp.dot(normed_mid, up_weight, precision=HIGHEST))
    inner = low(jax.nn.silu(gate) * up_rows)
    return hidden + jnp.dot(inner, down_weight, precision=HIGHEST)

def reference(tokens, attn_gain, qkv_weight, qk_bias, value_bias, out_weight, mlp_gain, gate_weight, up_weight, down_weight, cotangent):
    params = tuple((item.astype(jnp.float32) for item in (attn_gain, qkv_weight, qk_bias, value_bias, out_weight, mlp_gain, gate_weight, up_weight, down_weight)))

    def one_sequence(totals, pair):
        seq_tokens, seq_cotangent = pair
        inputs = natural_order(seq_tokens.astype(jnp.float32))
        incoming = natural_order(seq_cotangent.astype(jnp.float32))
        result, pullback = jax.vjp(layer, inputs, *params)
        grads = pullback(incoming)
        totals = tuple((acc + grad for acc, grad in zip(totals, grads[1:])))
        return (totals, (mirror_order(result).astype(jnp.bfloat16), mirror_order(grads[0])))
    zeros = tuple((jnp.zeros(item.shape, jnp.float32) for item in params))
    totals, (mixed, token_grad) = lax.scan(one_sequence, zeros, (tokens, cotangent))
    return (mixed, token_grad, totals[0], totals[1], totals[2], totals[3], totals[4], totals[5], totals[6], totals[7], totals[8])
```

```python
import jax
import jax.numpy as jnp
from jax import lax
from jax.sharding import Mesh, PartitionSpec as P

H = 14
KVH = 2
HD = 64
REP = H // KVH
D = 896
FF = 4864
FFT = FF // 4
QC = REP * HD
PC = QC + 2 * HD
BLK = 128
EPSILON = 1e-06
THETA = 1000000.0
AXES = ("yl", "c", "z", "x", "yh")
BF = jnp.bfloat16
F32 = jnp.float32


def shift(value, axis, size, step):
    return lax.ppermute(value, axis, [(i, (i + step) % size) for i in range(size)])


def swap(value, axis):
    return shift(value, axis, 2, 1)


def angles(positions):
    freqs = THETA ** (-(jnp.arange(HD // 2, dtype=F32) * 2.0 / HD))
    return positions.astype(F32)[:, None] * freqs[None, :]


def rotate(values, cosine, sine):
    half = HD // 2
    first = values[..., :half]
    second = values[..., half:]
    return jnp.concatenate(
        [first * cosine - second * sine, second * cosine + first * sine], axis=-1
    )


def rows_inner(left, right):
    return lax.dot_general(left, right, (((0,), (0,)), ((), ())), preferred_element_type=F32)


def cols_inner(left, right):
    return lax.dot_general(left, right, (((1,), (1,)), ((), ())), preferred_element_type=F32)


def dot(left, right):
    return jnp.dot(left, right, preferred_element_type=F32)


def norm_back(grad_normed, normed, inverse):
    return inverse * (grad_normed - normed * jnp.mean(grad_normed * normed, axis=-1, keepdims=True))


def ordered(own, other, place):
    first = jnp.where(place == 0, own, other)
    second = jnp.where(place == 0, other, own)
    return first, second


def put(pieces, place, size):
    total = jnp.zeros((size,) + pieces[0].shape, pieces[0].dtype)
    for step, piece in enumerate(pieces):
        total = lax.dynamic_update_index_in_dim(total, piece, (place + step) % size, 0)
    return total


def gather4(own, axis, place):
    from_next = shift(own, axis, 4, 3)
    from_last = shift(own, axis, 4, 1)
    from_far = shift(own, axis, 4, 2)
    return put([own, from_next, from_far, from_last], place, 4)


def gather4_ring(own, axis, place):
    half = own.shape[0] // 2
    low, high = own[:half], own[half:]
    low_next, high_next = shift(low, axis, 4, 3), shift(high, axis, 4, 3)
    low_last, high_last = shift(low, axis, 4, 1), shift(high, axis, 4, 1)
    low_far = shift(low_last, axis, 4, 1)
    high_far = shift(high_next, axis, 4, 3)
    lows = put([low, low_next, low_far, low_last], place, 4)
    highs = put([high, high_next, high_far, high_last], place, 4)
    return jnp.concatenate([lows, highs], axis=1)


def scatter4(parts, axis, place):
    def part(step):
        return lax.dynamic_index_in_dim(parts, (place + step) % 4, 0, keepdims=False)

    to_next = shift(part(1), axis, 4, 1)
    to_last = shift(part(3), axis, 4, 3)
    to_far = shift(part(2), axis, 4, 2)
    total = part(0).astype(F32) + to_next.astype(F32) + to_last.astype(F32) + to_far.astype(F32)
    return total.astype(BF)


def scatter2(parts, axis, place):
    keep = lax.dynamic_index_in_dim(parts, place, 0, keepdims=False)
    give = lax.dynamic_index_in_dim(parts, 1 - place, 0, keepdims=False)
    return (keep.astype(F32) + swap(give, axis).astype(F32)).astype(BF)


def plane_from(own, root, place):
    roots = [(r // 2, r % 2, r) for r in range(4)]
    axes = ("yl", "c", "z")

    def flat(yl, c, z):
        return (yl * 2 + c) * 4 + z % 4

    up = lax.ppermute(own, axes, [(flat(a, b, r), flat(a, b, r + 1)) for a, b, r in roots])
    down = lax.ppermute(own, axes, [(flat(a, b, r), flat(a, b, r + 3)) for a, b, r in roots])
    half = own.shape[0] // 2
    far_low = lax.ppermute(
        up[:half], axes, [(flat(a, b, r + 1), flat(a, b, r + 2)) for a, b, r in roots]
    )
    far_high = lax.ppermute(
        down[half:], axes, [(flat(a, b, r + 3), flat(a, b, r + 2)) for a, b, r in roots]
    )
    far = jnp.concatenate([far_low, far_high], axis=0)
    step = (place - root) % 4
    return jnp.where(step == 0, own, jnp.where(step == 1, up, jnp.where(step == 3, down, far)))


def plane_to(own, root, place):
    roots = [(r // 2, r % 2, r) for r in range(4)]
    axes = ("yl", "c", "z")

    def flat(yl, c, z):
        return (yl * 2 + c) * 4 + z % 4

    half = own.shape[0] // 2
    far_low = lax.ppermute(
        own[:half], axes, [(flat(a, b, r + 2), flat(a, b, r + 1)) for a, b, r in roots]
    )
    far_high = lax.ppermute(
        own[half:], axes, [(flat(a, b, r + 2), flat(a, b, r + 3)) for a, b, r in roots]
    )
    joined = own.astype(F32) + jnp.concatenate(
        [far_low.astype(F32), far_high.astype(F32)], axis=0
    )
    joined = joined.astype(BF)
    from_up = lax.ppermute(joined, axes, [(flat(a, b, r + 1), flat(a, b, r)) for a, b, r in roots])
    from_down = lax.ppermute(
        joined, axes, [(flat(a, b, r + 3), flat(a, b, r)) for a, b, r in roots]
    )
    return (own.astype(F32) + from_up.astype(F32) + from_down.astype(F32)).astype(BF)


def shards(
    tokens,
    attn_gain,
    qkv_weight,
    qk_bias,
    value_bias,
    out_weight,
    mlp_gain,
    gate_weight,
    up_weight,
    down_weight,
    cotangent,
):
    yl, c, z, x, yh = [lax.axis_index(name) for name in AXES]
    ctx = yl * 2 + c
    scale = HD ** (-0.5)
    rows = 2 * BLK

    tok = tokens.reshape(rows, D)
    tok_two = jnp.concatenate([tok, swap(tok, "c")], axis=0)
    q_w = D * 1
    qkv_part = jnp.concatenate(
        [
            lax.dynamic_slice_in_dim(qkv_weight, c * QC, QC, 1),
            lax.dynamic_slice_in_dim(qkv_weight, q_w + c * HD, HD, 1),
            lax.dynamic_slice_in_dim(qkv_weight, q_w + KVH * HD + c * HD, HD, 1),
        ],
        axis=1,
    )
    vectors = jnp.concatenate([attn_gain, mlp_gain, qk_bias, value_bias])
    vec_count = vectors.shape[0]
    vec_rows = jnp.zeros((4, PC), BF).at[0, :vec_count].set(vectors)
    packed = jnp.concatenate([qkv_part, vec_rows], axis=0)
    low, high = ordered(packed, swap(packed, "yh"), yh)
    packed = jnp.concatenate([low[:28], high[:28], low[28:], high[28:]], axis=0)
    packed = gather4(packed, "x", x)
    packed = gather4(packed, "z", z)
    qkv_half = packed[:, :, :56].reshape(D, PC)
    vec_all = packed[:, :, 56::4, :vec_count].reshape(32, vec_count).astype(F32)
    gain_one = vec_all[:, :28].reshape(D)
    gain_two = vec_all[:, 28:56].reshape(D)
    qk_bias_full = vec_all[:, 56:88].reshape(D + KVH * HD)
    value_bias_full = vec_all[:, 88:].reshape(KVH * HD)
    bias_part = jnp.concatenate(
        [
            lax.dynamic_slice_in_dim(qk_bias_full, c * QC, QC, 0),
            lax.dynamic_slice_in_dim(qk_bias_full, D + c * HD, HD, 0),
            lax.dynamic_slice_in_dim(value_bias_full, c * HD, HD, 0),
        ]
    )

    def czflat(cc, zz):
        return cc * 4 + zz % 4

    near = lax.ppermute(
        out_weight,
        ("c", "z"),
        [(czflat(a, 2 * a + b), czflat(a, 2 * a + 1 - b)) for a in (0, 1) for b in (0, 1)],
    )
    cross = lax.ppermute(
        out_weight,
        ("c", "z"),
        [(czflat(a, 2 * a), czflat(a, 2 * a + 3)) for a in (0, 1)]
        + [(czflat(a, 2 * a + 1), czflat(a, 2 * a + 2)) for a in (0, 1)],
    )
    cross_near = lax.ppermute(
        cross,
        ("c", "z"),
        [(czflat(a, 2 * a + 3), czflat(a, 2 * a + 2)) for a in (0, 1)]
        + [(czflat(a, 2 * a + 2), czflat(a, 2 * a + 3)) for a in (0, 1)],
    )
    inside = (z // 2) == c
    first_plane = jnp.where(
        inside, jnp.where(z % 2 == 0, out_weight, near), jnp.where(z % 2 == 1, cross, cross_near)
    )
    second_plane = jnp.where(
        inside, jnp.where(z % 2 == 1, out_weight, near), jnp.where(z % 2 == 0, cross, cross_near)
    )
    planes = jnp.stack([first_plane, second_plane])
    low, high = ordered(planes, swap(planes, "yh"), yh)
    planes = jnp.concatenate([low, high], axis=1)
    out_half = jnp.swapaxes(gather4(planes, "x", x), 0, 1).reshape(QC, D)

    gate_part = lax.dynamic_slice_in_dim(gate_weight, ctx * FFT, FFT, 1)
    up_part = lax.dynamic_slice_in_dim(up_weight, ctx * FFT, FFT, 1)
    both = jnp.concatenate([gate_part, up_part], axis=0)
    low, high = ordered(both, swap(both, "yh"), yh)
    gate_part = jnp.concatenate([low[:28], high[:28]], axis=0)
    up_part = jnp.concatenate([low[28:], high[28:]], axis=0)
    gate_t = gather4_ring(gather4(gate_part, "x", x), "z", z).reshape(D, FFT)
    up_rows = gather4(up_part, "z", z)
    up_t = jnp.swapaxes(gather4_ring(up_rows, "x", x), 0, 1).reshape(D, FFT)
    down_part = plane_from(down_weight, ctx, z)
    low, high = ordered(down_part, swap(down_part, "yh"), yh)
    down_part = jnp.concatenate([low, high], axis=0)
    down_t = gather4_ring(down_part, "x", x).reshape(FFT, D)

    offsets = jnp.arange(BLK, dtype=jnp.int32)

    def place_of(place):
        return jnp.concatenate([place * BLK + offsets, (7 - place) * BLK + offsets])

    other_c = yl * 2 + 1 - c
    query_pos = jnp.concatenate([place_of(ctx), place_of(other_c)])
    far_pos = jnp.concatenate([place_of((1 - yl) * 2 + c), place_of((1 - yl) * 2 + 1 - c)])
    key_pos = jnp.concatenate([query_pos, far_pos])
    turns = angles(query_pos)
    cosine, sine = jnp.cos(turns)[:, None, :], jnp.sin(turns)[:, None, :]
    inputs_two = tok_two.astype(F32)
    inverse_one = lax.rsqrt(jnp.mean(inputs_two * inputs_two, axis=-1, keepdims=True) + EPSILON)
    normed_one = inputs_two * inverse_one
    normed_in = (normed_one * gain_one).astype(BF)
    projected = dot(normed_in, qkv_half) + bias_part
    queries = rotate(projected[:, :QC].reshape(2 * rows, REP, HD), cosine, sine).astype(BF)
    key_own = rotate(projected[:, None, QC : QC + HD], cosine, sine)[:, 0].astype(BF)
    value_own = projected[:, QC + HD :].astype(BF)
    kv_own = jnp.concatenate([key_own, value_own], axis=1)
    kv = jnp.concatenate([kv_own, swap(kv_own, "yl")], axis=0)
    keys, values = kv[:, :HD], kv[:, HD:]
    causal = query_pos[:, None] >= key_pos[None, :]
    scores = jnp.einsum("qrd,kd->rqk", queries, keys, preferred_element_type=F32) * scale
    scores = jnp.where(causal, scores, -1e30)
    row_max = jnp.max(scores, axis=-1, keepdims=True)
    exp_scores = jnp.exp(scores - row_max)
    row_total = jnp.sum(exp_scores, axis=-1, keepdims=True)
    prob = exp_scores / row_total
    log_total = row_max + jnp.log(row_total)
    attn = jnp.einsum("rqk,kd->qrd", prob.astype(BF), values, preferred_element_type=F32)
    attn = attn.reshape(2 * rows, QC).astype(BF)
    branch = dot(attn, out_half)
    inputs = inputs_two[:rows]
    hidden = inputs + branch[:rows] + swap(branch[rows:].astype(BF), "c").astype(F32)

    def ctx_gather(own):
        far = swap(own, "yl")
        return jnp.concatenate([own, swap(own, "c"), far, swap(far, "c")], axis=0)

    def ctx_sum(parts):
        parts = parts.reshape(4, rows, D)
        given = swap(jnp.stack([parts[1], parts[3]]).astype(BF), "c").astype(F32)
        far = swap((parts[2] + given[1]).astype(BF), "yl").astype(F32)
        return parts[0] + given[0] + far

    inverse_two = lax.rsqrt(jnp.mean(hidden * hidden, axis=-1, keepdims=True) + EPSILON)
    normed_two = hidden * inverse_two
    normed_mid = ctx_gather((normed_two * gain_two).astype(BF))
    out_grad = cotangent.reshape(rows, D)
    out_grads = ctx_gather(out_grad)
    gate_pre = dot(normed_mid, gate_t)
    up_pre = dot(normed_mid, up_t)
    sigmoid_gate = jax.nn.sigmoid(gate_pre)
    silu_gate = gate_pre * sigmoid_gate
    inner = (silu_gate * up_pre).astype(BF)
    inner_grad = cols_inner(out_grads, down_t)
    gate_grad = (
        inner_grad * up_pre * sigmoid_gate * (1.0 + gate_pre * (1.0 - sigmoid_gate))
    ).astype(BF)
    up_grad = (inner_grad * silu_gate).astype(BF)
    mid_grad = ctx_sum(cols_inner(gate_grad, gate_t) + cols_inner(up_grad, up_t))
    mixed = (hidden + ctx_sum(dot(inner, down_t))).astype(BF)

    down_wgrad = rows_inner(inner, out_grads).astype(BF).reshape(4, 2, 152, D)
    gate_wgrad = rows_inner(normed_mid, gate_grad).astype(BF).reshape(4, 4, 2, 28, FFT)
    up_wgrad = rows_inner(normed_mid, up_grad).astype(BF).reshape(4, 4, 2, 28, FFT)
    down_sum = scatter2(scatter4(down_wgrad, "x", x), "yh", yh)
    down_sum = plane_to(down_sum, ctx, z)
    gate_sum = scatter4(scatter4(gate_wgrad, "z", z), "x", x)
    up_sum = scatter4(scatter4(jnp.swapaxes(up_wgrad, 0, 1), "x", x), "z", z)
    both_sum = scatter2(jnp.concatenate([gate_sum, up_sum], axis=1), "yh", yh)

    def quarters(own):
        near_own = swap(own, "c")
        low, high = ordered(own, near_own, c)
        pair = jnp.stack([low, high])
        low, high = ordered(pair, swap(pair, "yl"), yl)
        return jnp.concatenate([low, high], axis=0)

    both_all = quarters(both_sum).astype(F32)
    both_all = jnp.swapaxes(both_all, 0, 1).reshape(56, FF)
    down_yl = jnp.where(z // 2 == yl, down_sum, swap(down_sum, "yl"))
    down_own = jnp.where(z % 2 == c, down_yl, swap(down_yl, "c")).astype(F32)

    gain_two_grad = jnp.sum(mid_grad * normed_two, axis=0)
    hidden_grad = out_grad.astype(F32) + norm_back(mid_grad * gain_two, normed_two, inverse_two)
    branch_grad = hidden_grad.astype(BF)
    branch_grad = jnp.concatenate([branch_grad, swap(branch_grad, "c")], axis=0)
    out_wgrad = rows_inner(attn, branch_grad).astype(BF).reshape(2, 4, 2, 28, D)
    attn_grad = cols_inner(branch_grad, out_half).astype(BF)
    grad_heads = attn_grad.reshape(2 * rows, REP, HD)
    scores = jnp.einsum("qrd,kd->rqk", queries, keys, preferred_element_type=F32) * scale
    prob = jnp.exp(jnp.where(causal, scores, -1e30) - log_total)
    prob_grad = jnp.einsum("qrd,kd->rqk", grad_heads, values, preferred_element_type=F32)
    weighted = jnp.sum(prob * prob_grad, axis=-1, keepdims=True)
    score_grad = (prob * (prob_grad - weighted)).astype(BF)
    query_grad = jnp.einsum("rqk,kd->qrd", score_grad, keys, preferred_element_type=F32) * scale
    key_grad = jnp.einsum("rqk,qrd->kd", score_grad, queries, preferred_element_type=F32) * scale
    value_grad = jnp.einsum("rqk,qrd->kd", prob.astype(BF), grad_heads, preferred_element_type=F32)
    kv_grad = jnp.concatenate([key_grad, value_grad], axis=1)
    kv_grad = kv_grad[: 2 * rows] + swap(kv_grad[2 * rows :].astype(BF), "yl").astype(F32)
    query_back = rotate(query_grad, cosine, -sine).reshape(2 * rows, QC)
    key_back = rotate(kv_grad[:, None, :HD], cosine, -sine)[:, 0]
    projected_grad = jnp.concatenate([query_back, key_back, kv_grad[:, HD:]], axis=1).astype(BF)
    qkv_wgrad = rows_inner(normed_in, projected_grad).astype(BF)
    bias_grad = jnp.sum(projected_grad.astype(F32), axis=0)
    in_part = cols_inner(projected_grad, qkv_half)
    in_grad = in_part[:rows] + swap(in_part[rows:].astype(BF), "c").astype(F32)
    normed_own = normed_one[:rows]
    gain_one_grad = jnp.sum(in_grad * normed_own, axis=0)
    input_grad = hidden_grad + norm_back(in_grad * gain_one, normed_own, inverse_one[:rows])

    out_sum = scatter2(scatter4(jnp.swapaxes(out_wgrad, 0, 1), "x", x).swapaxes(0, 1), "yh", yh)
    cross_sum = lax.ppermute(
        out_sum,
        ("c", "z"),
        [(czflat(a, 2 * a + 3), czflat(a, 2 * a + 2)) for a in (0, 1)]
        + [(czflat(a, 2 * a + 2), czflat(a, 2 * a + 3)) for a in (0, 1)],
    )
    mine = jnp.where(z % 2 == 1, out_sum[0], out_sum[1]).astype(F32)
    theirs = jnp.where(z % 2 == 1, cross_sum[0], cross_sum[1]).astype(F32)
    collected = (mine + theirs).astype(BF)
    from_out = lax.ppermute(
        collected,
        ("c", "z"),
        [(czflat(a, 2 * a + 3), czflat(a, 2 * a)) for a in (0, 1)]
        + [(czflat(a, 2 * a + 2), czflat(a, 2 * a + 1)) for a in (0, 1)],
    )
    keep = jnp.where(z % 2 == 0, out_sum[0], out_sum[1]).astype(F32)
    give = jnp.where(z % 2 == 0, out_sum[1], out_sum[0])
    from_pair = lax.ppermute(
        give,
        ("c", "z"),
        [(czflat(a, 2 * a + b), czflat(a, 2 * a + 1 - b)) for a in (0, 1) for b in (0, 1)],
    )
    out_own = (keep + from_out.astype(F32) + from_pair.astype(F32)).astype(BF)
    out_own = jnp.where(z // 2 == c, out_own, swap(out_own, "c")).astype(F32)
    out_own = out_own + swap(out_own.astype(BF), "yl").astype(F32)

    zeros_qk = jnp.zeros((D + KVH * HD,), F32)
    qk_grad = lax.dynamic_update_slice(zeros_qk, bias_grad[:QC], (c * QC,))
    qk_grad = lax.dynamic_update_slice(qk_grad, bias_grad[QC : QC + HD], (D + c * HD,))
    value_grad_bias = lax.dynamic_update_slice(
        jnp.zeros((KVH * HD,), F32), bias_grad[QC + HD :], (c * HD,)
    )
    vec_grads = jnp.concatenate(
        [
            gain_one_grad.reshape(32, 28),
            gain_two_grad.reshape(32, 28),
            qk_grad.reshape(32, 32),
            value_grad_bias.reshape(32, 4),
        ],
        axis=1,
    ).astype(BF)
    vec_rows = jnp.zeros((16, 2, 4, PC), BF).at[:, :, 0, :vec_count].set(
        vec_grads.reshape(16, 2, vec_count)
    )
    packed_grad = jnp.concatenate(
        [qkv_wgrad.reshape(16, 56, PC), vec_rows.reshape(16, 8, PC)], axis=1
    ).reshape(4, 4, 64, PC)
    packed_sum = scatter4(scatter4(packed_grad, "z", z), "x", x)
    packed_sum = scatter2(
        jnp.stack(
            [
                jnp.concatenate([packed_sum[:28], packed_sum[56:60]], axis=0),
                jnp.concatenate([packed_sum[28:56], packed_sum[60:]], axis=0),
            ]
        ),
        "yh",
        yh,
    )
    packed_sum = packed_sum.astype(F32) + swap(packed_sum, "yl").astype(F32)
    low, high = ordered(packed_sum, swap(packed_sum.astype(BF), "c").astype(F32), c)
    qkv_own = jnp.concatenate(
        [
            low[:28, :QC],
            high[:28, :QC],
            low[:28, QC : QC + HD],
            high[:28, QC : QC + HD],
            low[:28, QC + HD :],
            high[:28, QC + HD :],
        ],
        axis=1,
    )
    vec_own = low[28, :vec_count] + high[28, :vec_count]

    return (
        mixed.reshape(tokens.shape),
        input_grad.reshape(tokens.shape),
        vec_own[:28],
        qkv_own,
        vec_own[56:88],
        vec_own[88:],
        out_own,
        vec_own[28:56],
        both_all[:28],
        both_all[28:],
        down_own,
    )


def solution(mesh):
    devices = mesh.devices.reshape(2, 2, 4, 4, 2)
    split = Mesh(devices, AXES)
    ctx, fsdp = ("yl", "c"), ("z", "x", "yh")
    rows = P(fsdp, None, ctx, None, None)
    in_specs = (
        rows,
        P(fsdp),
        P(fsdp, None),
        P(fsdp),
        P(fsdp),
        P(fsdp, None),
        P(fsdp),
        P(fsdp, None),
        P(fsdp, None),
        P(fsdp, None),
        rows,
    )
    out_specs = (
        rows,
        rows,
        P(fsdp),
        P(fsdp, None),
        P(fsdp),
        P(fsdp),
        P(fsdp, None),
        P(fsdp),
        P(fsdp, None),
        P(fsdp, None),
        P(fsdp, None),
    )
    return jax.shard_map(
        shards, mesh=split, in_specs=in_specs, out_specs=out_specs, check_vma=False
    )
```

```python
import jax
import jax.numpy as jnp
from jax import lax
from jax.experimental import pallas as pl
from jax.experimental.pallas import tpu as pltpu
from jax.sharding import Mesh, PartitionSpec as P

KVH = 2
HD = 64
REP = 7
D = 896
FF = 4864
FFT = FF // 4
CH = 256
CHUNKS = 5
FFP = CH * CHUNKS
QC = REP * HD
STACK = REP * 128
PC = QC + 2 * HD
PACK = PC + QC
BLK = 128
EPSILON = 1e-06
THETA = 1000000.0
AXES = ("yl", "c", "z", "x", "yh")
BF = jnp.bfloat16
F32 = jnp.float32


def shift(value, axis, size, step):
    return lax.ppermute(value, axis, [(i, (i + step) % size) for i in range(size)])


def swap(value, axis):
    return shift(value, axis, 2, 1)


def angles(positions):
    freqs = THETA ** (-(jnp.arange(HD // 2, dtype=F32) * 2.0 / HD))
    return positions.astype(F32)[:, None] * freqs[None, :]


def rows_inner(left, right):
    return lax.dot_general(left, right, (((0,), (0,)), ((), ())), preferred_element_type=F32)


def cols_inner(left, right):
    return lax.dot_general(left, right, (((1,), (1,)), ((), ())), preferred_element_type=F32)


def dot(left, right):
    return jnp.dot(left, right, preferred_element_type=F32)


def norm_back(grad_normed, normed, inverse):
    return inverse * (grad_normed - normed * jnp.mean(grad_normed * normed, axis=-1, keepdims=True))


def ordered(own, other, place):
    first = jnp.where(place == 0, own, other)
    second = jnp.where(place == 0, other, own)
    return first, second


def spread4(parts, axis, place):
    def part(step):
        return lax.dynamic_index_in_dim(parts, (place + step) % 4, 0, keepdims=False)

    return [
        part(0),
        shift(part(1), axis, 4, 1),
        shift(part(3), axis, 4, 3),
        shift(part(2), axis, 4, 2),
    ]


def total4(pieces):
    return sum(piece.astype(F32) for piece in pieces).astype(BF)


def scatter2(parts, axis, place):
    keep = lax.dynamic_index_in_dim(parts, place, 0, keepdims=False)
    give = lax.dynamic_index_in_dim(parts, 1 - place, 0, keepdims=False)
    return (keep.astype(F32) + swap(give, axis).astype(F32)).astype(BF)


def after(value, *others):
    return lax.optimization_barrier((value,) + others)[0]


def quarter_kernel(ctx_ref, gate_ref, up_ref, out_ref):
    out_ref[...] = jnp.zeros_like(out_ref)
    for t in range(4):

        @pl.when(ctx_ref[0] == t)
        def _():
            for which, ref in enumerate((gate_ref, up_ref)):
                for run in range(16):
                    source, place, left = 304 * run + 76 * t, 80 * run, 76
                    while left:
                        size = min(left, CH - place % CH)
                        target = place // CH * 2 * CH + which * CH + place % CH
                        out_ref[:, target : target + size] = ref[:, source : source + size]
                        source, place, left = source + size, place + size, left - size


def quarter(ctx, gate, up):
    smem = pl.BlockSpec(memory_space=pltpu.SMEM)
    vmem = pl.BlockSpec(memory_space=pltpu.VMEM)
    return pl.pallas_call(
        quarter_kernel,
        in_specs=[smem, vmem, vmem],
        out_shape=jax.ShapeDtypeStruct((gate.shape[0], 2 * FFP), BF),
        cost_estimate=pl.CostEstimate(flops=0, bytes_accessed=2**20, transcendentals=0),
        name="quarter",
    )(ctx, gate, up)


def tiles_down(part):
    return part.reshape(10, 8, 7, 128).transpose(2, 1, 0, 3).reshape(56, FFP)


def tiles_up(parts):
    parts = parts.reshape(16, 7, 8, 10, 128).transpose(0, 3, 2, 1, 4)
    return parts.reshape(FFP, D)


PARTS = 4


def mlp_kernel(*refs):
    rows_refs, grads_refs = refs[:PARTS], refs[PARTS : 2 * PARTS]
    gu_ref, down_ref, inner_ref, gu_grad_ref, out_ref, mid_ref = refs[2 * PARTS : -4]
    gu, down, inner_all, gu_grad_all = refs[-4:]
    step = pl.program_id(0)
    size = rows_refs[0].shape[0]
    for j in range(CHUNKS):

        @pl.when(step == j)
        def _():
            gate_w, up_w, down_w = gu_ref[:, :CH], gu_ref[:, CH:], down_ref[...]
            gu[:, 2 * CH * j : 2 * CH * (j + 1)] = gu_ref[...]
            down[CH * j : CH * (j + 1), :] = down_w
            for p in range(PARTS):
                span = slice(p * size, (p + 1) * size)
                gate = dot(rows_refs[p][...], gate_w)
                up = dot(rows_refs[p][...], up_w)
                inner_grad = cols_inner(grads_refs[p][...], down_w)
                sigma = 0.5 + 0.5 * jnp.tanh(0.5 * gate)
                silu = gate * sigma
                inner = (silu * up).astype(BF)
                slope = sigma + silu - silu * sigma
                gate_grad = (inner_grad * up * slope).astype(BF)
                up_grad = (inner_grad * silu).astype(BF)
                inner_ref[span, :] = inner
                inner_all[span, CH * j : CH * (j + 1)] = inner
                gu_grad_ref[span, :CH] = gate_grad
                gu_grad_ref[span, CH:] = up_grad
                gu_grad_all[span, 2 * CH * j : 2 * CH * j + CH] = gate_grad
                gu_grad_all[span, 2 * CH * j + CH : 2 * CH * (j + 1)] = up_grad

    @pl.when(step >= CHUNKS)
    def _():
        start = pl.multiple_of((step - CHUNKS) * size, size)
        out_ref[...] = dot(inner_all[pl.ds(start, size), :], down[...]).astype(BF)
        mid_ref[...] = cols_inner(gu_grad_all[pl.ds(start, size), :], gu[...]).astype(BF)


def mlp(rows, grads, weights, down):
    size = rows[0].shape[0]
    count = PARTS * size
    whole = pl.BlockSpec((size, D), lambda j: (0, 0))

    def chunk(j):
        return jnp.minimum(j, CHUNKS - 1)

    part = pl.BlockSpec((size, D), lambda j: (jnp.maximum(j - CHUNKS, 0), 0))
    return pl.pallas_call(
        mlp_kernel,
        grid=(CHUNKS + PARTS,),
        in_specs=[
            *[whole] * (2 * PARTS),
            pl.BlockSpec((D, 2 * CH), lambda j: (0, chunk(j))),
            pl.BlockSpec((CH, D), lambda j: (chunk(j), 0)),
        ],
        out_specs=[
            pl.BlockSpec((count, CH), lambda j: (0, chunk(j))),
            pl.BlockSpec((count, 2 * CH), lambda j: (0, chunk(j))),
            part,
            part,
        ],
        out_shape=[
            jax.ShapeDtypeStruct((count, FFP), BF),
            jax.ShapeDtypeStruct((count, 2 * FFP), BF),
            jax.ShapeDtypeStruct((count, D), BF),
            jax.ShapeDtypeStruct((count, D), BF),
        ],
        scratch_shapes=[
            pltpu.VMEM((D, 2 * FFP), BF),
            pltpu.VMEM((FFP, D), BF),
            pltpu.VMEM((count, FFP), BF),
            pltpu.VMEM((count, 2 * FFP), BF),
        ],
        compiler_params=pltpu.CompilerParams(vmem_limit_bytes=56 * 2**20),
        cost_estimate=pl.CostEstimate(
            flops=12 * count * D * FFP, bytes_accessed=20 * 2**20, transcendentals=count * FFP
        ),
        name="mlp",
    )(*rows, *grads, weights, down)


def gu_wgrad_kernel(*refs):
    grad_ref, out_ref, turned_rows = refs[PARTS:]
    size = refs[0].shape[0]

    @pl.when(pl.program_id(0) == 0)
    def _():
        for p in range(PARTS):
            turned_rows[:, p * size : (p + 1) * size] = jnp.transpose(refs[p][...])

    out_ref[...] = dot(turned_rows[...], grad_ref[...]).astype(BF).reshape(out_ref.shape)


def gu_wgrad(rows, grad):
    count = grad.shape[0]
    return pl.pallas_call(
        gu_wgrad_kernel,
        grid=(CHUNKS,),
        in_specs=[
            *[pl.BlockSpec((count // PARTS, D), lambda j: (0, 0))] * PARTS,
            pl.BlockSpec((count, 2 * CH), lambda j: (0, j)),
        ],
        out_specs=pl.BlockSpec((4, D // 4, 2 * CH), lambda j: (0, 0, j)),
        out_shape=jax.ShapeDtypeStruct((4, D // 4, 2 * FFP), BF),
        scratch_shapes=[pltpu.VMEM((D, count), BF)],
        compiler_params=pltpu.CompilerParams(vmem_limit_bytes=48 * 2**20),
        cost_estimate=pl.CostEstimate(
            flops=4 * count * D * FFP, bytes_accessed=12 * 2**20, transcendentals=0
        ),
        name="gu_wgrad",
    )(*rows, grad)


def down_wgrad_kernel(inner_ref, *refs):
    grads = jnp.concatenate([ref[...] for ref in refs[:PARTS]], axis=0)
    refs[PARTS][...] = rows_inner(inner_ref[...], grads).astype(BF)


def down_wgrad(inner, grads):
    count = inner.shape[0]
    return pl.pallas_call(
        down_wgrad_kernel,
        grid=(CHUNKS,),
        in_specs=[
            pl.BlockSpec((count, CH), lambda j: (0, j)),
            *[pl.BlockSpec((count // PARTS, D), lambda j: (0, 0))] * PARTS,
        ],
        out_specs=pl.BlockSpec((CH, D), lambda j: (j, 0)),
        out_shape=jax.ShapeDtypeStruct((FFP, D), BF),
        compiler_params=pltpu.CompilerParams(vmem_limit_bytes=32 * 2**20),
        cost_estimate=pl.CostEstimate(
            flops=2 * count * D * FFP, bytes_accessed=8 * 2**20, transcendentals=0
        ),
        name="down_wgrad",
    )(inner, *grads)


ORDER = (0, 7, 1, 6, 2, 5, 3, 4)
LENGTHS = {1: (0, 0), 8: (1, 0), 2: (2, 0), 7: (3, 0), 3: (0, 1), 6: (1, 1), 4: (2, 1), 5: (3, 1)}


def turned(value, cosine, sine):
    first, second = value[: HD // 2], value[HD // 2 :]
    return jnp.concatenate(
        [first * cosine - second * sine, second * cosine + first * sine], axis=0
    )


def project_kernel(
    tok_ref, packed_ref, gain_ref, bias_ref, cos_ref, sin_ref, rows_ref, query_ref, kv_ref, weight
):
    for s in range(16):
        weight[56 * s : 56 * s + 56, :] = packed_ref[s, :56, :PC]
    inputs = tok_ref[...].astype(F32)
    inverse = lax.rsqrt(jnp.mean(inputs * inputs, axis=-1, keepdims=True) + EPSILON)
    rows = (inputs * inverse * gain_ref[...]).astype(BF)
    rows_ref[...] = rows
    projected = dot(rows, weight[...]) + bias_ref[...]
    for b in range(4):
        cosine, sine = cos_ref[b], sin_ref[b]
        block = projected[b * BLK : (b + 1) * BLK]
        for pair in range(4):
            both = jnp.transpose(block[:, 2 * HD * pair : 2 * HD * (pair + 1)])
            head = turned(both[:HD], cosine, sine).astype(BF)
            query_ref[b, :, 2 * pair * BLK : (2 * pair + 1) * BLK] = head
            other = turned(both[HD:], cosine, sine)
            if pair < 3:
                query_ref[b, :, (2 * pair + 1) * BLK : (2 * pair + 2) * BLK] = other.astype(BF)
            else:
                value = block[:, QC + HD :]
                kv_ref[b * BLK : (b + 1) * BLK, :] = jnp.concatenate(
                    [jnp.transpose(other), value], axis=1
                ).astype(BF)


def project(tok, packed, gain, bias, cosine, sine):
    return pl.pallas_call(
        project_kernel,
        out_shape=[
            jax.ShapeDtypeStruct((4 * BLK, D), BF),
            jax.ShapeDtypeStruct((4, HD, STACK), BF),
            jax.ShapeDtypeStruct((4 * BLK, 2 * HD), BF),
        ],
        scratch_shapes=[pltpu.VMEM((D, PC), BF)],
        compiler_params=pltpu.CompilerParams(vmem_limit_bytes=32 * 2**20),
        cost_estimate=pl.CostEstimate(
            flops=2 * 4 * BLK * D * PC, bytes_accessed=6 * 2**20, transcendentals=0
        ),
        name="project",
    )(tok, packed, gain, bias, cosine, sine)


def split_kv(kv_ref, keys, values):
    for place, block in enumerate(ORDER):
        rows = kv_ref[place * BLK : (place + 1) * BLK, :]
        keys[block * BLK : (block + 1) * BLK, :] = rows[:, :HD]
        values[block * BLK : (block + 1) * BLK, :] = rows[:, HD:]


def masked_scores(keys, query, length):
    scores = dot(keys[: length * BLK, :], query) * HD ** (-0.5)
    key = lax.broadcasted_iota(jnp.int32, (BLK, STACK), 0)
    token = lax.rem(lax.broadcasted_iota(jnp.int32, (BLK, STACK), 1), BLK)
    last = jnp.where(key <= token, scores[(length - 1) * BLK :], -1e30)
    if length == 1:
        return last
    return jnp.concatenate([scores[: (length - 1) * BLK], last], axis=0)


def heads_out(stacked, ref, block):
    rows = slice(block * BLK, (block + 1) * BLK)
    for pair in range(3):
        first = stacked[:, 2 * pair * BLK : (2 * pair + 1) * BLK]
        second = stacked[:, (2 * pair + 1) * BLK : (2 * pair + 2) * BLK]
        both = jnp.transpose(jnp.concatenate([first, second], axis=0))
        ref[rows, 2 * HD * pair : 2 * HD * (pair + 1)] = both.astype(ref.dtype)
    ref[rows, 6 * HD :] = jnp.transpose(stacked[:, 6 * BLK :]).astype(ref.dtype)


def attend_kernel(chip_ref, query_ref, kv_ref, out_ref, attn_ref, total_ref, branch_ref, keys, values):
    split_kv(kv_ref, keys, values)
    for length, (block, chip) in LENGTHS.items():

        @pl.when(chip_ref[0] == chip)
        def _():
            scores = masked_scores(keys, query_ref[block], length)
            top = jnp.max(scores, axis=0, keepdims=True)
            prob = jnp.exp(scores - top)
            total = jnp.sum(prob, axis=0, keepdims=True)
            total_ref[block] = top + jnp.log(total)
            attn = rows_inner(values[: length * BLK, :], prob.astype(BF)) / total
            heads_out(attn, attn_ref, block)

    branch_ref[...] = dot(attn_ref[...], out_ref[...]).astype(BF)


def attend(chip, query, kv, out_half):
    smem = pl.BlockSpec(memory_space=pltpu.SMEM)
    vmem = pl.BlockSpec(memory_space=pltpu.VMEM)
    return pl.pallas_call(
        attend_kernel,
        in_specs=[smem, vmem, vmem, vmem],
        out_shape=[
            jax.ShapeDtypeStruct((4 * BLK, QC), BF),
            jax.ShapeDtypeStruct((4, 1, STACK), F32),
            jax.ShapeDtypeStruct((4 * BLK, D), BF),
        ],
        scratch_shapes=[pltpu.VMEM((8 * BLK, HD), BF), pltpu.VMEM((8 * BLK, HD), BF)],
        compiler_params=pltpu.CompilerParams(vmem_limit_bytes=48 * 2**20),
        cost_estimate=pl.CostEstimate(
            flops=2 * 18 * BLK * STACK * HD * 8, bytes_accessed=4 * 2**20, transcendentals=2**21
        ),
        name="attend",
    )(chip, query, kv, out_half)


def attend_back_kernel(
    chip_ref,
    query_ref,
    kv_ref,
    out_ref,
    total_ref,
    branch_ref,
    cos_ref,
    sin_ref,
    grad_ref,
    keep_ref,
    give_ref,
    keys,
    values,
    key_sum,
    value_sum,
    heads,
):
    split_kv(kv_ref, keys, values)
    key_sum[...] = jnp.zeros_like(key_sum)
    value_sum[...] = jnp.zeros_like(value_sum)
    attn_grad = cols_inner(branch_ref[...], out_ref[...])
    for b in range(4):
        part = attn_grad[b * BLK : (b + 1) * BLK]
        for pair in range(4):
            both = jnp.transpose(part[:, 2 * HD * pair : min(2 * HD * (pair + 1), QC)]).astype(BF)
            heads[b, :, 2 * pair * BLK : (2 * pair + 1) * BLK] = both[:HD]
            if pair < 3:
                heads[b, :, (2 * pair + 1) * BLK : (2 * pair + 2) * BLK] = both[HD:]
    for length, (block, chip) in LENGTHS.items():

        @pl.when(chip_ref[0] == chip)
        def _():
            span = length * BLK
            query = query_ref[block]
            grads = heads[block]
            prob = jnp.exp(masked_scores(keys, query, length) - total_ref[block])
            prob_grad = dot(values[:span, :], grads)
            weighted = jnp.sum(prob * prob_grad, axis=0, keepdims=True)
            score_grad = (prob * (prob_grad - weighted)).astype(BF)
            value_sum[:span, :] += cols_inner(prob.astype(BF), grads)
            key_sum[:span, :] += cols_inner(score_grad, query)
            query_grad = rows_inner(keys[:span, :], score_grad) * HD ** (-0.5)
            cosine = jnp.concatenate([cos_ref[block]] * REP, axis=1)
            sine = jnp.concatenate([sin_ref[block]] * REP, axis=1)
            heads_out(turned(query_grad, cosine, -sine), grad_ref, block)

    for place, block in enumerate(ORDER):
        span = slice(block * BLK, (block + 1) * BLK)
        both = jnp.concatenate([key_sum[span, :] * HD ** (-0.5), value_sum[span, :]], axis=1)
        rows = slice(place % 4 * BLK, (place % 4 + 1) * BLK)

        @pl.when(chip_ref[0] == place // 4)
        def _():
            keep_ref[rows, :] = both

        @pl.when(chip_ref[0] != place // 4)
        def _():
            give_ref[rows, :] = both.astype(BF)


def attend_back(chip, query, kv, out_half, total, branch_grad, cosine, sine):
    smem = pl.BlockSpec(memory_space=pltpu.SMEM)
    vmem = pl.BlockSpec(memory_space=pltpu.VMEM)
    return pl.pallas_call(
        attend_back_kernel,
        in_specs=[smem] + [vmem] * 7,
        out_shape=[
            jax.ShapeDtypeStruct((4 * BLK, QC), BF),
            jax.ShapeDtypeStruct((4 * BLK, 2 * HD), F32),
            jax.ShapeDtypeStruct((4 * BLK, 2 * HD), BF),
        ],
        scratch_shapes=[
            pltpu.VMEM((8 * BLK, HD), BF),
            pltpu.VMEM((8 * BLK, HD), BF),
            pltpu.VMEM((8 * BLK, HD), F32),
            pltpu.VMEM((8 * BLK, HD), F32),
            pltpu.VMEM((4, HD, STACK), BF),
        ],
        compiler_params=pltpu.CompilerParams(vmem_limit_bytes=56 * 2**20),
        cost_estimate=pl.CostEstimate(
            flops=2 * 18 * BLK * STACK * HD * 20, bytes_accessed=6 * 2**20, transcendentals=2**21
        ),
        name="attend_back",
    )(chip, query, kv, out_half, total, branch_grad, cosine, sine)


def project_back_kernel(
    core_ref,
    grad_ref,
    keep_ref,
    come_ref,
    rows_ref,
    tok_ref,
    packed_ref,
    gain_two_ref,
    cos_ref,
    sin_ref,
    wgrad_ref,
    in_ref,
    weight,
):
    for s in range(16):
        weight[56 * s : 56 * s + 56, :] = packed_ref[s, :56, :PC]
    kv_grad = keep_ref[...] + come_ref[...].astype(F32)
    keys = []
    for b in range(4):
        key = jnp.transpose(kv_grad[b * BLK : (b + 1) * BLK, :HD])
        keys.append(jnp.transpose(turned(key, cos_ref[b], -sin_ref[b])))
    key_back = jnp.concatenate(keys, axis=0)
    grads = jnp.concatenate(
        [grad_ref[...], key_back.astype(BF), kv_grad[:, HD:].astype(BF)], axis=1
    )
    wgrad = rows_inner(rows_ref[...], grads).astype(BF)
    in_part = cols_inner(grads, weight[...])
    in_ref[...] = in_part.astype(BF)
    inputs = tok_ref[...].astype(F32)
    inverse = lax.rsqrt(jnp.mean(inputs * inputs, axis=-1, keepdims=True) + EPSILON)
    gain_one = jnp.sum(in_part * inputs * inverse, axis=0, keepdims=True)
    gain_two = gain_two_ref[...]
    bias = jnp.sum(grads.astype(F32), axis=0, keepdims=True)
    core = core_ref[0]
    wgrad_ref[:, 56:, :] = jnp.zeros((16, 8, PC), BF)
    for s in range(16):
        wgrad_ref[s, :56, :] = wgrad[56 * s : 56 * s + 56]
        group, start = (s // 7, HD * (s % 7)) if s < 14 else (s - 14, QC)
        qk = jnp.where(core == group, bias[:, start : start + HD], 0.0)
        start = QC + HD + 8 * (s % 8)
        value = jnp.where(core == s // 8, bias[:, start : start + 8], 0.0)
        wgrad_ref[s, 56:57, :56] = gain_one[:, 56 * s : 56 * s + 56].astype(BF)
        wgrad_ref[s, 57:58, :56] = gain_two[:, 56 * s : 56 * s + 56].astype(BF)
        wgrad_ref[s, 58:59, :HD] = qk.astype(BF)
        wgrad_ref[s, 59:60, :8] = value.astype(BF)


def project_back(core, grad, keep, come, rows, tok, packed, gain_two, cosine, sine):
    smem = pl.BlockSpec(memory_space=pltpu.SMEM)
    vmem = pl.BlockSpec(memory_space=pltpu.VMEM)
    return pl.pallas_call(
        project_back_kernel,
        in_specs=[smem] + [vmem] * 9,
        out_shape=[
            jax.ShapeDtypeStruct((16, 64, PC), BF),
            jax.ShapeDtypeStruct((4 * BLK, D), BF),
        ],
        scratch_shapes=[pltpu.VMEM((D, PC), BF)],
        compiler_params=pltpu.CompilerParams(vmem_limit_bytes=48 * 2**20),
        cost_estimate=pl.CostEstimate(
            flops=4 * 4 * BLK * D * PC, bytes_accessed=8 * 2**20, transcendentals=0
        ),
        name="project_back",
    )(core, grad, keep, come, rows, tok, packed, gain_two, cosine, sine)


def shards(
    tokens,
    attn_gain,
    qkv_weight,
    qk_bias,
    value_bias,
    out_weight,
    mlp_gain,
    gate_weight,
    up_weight,
    down_weight,
    cotangent,
):
    yl, c, z, x, yh = [lax.axis_index(name) for name in AXES]
    ctx = yl * 2 + c
    rows = 2 * BLK

    tok = tokens.reshape(rows, D)
    out_grad = cotangent.reshape(rows, D)
    chip = jnp.stack([yl])
    core = jnp.stack([c])

    vectors = jnp.concatenate([attn_gain, mlp_gain, qk_bias, value_bias])
    vec_count = vectors.shape[0]
    packed = jnp.concatenate(
        [
            lax.dynamic_slice_in_dim(qkv_weight, c * QC, QC, 1),
            lax.dynamic_slice_in_dim(qkv_weight, D + c * HD, HD, 1),
            lax.dynamic_slice_in_dim(qkv_weight, D + KVH * HD + c * HD, HD, 1),
            lax.dynamic_slice_in_dim(out_weight, c * QC, QC, 1),
        ],
        axis=1,
    )
    vec_rows = jnp.zeros((4, PACK), BF).at[0, :vec_count].set(vectors)
    packed = jnp.concatenate([packed, vec_rows], axis=0)
    low, high = ordered(packed, swap(packed, "yh"), yh)
    packed = jnp.concatenate([low[:28], high[:28], low[28:], high[28:]], axis=0)
    packed = jnp.broadcast_to(packed, (16, 64, PACK))
    packed, tok = lax.optimization_barrier((packed, tok))
    packed = lax.all_to_all(packed, ("z", "x"), 0, 0, tiled=True)

    tok_two = lax.all_gather(tok, "c", axis=0, tiled=True)
    tok_two, gate_weight, up_weight, down_weight, out_grad = lax.optimization_barrier(
        (tok_two, gate_weight, up_weight, down_weight, out_grad)
    )
    gu_part = quarter(jnp.stack([ctx]), gate_weight, up_weight)
    gu_far = swap(gu_part, "yh")
    down_part = lax.dynamic_slice_in_dim(down_weight, c * 76, 76, 0)
    down_far = lax.ppermute(down_part, ("yl", "yh"), [(0, 1), (3, 2)])
    low, high = ordered(gu_part, gu_far, yh)
    gu_part = jnp.concatenate([low, high], axis=0)
    down_part = jnp.pad(jnp.where(yh == yl, down_part, down_far), ((0, 4), (0, 0)))
    mlp_part = jnp.concatenate([gu_part, tiles_down(down_part)], axis=1)
    grads_far = swap(out_grad, "yl")
    packed, mlp_part = lax.optimization_barrier((packed, mlp_part))
    mlp_all = lax.all_gather(mlp_part, ("z", "x"), axis=0, tiled=True)

    vec_all = packed[:, 56::4, :vec_count].reshape(32, vec_count).astype(F32)
    gain_one = vec_all[:, :28].reshape(1, D)
    gain_two = vec_all[:, 28:56].reshape(1, D)
    qk_bias_full = vec_all[:, 56:88].reshape(D + KVH * HD)
    value_bias_full = vec_all[:, 88:].reshape(KVH * HD)
    bias_part = jnp.concatenate(
        [
            lax.dynamic_slice_in_dim(qk_bias_full, c * QC, QC, 0),
            lax.dynamic_slice_in_dim(qk_bias_full, D + c * HD, HD, 0),
            lax.dynamic_slice_in_dim(value_bias_full, c * HD, HD, 0),
        ]
    ).reshape(1, PC)
    places = jnp.stack([2 * yl, 7 - 2 * yl, 2 * yl + 1, 6 - 2 * yl])
    positions = places[:, None] * BLK + jnp.arange(BLK, dtype=jnp.int32)[None, :]
    freqs = THETA ** (-(jnp.arange(HD // 2, dtype=F32) * 2.0 / HD))
    turns = positions.astype(F32)[:, None, :] * freqs[None, :, None]
    cosine, sine = jnp.cos(turns), jnp.sin(turns)
    normed_in, query, kv_own = project(
        tok_two, packed, gain_one, bias_part, cosine, sine
    )
    kv = lax.all_gather(kv_own, "yl", axis=0, tiled=True)
    out_cols = packed[:, :56, PC:].reshape(2, QC, QC)
    out_give = lax.dynamic_index_in_dim(out_cols, 1 - c, 0, keepdims=False)
    out_keep = lax.dynamic_index_in_dim(out_cols, c, 0, keepdims=False)
    out_half = jnp.concatenate(ordered(out_keep, swap(out_give, "c"), c), axis=1)
    grads = [out_grad, grads_far, swap(out_grad, "c"), swap(grads_far, "c")]
    query, *grads = lax.optimization_barrier((query, *grads))

    attn, total, branch = attend(chip, query, kv, out_half)

    def own_rows(parts):
        return lax.dynamic_slice_in_dim(parts, c * rows, rows, 0)

    def chip_sum(parts):
        give = lax.dynamic_slice_in_dim(parts, (1 - c) * rows, rows, 0)
        return own_rows(parts).astype(F32) + swap(give, "c").astype(F32)

    inputs = tok.astype(F32)
    hidden = inputs + chip_sum(branch)

    inverse_two = lax.rsqrt(jnp.mean(hidden * hidden, axis=-1, keepdims=True) + EPSILON)
    normed_two = hidden * inverse_two
    normed_mid = (normed_two * gain_two).astype(BF)
    mid_far = swap(normed_mid, "yl")
    mids = [normed_mid, mid_far, swap(normed_mid, "c"), swap(mid_far, "c")]
    down_t = tiles_up(mlp_all[:, 2 * FFP :])
    inner, gu_grad, out_parts, mid_parts = mlp(mids, grads, mlp_all, down_t)

    def near_sum(parts):
        parts = parts.reshape(2, 2, rows, D)
        return parts[0].astype(F32) + swap(parts[1], "c").astype(F32)

    mid_near = near_sum(mid_parts)
    mid_grad = mid_near[0] + swap(mid_near[1].astype(BF), "yl").astype(F32)

    gu_sum = lax.psum_scatter(gu_wgrad(mids, gu_grad), "z", scatter_dimension=0, tiled=True)
    down_parts = down_wgrad(inner, grads).reshape(4, 4, 80, D)
    mid_grad, down_parts = lax.optimization_barrier((mid_grad, down_parts))

    gain_two_grad = jnp.sum(mid_grad * normed_two, axis=0, keepdims=True)
    hidden_grad = out_grad.astype(F32) + norm_back(mid_grad * gain_two, normed_two, inverse_two)
    branch_grad = lax.all_gather(hidden_grad.astype(BF), "c", axis=0, tiled=True)
    out_wgrad = rows_inner(attn, branch_grad).astype(BF).reshape(QC, 2, QC)
    out_give = lax.dynamic_index_in_dim(out_wgrad, 1 - c, 1, keepdims=False)
    out_keep = lax.dynamic_index_in_dim(out_wgrad, c, 1, keepdims=False)
    out_cols = jnp.concatenate(ordered(out_keep, swap(out_give, "c"), c), axis=0)
    branch_grad, out_cols, down_parts, out_parts = lax.optimization_barrier(
        (branch_grad, out_cols, down_parts, out_parts)
    )
    out_wparts = lax.all_to_all(out_cols.reshape(16, 56, QC), ("z", "x"), 0, 0, tiled=True)
    down_pieces = spread4(jnp.swapaxes(down_parts, 0, 1), "x", x)
    query_grad, kv_keep, kv_give = attend_back(
        chip, query, kv, out_half, total, branch_grad, cosine, sine
    )
    kv_give, *down_pieces = lax.optimization_barrier((kv_give, *down_pieces))
    kv_come = swap(kv_give, "yl")
    kv_come, out_wparts = lax.optimization_barrier((kv_come, out_wparts))
    down_pieces = spread4(total4(down_pieces), "z", z)
    out_near = near_sum(out_parts)
    out_away = swap(out_near[1].astype(BF), "yl")
    mixed = (hidden + out_near[0] + out_away.astype(F32)).astype(BF)
    qkv_wgrad, in_parts = project_back(
        core,
        query_grad,
        kv_keep,
        kv_come,
        normed_in,
        tok_two,
        packed,
        gain_two_grad,
        cosine,
        sine,
    )

    qkv_wparts = lax.all_to_all(qkv_wgrad, ("z", "x"), 0, 0, tiled=True)
    in_grad = chip_sum(in_parts)
    normed_one = inputs * lax.rsqrt(jnp.mean(inputs * inputs, axis=-1, keepdims=True) + EPSILON)
    inverse_one = lax.rsqrt(jnp.mean(inputs * inputs, axis=-1, keepdims=True) + EPSILON)
    input_grad = hidden_grad + norm_back(in_grad * gain_one, normed_one, inverse_one)

    def part_sum(parts):
        return jnp.sum(parts.astype(F32), axis=0).astype(BF)

    gu_sum, qkv_wparts = lax.optimization_barrier((gu_sum, qkv_wparts))
    gu_pieces = spread4(gu_sum.reshape(4, 56, 2 * FFP), "x", x)
    out_sum = part_sum(out_wparts)
    qkv_sum = part_sum(qkv_wparts)
    both = jnp.concatenate([qkv_sum[:56], out_sum], axis=1).reshape(2, 28, PACK)
    vec_sum = jnp.pad(qkv_sum[56:60], ((0, 0), (0, PACK - PC)))
    packed_sum = jnp.concatenate([both, jnp.broadcast_to(vec_sum, (2, 4, PACK))], axis=1)
    packed_sum = jnp.broadcast_to(packed_sum, (4, 2, 32, PACK)).reshape(8, 32, PACK)
    packed_sum = lax.all_to_all(packed_sum, ("yl", "c", "yh"), 0, 0, tiled=True)
    packed_sum = packed_sum.reshape(2, 2, 2, 32, PACK).astype(F32)
    packed_sum = jnp.sum(packed_sum, axis=(0, 2))
    low, high = packed_sum[0], packed_sum[1]
    qkv_own = jnp.concatenate(
        [
            low[:28, :QC],
            high[:28, :QC],
            low[:28, QC : QC + HD],
            high[:28, QC : QC + HD],
            low[:28, QC + HD : PC],
            high[:28, QC + HD : PC],
        ],
        axis=1,
    )
    out_own = jnp.concatenate([low[:28, PC:], high[:28, PC:]], axis=1)
    vec_own = low[28:] + high[28:]

    def own_vector(row, size):
        return lax.dynamic_slice_in_dim(vec_own[row], yh * size, size, 0)

    down_sum = total4(down_pieces)
    down_sum = (down_sum.astype(F32) + swap(down_sum, "yh").astype(F32)).astype(BF)[:76]
    down_far = lax.ppermute(down_sum, ("yl", "yh"), [(0, 2), (3, 1)])
    down_own = jnp.where(yl == yh, down_sum, down_far)
    down_own = lax.all_gather(down_own, "c", axis=0, tiled=True).astype(F32)

    gu_sum = total4(gu_pieces)
    gu_sum = scatter2(gu_sum.reshape(2, 28, 2 * FFP), "yh", yh)
    gu_pair = jnp.stack(ordered(gu_sum, swap(gu_sum, "yl"), yl))
    gu_all = jnp.swapaxes(lax.all_gather(gu_pair, "c", axis=0), 0, 1)
    gu_all = gu_all.reshape(4, 28, CHUNKS, 2, CH)

    def columns(which):
        parts = gu_all[:, :, :, which].reshape(4, 28, 16, 80)[:, :, :, :76]
        return jnp.transpose(parts, (1, 2, 0, 3)).reshape(28, FF).astype(F32)

    return (
        mixed.reshape(tokens.shape),
        input_grad.reshape(tokens.shape),
        own_vector(0, 28),
        qkv_own,
        own_vector(2, 32),
        own_vector(3, 4),
        out_own,
        own_vector(1, 28),
        columns(0),
        columns(1),
        down_own,
    )


def solution(mesh):
    devices = mesh.devices.reshape(2, 2, 4, 4, 2)
    split = Mesh(devices, AXES)
    ctx, fsdp = ("yl", "c"), ("z", "x", "yh")
    rows = P(fsdp, None, ctx, None, None)
    in_specs = (
        rows,
        P(fsdp),
        P(fsdp, None),
        P(fsdp),
        P(fsdp),
        P(fsdp, None),
        P(fsdp),
        P(fsdp, None),
        P(fsdp, None),
        P(fsdp, None),
        rows,
    )
    out_specs = (
        rows,
        rows,
        P(fsdp),
        P(fsdp, None),
        P(fsdp),
        P(fsdp),
        P(fsdp, None),
        P(fsdp),
        P(fsdp, None),
        P(fsdp, None),
        P(fsdp, None),
    )
    return jax.shard_map(
        shards, mesh=split, in_specs=in_specs, out_specs=out_specs, check_vma=False
    )
```

```python
import jax
import jax.numpy as jnp
from jax import lax
from jax.experimental import pallas as pl
from jax.experimental.pallas import tpu as pltpu
from jax.sharding import Mesh, PartitionSpec as P

KVH = 2
HD = 64
REP = 7
D = 896
FF = 4864
FFT = FF // 4
CH = 256
CHUNKS = 5
FFP = CH * CHUNKS
VMEM_BYTES = 60 * 2**20
QC = REP * HD
STACK = REP * 128
PC = QC + 2 * HD
PACK = PC + QC
BLK = 128
EPSILON = 1e-06
THETA = 1000000.0
AXES = ("yl", "c", "z", "x", "yh")
BF = jnp.bfloat16
F32 = jnp.float32


def shift(value, axis, size, step):
    return lax.ppermute(value, axis, [(i, (i + step) % size) for i in range(size)])


def swap(value, axis):
    return shift(value, axis, 2, 1)


def angles(positions):
    freqs = THETA ** (-(jnp.arange(HD // 2, dtype=F32) * 2.0 / HD))
    return positions.astype(F32)[:, None] * freqs[None, :]


def rows_inner(left, right):
    return lax.dot_general(left, right, (((0,), (0,)), ((), ())), preferred_element_type=F32)


def cols_inner(left, right):
    return lax.dot_general(left, right, (((1,), (1,)), ((), ())), preferred_element_type=F32)


def dot(left, right):
    return jnp.dot(left, right, preferred_element_type=F32)


def norm_back(grad_normed, normed, inverse):
    return inverse * (grad_normed - normed * jnp.mean(grad_normed * normed, axis=-1, keepdims=True))


def ordered(own, other, place):
    first = jnp.where(place == 0, own, other)
    second = jnp.where(place == 0, other, own)
    return first, second


def spread4(parts, axis, place):
    def part(step):
        return lax.dynamic_index_in_dim(parts, (place + step) % 4, 0, keepdims=False)

    return [
        part(0),
        shift(part(1), axis, 4, 1),
        shift(part(3), axis, 4, 3),
        shift(part(2), axis, 4, 2),
    ]


def total4(pieces):
    return sum(piece.astype(F32) for piece in pieces).astype(BF)


def scatter2(parts, axis, place):
    keep = lax.dynamic_index_in_dim(parts, place, 0, keepdims=False)
    give = lax.dynamic_index_in_dim(parts, 1 - place, 0, keepdims=False)
    return (keep.astype(F32) + swap(give, axis).astype(F32)).astype(BF)


def after(value, *others):
    return lax.optimization_barrier((value,) + others)[0]


def quarter_kernel(ctx_ref, gate_ref, up_ref, out_ref):
    out_ref[...] = jnp.zeros_like(out_ref)
    for t in range(4):

        @pl.when(ctx_ref[0] == t)
        def _():
            for which, ref in enumerate((gate_ref, up_ref)):
                for run in range(16):
                    source, place, left = 304 * run + 76 * t, 80 * run, 76
                    while left:
                        size = min(left, CH - place % CH)
                        target = place // CH * 2 * CH + which * CH + place % CH
                        out_ref[:, target : target + size] = ref[:, source : source + size]
                        source, place, left = source + size, place + size, left - size


def quarter(ctx, gate, up):
    smem = pl.BlockSpec(memory_space=pltpu.SMEM)
    vmem = pl.BlockSpec(memory_space=pltpu.VMEM)
    return pl.pallas_call(
        quarter_kernel,
        in_specs=[smem, vmem, vmem],
        out_shape=jax.ShapeDtypeStruct((gate.shape[0], 2 * FFP), BF),
        compiler_params=pltpu.CompilerParams(vmem_limit_bytes=VMEM_BYTES),
        cost_estimate=pl.CostEstimate(flops=0, bytes_accessed=2**20, transcendentals=0),
        name="quarter",
    )(ctx, gate, up)


def tiles_down(part):
    return part.reshape(10, 8, 7, 128).transpose(2, 1, 0, 3).reshape(56, FFP)


PARTS = 4


def mlp_kernel(*refs):
    rows_refs, grads_refs = refs[:PARTS], refs[PARTS : 2 * PARTS]
    gu_ref, tiles_ref, inner_ref, gu_grad_ref, down_ref = refs[2 * PARTS :]
    step = pl.program_id(0)
    size = rows_refs[0].shape[0]

    @pl.when(step == 0)
    def _():
        for s in range(16):
            for pair in range(5):
                for lane in range(7):
                    rows = slice(56 * s + 8 * lane, 56 * s + 8 * lane + 8)
                    first = tiles_ref[rows, 256 * pair : 256 * pair + 128]
                    second = tiles_ref[rows, 256 * pair + 128 : 256 * pair + 256]
                    target = slice(80 * s + 16 * pair, 80 * s + 16 * pair + 16)
                    down_ref[target, 128 * lane : 128 * lane + 128] = jnp.concatenate(
                        [first, second], axis=0
                    )

    gate_w, up_w = gu_ref[:, :CH], gu_ref[:, CH:]
    down_w = down_ref[pl.ds(pl.multiple_of(step * CH, CH), CH), :]
    for p in range(PARTS):
        span = slice(p * size, (p + 1) * size)
        gate = dot(rows_refs[p][...], gate_w)
        up = dot(rows_refs[p][...], up_w)
        inner_grad = cols_inner(grads_refs[p][...], down_w)
        sigma = 0.5 + 0.5 * jnp.tanh(0.5 * gate)
        silu = gate * sigma
        slope = sigma + silu - silu * sigma
        inner_ref[span, :] = (silu * up).astype(BF)
        gu_grad_ref[span, :CH] = (inner_grad * up * slope).astype(BF)
        gu_grad_ref[span, CH:] = (inner_grad * silu).astype(BF)


def mlp(rows, grads, weights):
    size = rows[0].shape[0]
    count = PARTS * size
    whole = pl.BlockSpec((size, D), lambda j: (0, 0))
    return pl.pallas_call(
        mlp_kernel,
        grid=(CHUNKS,),
        in_specs=[
            *[whole] * (2 * PARTS),
            pl.BlockSpec((D, 2 * CH), lambda j: (0, j)),
            pl.BlockSpec((D, FFP), lambda j: (0, 2)),
        ],
        out_specs=[
            pl.BlockSpec((count, CH), lambda j: (0, j)),
            pl.BlockSpec((count, 2 * CH), lambda j: (0, j)),
            pl.BlockSpec((FFP, D), lambda j: (0, 0)),
        ],
        out_shape=[
            jax.ShapeDtypeStruct((count, FFP), BF),
            jax.ShapeDtypeStruct((count, 2 * FFP), BF),
            jax.ShapeDtypeStruct((FFP, D), BF),
        ],
        compiler_params=pltpu.CompilerParams(vmem_limit_bytes=VMEM_BYTES),
        cost_estimate=pl.CostEstimate(
            flops=6 * count * D * FFP, bytes_accessed=20 * 2**20, transcendentals=count * FFP
        ),
        name="mlp",
    )(*rows, *grads, weights, weights)


def mid_kernel(gu_grad_ref, gu_ref, keep_ref, give_ref):
    part = cols_inner(gu_grad_ref[...], gu_ref[...]).astype(BF)
    step = pl.program_id(0)

    @pl.when(step < PARTS // 2)
    def _():
        keep_ref[...] = part

    @pl.when(step >= PARTS // 2)
    def _():
        give_ref[...] = part


def mid(gu_grad, weights):
    count = gu_grad.shape[0]
    return pl.pallas_call(
        mid_kernel,
        grid=(PARTS,),
        in_specs=[
            pl.BlockSpec((count // PARTS, 2 * FFP), lambda j: (j, 0)),
            pl.BlockSpec((D, 2 * FFP), lambda j: (0, 0)),
        ],
        out_specs=[
            pl.BlockSpec((count // PARTS, D), lambda j: (jnp.minimum(j, PARTS // 2 - 1), 0)),
            pl.BlockSpec((count // PARTS, D), lambda j: (jnp.maximum(j - PARTS // 2, 0), 0)),
        ],
        out_shape=[jax.ShapeDtypeStruct((count // 2, D), BF)] * 2,
        compiler_params=pltpu.CompilerParams(vmem_limit_bytes=VMEM_BYTES),
        cost_estimate=pl.CostEstimate(
            flops=4 * count * D * FFP, bytes_accessed=12 * 2**20, transcendentals=0
        ),
        name="mid",
    )(gu_grad, weights)


def gu_wgrad_kernel(*refs):
    grad_ref, out_ref, turned_rows = refs[PARTS:]
    size = refs[0].shape[0]

    @pl.when(pl.program_id(0) == 0)
    def _():
        for p in range(PARTS):
            turned_rows[:, p * size : (p + 1) * size] = jnp.transpose(refs[p][...])

    out_ref[...] = dot(turned_rows[...], grad_ref[...]).astype(BF).reshape(out_ref.shape)


def gu_wgrad(rows, grad):
    count = grad.shape[0]
    return pl.pallas_call(
        gu_wgrad_kernel,
        grid=(CHUNKS,),
        in_specs=[
            *[pl.BlockSpec((count // PARTS, D), lambda j: (0, 0))] * PARTS,
            pl.BlockSpec((count, 2 * CH), lambda j: (0, j)),
        ],
        out_specs=pl.BlockSpec((4, D // 4, 2 * CH), lambda j: (0, 0, j)),
        out_shape=jax.ShapeDtypeStruct((4, D // 4, 2 * FFP), BF),
        scratch_shapes=[pltpu.VMEM((D, count), BF)],
        compiler_params=pltpu.CompilerParams(vmem_limit_bytes=VMEM_BYTES),
        cost_estimate=pl.CostEstimate(
            flops=4 * count * D * FFP, bytes_accessed=12 * 2**20, transcendentals=0
        ),
        name="gu_wgrad",
    )(*rows, grad)


def down_wgrad_kernel(inner_ref, *refs):
    grads = jnp.concatenate([ref[...] for ref in refs[:PARTS]], axis=0)
    part = rows_inner(inner_ref[...], grads).astype(BF)
    for j in range(CHUNKS):

        @pl.when(pl.program_id(0) == j)
        def _():
            place = CH * j
            while place < CH * (j + 1):
                run, start = place // 80, place % 80
                size = min(80 - start, CH * (j + 1) - place)
                rows = part[place - CH * j : place - CH * j + size]
                refs[PARTS][run % 4, run // 4, start : start + size, :] = rows
                place += size


def down_wgrad(inner, grads):
    count = inner.shape[0]
    return pl.pallas_call(
        down_wgrad_kernel,
        grid=(CHUNKS,),
        in_specs=[
            pl.BlockSpec((count, CH), lambda j: (0, j)),
            *[pl.BlockSpec((count // PARTS, D), lambda j: (0, 0))] * PARTS,
        ],
        out_specs=pl.BlockSpec((4, 4, 80, D), lambda j: (0, 0, 0, 0)),
        out_shape=jax.ShapeDtypeStruct((4, 4, 80, D), BF),
        compiler_params=pltpu.CompilerParams(vmem_limit_bytes=VMEM_BYTES),
        cost_estimate=pl.CostEstimate(
            flops=2 * count * D * FFP, bytes_accessed=8 * 2**20, transcendentals=0
        ),
        name="down_wgrad",
    )(inner, *grads)


ORDER = (0, 7, 1, 6, 2, 5, 3, 4)
LENGTHS = {1: (0, 0), 8: (1, 0), 2: (2, 0), 7: (3, 0), 3: (0, 1), 6: (1, 1), 4: (2, 1), 5: (3, 1)}


def turned(value, cosine, sine):
    first, second = value[: HD // 2], value[HD // 2 :]
    return jnp.concatenate(
        [first * cosine - second * sine, second * cosine + first * sine], axis=0
    )


def project_kernel(
    core_ref,
    tok_ref,
    packed_ref,
    cos_ref,
    sin_ref,
    rows_ref,
    query_ref,
    kv_ref,
    gain_two_ref,
    weight,
    gain,
    bias,
):
    for s in range(16):
        weight[56 * s : 56 * s + 56, :] = packed_ref[s, :56, :PC]
        for h in range(2):
            vector = packed_ref[s, 56 + 4 * h : 57 + 4 * h, :128].astype(F32)
            k = 2 * s + h
            gain[:, 28 * k : 28 * k + 28] = vector[:, :28]
            gain_two_ref[:, 28 * k : 28 * k + 28] = vector[:, 28:56]
            group, start = (k // 14, 32 * (k % 14)) if k < 28 else (k // 2 - 14, QC + 32 * (k % 2))

            @pl.when(core_ref[0] == group)
            def _():
                bias[:, start : start + 32] = vector[:, 56:88]

            start = QC + HD + 4 * (k % 16)

            @pl.when(core_ref[0] == k // 16)
            def _():
                bias[:, start : start + 4] = vector[:, 88:92]

    inputs = tok_ref[...].astype(F32)
    inverse = lax.rsqrt(jnp.mean(inputs * inputs, axis=-1, keepdims=True) + EPSILON)
    rows = (inputs * inverse * gain[...]).astype(BF)
    rows_ref[...] = rows
    projected = dot(rows, weight[...]) + bias[...]
    for b in range(4):
        cosine, sine = cos_ref[b], sin_ref[b]
        block = projected[b * BLK : (b + 1) * BLK]
        for pair in range(4):
            both = jnp.transpose(block[:, 2 * HD * pair : 2 * HD * (pair + 1)])
            head = turned(both[:HD], cosine, sine).astype(BF)
            query_ref[b, :, 2 * pair * BLK : (2 * pair + 1) * BLK] = head
            other = turned(both[HD:], cosine, sine)
            if pair < 3:
                query_ref[b, :, (2 * pair + 1) * BLK : (2 * pair + 2) * BLK] = other.astype(BF)
            else:
                value = block[:, QC + HD :]
                kv_ref[b * BLK : (b + 1) * BLK, :] = jnp.concatenate(
                    [jnp.transpose(other), value], axis=1
                ).astype(BF)


def project(core, tok, packed, cosine, sine):
    smem = pl.BlockSpec(memory_space=pltpu.SMEM)
    vmem = pl.BlockSpec(memory_space=pltpu.VMEM)
    return pl.pallas_call(
        project_kernel,
        in_specs=[smem] + [vmem] * 4,
        out_shape=[
            jax.ShapeDtypeStruct((4 * BLK, D), BF),
            jax.ShapeDtypeStruct((4, HD, STACK), BF),
            jax.ShapeDtypeStruct((4 * BLK, 2 * HD), BF),
            jax.ShapeDtypeStruct((1, D), F32),
        ],
        scratch_shapes=[
            pltpu.VMEM((D, PC), BF),
            pltpu.VMEM((1, D), F32),
            pltpu.VMEM((1, PC), F32),
        ],
        compiler_params=pltpu.CompilerParams(vmem_limit_bytes=VMEM_BYTES),
        cost_estimate=pl.CostEstimate(
            flops=2 * 4 * BLK * D * PC, bytes_accessed=6 * 2**20, transcendentals=0
        ),
        name="project",
    )(core, tok, packed, cosine, sine)


def split_kv(kv_ref, keys, values):
    for place, block in enumerate(ORDER):
        rows = kv_ref[place * BLK : (place + 1) * BLK, :]
        keys[block * BLK : (block + 1) * BLK, :] = rows[:, :HD]
        values[block * BLK : (block + 1) * BLK, :] = rows[:, HD:]


def masked_scores(keys, query, length):
    scores = dot(keys[: length * BLK, :], query) * HD ** (-0.5)
    key = lax.broadcasted_iota(jnp.int32, (BLK, STACK), 0)
    token = lax.rem(lax.broadcasted_iota(jnp.int32, (BLK, STACK), 1), BLK)
    last = jnp.where(key <= token, scores[(length - 1) * BLK :], -1e30)
    if length == 1:
        return last
    return jnp.concatenate([scores[: (length - 1) * BLK], last], axis=0)


def heads_out(stacked, ref, block):
    rows = slice(block * BLK, (block + 1) * BLK)
    for pair in range(3):
        first = stacked[:, 2 * pair * BLK : (2 * pair + 1) * BLK]
        second = stacked[:, (2 * pair + 1) * BLK : (2 * pair + 2) * BLK]
        both = jnp.transpose(jnp.concatenate([first, second], axis=0))
        ref[rows, 2 * HD * pair : 2 * HD * (pair + 1)] = both.astype(ref.dtype)
    ref[rows, 6 * HD :] = jnp.transpose(stacked[:, 6 * BLK :]).astype(ref.dtype)


def attend_kernel(chip_ref, query_ref, kv_ref, out_ref, attn_ref, total_ref, branch_ref, keys, values):
    split_kv(kv_ref, keys, values)
    for length, (block, chip) in LENGTHS.items():

        @pl.when(chip_ref[0] == chip)
        def _():
            scores = masked_scores(keys, query_ref[block], length)
            top = jnp.max(scores, axis=0, keepdims=True)
            prob = jnp.exp(scores - top)
            total = jnp.sum(prob, axis=0, keepdims=True)
            total_ref[block] = top + jnp.log(total)
            attn = rows_inner(values[: length * BLK, :], prob.astype(BF)) / total
            heads_out(attn, attn_ref, block)

    branch_ref[...] = dot(attn_ref[...], out_ref[...]).astype(BF)


def attend(chip, query, kv, out_half):
    smem = pl.BlockSpec(memory_space=pltpu.SMEM)
    vmem = pl.BlockSpec(memory_space=pltpu.VMEM)
    return pl.pallas_call(
        attend_kernel,
        in_specs=[smem, vmem, vmem, vmem],
        out_shape=[
            jax.ShapeDtypeStruct((4 * BLK, QC), BF),
            jax.ShapeDtypeStruct((4, 1, STACK), F32),
            jax.ShapeDtypeStruct((4 * BLK, D), BF),
        ],
        scratch_shapes=[pltpu.VMEM((8 * BLK, HD), BF), pltpu.VMEM((8 * BLK, HD), BF)],
        compiler_params=pltpu.CompilerParams(vmem_limit_bytes=VMEM_BYTES),
        cost_estimate=pl.CostEstimate(
            flops=2 * 18 * BLK * STACK * HD * 8, bytes_accessed=4 * 2**20, transcendentals=2**21
        ),
        name="attend",
    )(chip, query, kv, out_half)


def attend_back_kernel(
    chip_ref,
    query_ref,
    kv_ref,
    out_ref,
    total_ref,
    branch_ref,
    cos_ref,
    sin_ref,
    grad_ref,
    keep_ref,
    give_ref,
    keys,
    values,
    key_sum,
    value_sum,
    heads,
):
    split_kv(kv_ref, keys, values)
    key_sum[...] = jnp.zeros_like(key_sum)
    value_sum[...] = jnp.zeros_like(value_sum)
    attn_grad = cols_inner(branch_ref[...], out_ref[...])
    for b in range(4):
        part = attn_grad[b * BLK : (b + 1) * BLK]
        for pair in range(4):
            both = jnp.transpose(part[:, 2 * HD * pair : min(2 * HD * (pair + 1), QC)]).astype(BF)
            heads[b, :, 2 * pair * BLK : (2 * pair + 1) * BLK] = both[:HD]
            if pair < 3:
                heads[b, :, (2 * pair + 1) * BLK : (2 * pair + 2) * BLK] = both[HD:]
    for length, (block, chip) in LENGTHS.items():

        @pl.when(chip_ref[0] == chip)
        def _():
            span = length * BLK
            query = query_ref[block]
            grads = heads[block]
            prob = jnp.exp(masked_scores(keys, query, length) - total_ref[block])
            prob_grad = dot(values[:span, :], grads)
            weighted = jnp.sum(prob * prob_grad, axis=0, keepdims=True)
            score_grad = (prob * (prob_grad - weighted)).astype(BF)
            value_sum[:span, :] += cols_inner(prob.astype(BF), grads)
            key_sum[:span, :] += cols_inner(score_grad, query)
            query_grad = rows_inner(keys[:span, :], score_grad) * HD ** (-0.5)
            cosine = jnp.concatenate([cos_ref[block]] * REP, axis=1)
            sine = jnp.concatenate([sin_ref[block]] * REP, axis=1)
            heads_out(turned(query_grad, cosine, -sine), grad_ref, block)

    for place, block in enumerate(ORDER):
        span = slice(block * BLK, (block + 1) * BLK)
        both = jnp.concatenate([key_sum[span, :] * HD ** (-0.5), value_sum[span, :]], axis=1)
        rows = slice(place % 4 * BLK, (place % 4 + 1) * BLK)

        @pl.when(chip_ref[0] == place // 4)
        def _():
            keep_ref[rows, :] = both

        @pl.when(chip_ref[0] != place // 4)
        def _():
            give_ref[rows, :] = both.astype(BF)


def attend_back(chip, query, kv, out_half, total, branch_grad, cosine, sine):
    smem = pl.BlockSpec(memory_space=pltpu.SMEM)
    vmem = pl.BlockSpec(memory_space=pltpu.VMEM)
    return pl.pallas_call(
        attend_back_kernel,
        in_specs=[smem] + [vmem] * 7,
        out_shape=[
            jax.ShapeDtypeStruct((4 * BLK, QC), BF),
            jax.ShapeDtypeStruct((4 * BLK, 2 * HD), F32),
            jax.ShapeDtypeStruct((4 * BLK, 2 * HD), BF),
        ],
        scratch_shapes=[
            pltpu.VMEM((8 * BLK, HD), BF),
            pltpu.VMEM((8 * BLK, HD), BF),
            pltpu.VMEM((8 * BLK, HD), F32),
            pltpu.VMEM((8 * BLK, HD), F32),
            pltpu.VMEM((4, HD, STACK), BF),
        ],
        compiler_params=pltpu.CompilerParams(vmem_limit_bytes=VMEM_BYTES),
        cost_estimate=pl.CostEstimate(
            flops=2 * 18 * BLK * STACK * HD * 20, bytes_accessed=6 * 2**20, transcendentals=2**21
        ),
        name="attend_back",
    )(chip, query, kv, out_half, total, branch_grad, cosine, sine)


def project_back_kernel(
    core_ref,
    grad_ref,
    keep_ref,
    come_ref,
    rows_ref,
    tok_ref,
    packed_ref,
    gain_two_ref,
    out_keep_ref,
    out_come_ref,
    cos_ref,
    sin_ref,
    wgrad_ref,
    in_ref,
    weight,
):
    for s in range(16):
        weight[56 * s : 56 * s + 56, :] = packed_ref[s, :56, :PC]
    kv_grad = keep_ref[...] + come_ref[...].astype(F32)
    keys = []
    for b in range(4):
        key = jnp.transpose(kv_grad[b * BLK : (b + 1) * BLK, :HD])
        keys.append(jnp.transpose(turned(key, cos_ref[b], -sin_ref[b])))
    key_back = jnp.concatenate(keys, axis=0)
    grads = jnp.concatenate(
        [grad_ref[...], key_back.astype(BF), kv_grad[:, HD:].astype(BF)], axis=1
    )
    wgrad = rows_inner(rows_ref[...], grads).astype(BF)
    in_part = cols_inner(grads, weight[...])
    in_ref[...] = in_part.astype(BF)
    inputs = tok_ref[...].astype(F32)
    inverse = lax.rsqrt(jnp.mean(inputs * inputs, axis=-1, keepdims=True) + EPSILON)
    gain_one = jnp.sum(in_part * inputs * inverse, axis=0, keepdims=True)
    gain_two = gain_two_ref[...]
    bias = jnp.sum(grads.astype(F32), axis=0, keepdims=True)
    core = core_ref[0]
    wgrad_ref[:, 56:, :] = jnp.zeros((16, 8, PACK), BF)
    for group in range(2):

        @pl.when(core == group)
        def _():
            for s in range(8):
                span = slice(56 * s, 56 * s + 56)
                wgrad_ref[8 * group + s, :56, PC:] = out_keep_ref[span, :]
                wgrad_ref[8 * (1 - group) + s, :56, PC:] = out_come_ref[span, :]

    for s in range(16):
        wgrad_ref[s, :56, :PC] = wgrad[56 * s : 56 * s + 56]
        group, start = (s // 7, HD * (s % 7)) if s < 14 else (s - 14, QC)
        qk = jnp.where(core == group, bias[:, start : start + HD], 0.0)
        start = QC + HD + 8 * (s % 8)
        value = jnp.where(core == s // 8, bias[:, start : start + 8], 0.0)
        wgrad_ref[s, 56:57, :56] = gain_one[:, 56 * s : 56 * s + 56].astype(BF)
        wgrad_ref[s, 57:58, :56] = gain_two[:, 56 * s : 56 * s + 56].astype(BF)
        wgrad_ref[s, 58:59, :HD] = qk.astype(BF)
        wgrad_ref[s, 59:60, :8] = value.astype(BF)


def project_back(
    core, grad, keep, come, rows, tok, packed, gain_two, out_keep, out_come, cosine, sine
):
    smem = pl.BlockSpec(memory_space=pltpu.SMEM)
    vmem = pl.BlockSpec(memory_space=pltpu.VMEM)
    return pl.pallas_call(
        project_back_kernel,
        in_specs=[smem] + [vmem] * 11,
        out_shape=[
            jax.ShapeDtypeStruct((16, 64, PACK), BF),
            jax.ShapeDtypeStruct((4 * BLK, D), BF),
        ],
        scratch_shapes=[pltpu.VMEM((D, PC), BF)],
        compiler_params=pltpu.CompilerParams(vmem_limit_bytes=VMEM_BYTES),
        cost_estimate=pl.CostEstimate(
            flops=4 * 4 * BLK * D * PC, bytes_accessed=10 * 2**20, transcendentals=0
        ),
        name="project_back",
    )(core, grad, keep, come, rows, tok, packed, gain_two, out_keep, out_come, cosine, sine)


def part_sum_kernel(parts_ref, out_ref):
    total = parts_ref[0].astype(F32)
    for s in range(1, 16):
        total += parts_ref[s].astype(F32)
    total = total.astype(BF)
    for place in range(8):
        half = 28 * (place % 2)
        out_ref[place, :28, :] = total[half : half + 28]
        out_ref[place, 28:, :] = total[56:60]


def part_sum(parts):
    return pl.pallas_call(
        part_sum_kernel,
        out_shape=jax.ShapeDtypeStruct((8, 32, PACK), BF),
        compiler_params=pltpu.CompilerParams(vmem_limit_bytes=VMEM_BYTES),
        cost_estimate=pl.CostEstimate(flops=0, bytes_accessed=3 * 2**20, transcendentals=0),
        name="part_sum",
    )(parts)


def finish_kernel(parts_ref, qkv_ref, out_ref, vec_ref):
    vectors = 0.0
    for group in range(2):
        total = 0.0
        for place in (0, 1, 4, 5):
            total += parts_ref[2 * group + place].astype(F32)
        rows = total[:28]
        vectors += total[28:, :128]
        qkv_ref[:, QC * group : QC * (group + 1)] = rows[:, :QC]
        qkv_ref[:, D + HD * group : D + HD * (group + 1)] = rows[:, QC : QC + HD]
        start = D + HD * (KVH + group)
        qkv_ref[:, start : start + HD] = rows[:, QC + HD : PC]
        out_ref[:, QC * group : QC * (group + 1)] = rows[:, PC:]
    vec_ref[...] = vectors


def finish(parts):
    return pl.pallas_call(
        finish_kernel,
        out_shape=[
            jax.ShapeDtypeStruct((28, D + 2 * KVH * HD), F32),
            jax.ShapeDtypeStruct((28, D), F32),
            jax.ShapeDtypeStruct((4, 128), F32),
        ],
        compiler_params=pltpu.CompilerParams(vmem_limit_bytes=VMEM_BYTES),
        cost_estimate=pl.CostEstimate(flops=0, bytes_accessed=2**20, transcendentals=0),
        name="finish",
    )(parts)


def out_wgrad_kernel(core_ref, attn_ref, branch_ref, keep_ref, give_ref):
    wgrad = rows_inner(attn_ref[...], branch_ref[...]).astype(BF)
    for group in range(2):

        @pl.when(core_ref[0] == group)
        def _():
            keep_ref[...] = wgrad[:, QC * group : QC * (group + 1)]
            give_ref[...] = wgrad[:, QC * (1 - group) : QC * (2 - group)]


def out_wgrad(core, attn, branch_grad):
    smem = pl.BlockSpec(memory_space=pltpu.SMEM)
    vmem = pl.BlockSpec(memory_space=pltpu.VMEM)
    return pl.pallas_call(
        out_wgrad_kernel,
        in_specs=[smem, vmem, vmem],
        out_shape=[jax.ShapeDtypeStruct((QC, QC), BF)] * 2,
        compiler_params=pltpu.CompilerParams(vmem_limit_bytes=VMEM_BYTES),
        cost_estimate=pl.CostEstimate(
            flops=8 * BLK * QC * D, bytes_accessed=3 * 2**20, transcendentals=0
        ),
        name="out_wgrad",
    )(core, attn, branch_grad)


def deal_kernel(parts_ref, gate_ref, up_ref):
    for t in range(4):
        for which, ref in enumerate((gate_ref, up_ref)):
            for run in range(16):
                target, place, left = 304 * run + 76 * t, 80 * run, 76
                while left:
                    size = min(left, CH - place % CH)
                    source = place // CH * 2 * CH + which * CH + place % CH
                    part = parts_ref[t, :, source : source + size]
                    ref[:, target : target + size] = part.astype(F32)
                    target, place, left = target + size, place + size, left - size


def deal(parts):
    return pl.pallas_call(
        deal_kernel,
        out_shape=[jax.ShapeDtypeStruct((parts.shape[1], 19 * CH), F32)] * 2,
        compiler_params=pltpu.CompilerParams(vmem_limit_bytes=VMEM_BYTES),
        cost_estimate=pl.CostEstimate(flops=0, bytes_accessed=2**21, transcendentals=0),
        name="deal",
    )(parts)


def shards(
    tokens,
    attn_gain,
    qkv_weight,
    qk_bias,
    value_bias,
    out_weight,
    mlp_gain,
    gate_weight,
    up_weight,
    down_weight,
    cotangent,
):
    yl, c, z, x, yh = [lax.axis_index(name) for name in AXES]
    ctx = yl * 2 + c
    rows = 2 * BLK

    tok = tokens.reshape(rows, D)
    out_grad = cotangent.reshape(rows, D)
    chip = jnp.stack([yl])
    core = jnp.stack([c])

    vectors = jnp.concatenate([attn_gain, mlp_gain, qk_bias, value_bias])
    vec_count = vectors.shape[0]
    packed = jnp.concatenate(
        [
            lax.dynamic_slice_in_dim(qkv_weight, c * QC, QC, 1),
            lax.dynamic_slice_in_dim(qkv_weight, D + c * HD, HD, 1),
            lax.dynamic_slice_in_dim(qkv_weight, D + KVH * HD + c * HD, HD, 1),
            lax.dynamic_slice_in_dim(out_weight, c * QC, QC, 1),
        ],
        axis=1,
    )
    vec_rows = jnp.zeros((4, PACK), BF).at[0, :vec_count].set(vectors)
    packed = jnp.concatenate([packed, vec_rows], axis=0)
    low, high = ordered(packed, swap(packed, "yh"), yh)
    packed = jnp.concatenate([low[:28], high[:28], low[28:], high[28:]], axis=0)
    packed = jnp.broadcast_to(packed, (16, 64, PACK))
    packed, tok = lax.optimization_barrier((packed, tok))
    packed = lax.all_to_all(packed, ("z", "x"), 0, 0, tiled=True)

    tok_two = lax.all_gather(tok, "c", axis=0, tiled=True)
    tok_two, gate_weight, up_weight, down_weight, out_grad = lax.optimization_barrier(
        (tok_two, gate_weight, up_weight, down_weight, out_grad)
    )
    gu_part = quarter(jnp.stack([ctx]), gate_weight, up_weight)
    gu_far = swap(gu_part, "yh")
    down_part = lax.dynamic_slice_in_dim(down_weight, c * 76, 76, 0)
    down_far = lax.ppermute(down_part, ("yl", "yh"), [(0, 1), (3, 2)])
    low, high = ordered(gu_part, gu_far, yh)
    gu_part = jnp.concatenate([low, high], axis=0)
    down_part = jnp.pad(jnp.where(yh == yl, down_part, down_far), ((0, 4), (0, 0)))
    mlp_part = jnp.concatenate([gu_part, tiles_down(down_part)], axis=1)
    grads_far = swap(out_grad, "yl")
    places = jnp.stack([2 * yl, 7 - 2 * yl, 2 * yl + 1, 6 - 2 * yl])
    positions = places[:, None] * BLK + jnp.arange(BLK, dtype=jnp.int32)[None, :]
    freqs = THETA ** (-(jnp.arange(HD // 2, dtype=F32) * 2.0 / HD))
    turns = positions.astype(F32)[:, None, :] * freqs[None, :, None]
    cosine, sine = jnp.cos(turns), jnp.sin(turns)
    packed, mlp_part, cosine, sine = lax.optimization_barrier((packed, mlp_part, cosine, sine))
    mlp_all = lax.all_gather(mlp_part, ("z", "x"), axis=0, tiled=True)

    normed_in, query, kv_own, gain_two = project(core, tok_two, packed, cosine, sine)
    vec_late, kv_own = lax.optimization_barrier((packed, kv_own))
    gain_one = vec_late[:, 56::4, :28].reshape(1, D).astype(F32)
    kv = lax.all_gather(kv_own, "yl", axis=0, tiled=True)
    out_cols = vec_late[:, :56, PC:].reshape(2, QC, QC)
    out_give = lax.dynamic_index_in_dim(out_cols, 1 - c, 0, keepdims=False)
    out_keep = lax.dynamic_index_in_dim(out_cols, c, 0, keepdims=False)
    out_half = jnp.concatenate(ordered(out_keep, swap(out_give, "c"), c), axis=1)
    grads = [out_grad, grads_far, swap(out_grad, "c"), swap(grads_far, "c")]

    attn, total, branch = attend(chip, query, kv, out_half)
    branch, *grads = lax.optimization_barrier((branch, *grads))

    def own_rows(parts):
        return lax.dynamic_slice_in_dim(parts, c * rows, rows, 0)

    def chip_sum(parts):
        give = lax.dynamic_slice_in_dim(parts, (1 - c) * rows, rows, 0)
        return own_rows(parts).astype(F32) + swap(give, "c").astype(F32)

    inputs = tok.astype(F32)
    hidden = inputs + chip_sum(branch)

    inverse_two = lax.rsqrt(jnp.mean(hidden * hidden, axis=-1, keepdims=True) + EPSILON)
    normed_two = hidden * inverse_two
    normed_mid = (normed_two * gain_two).astype(BF)
    mid_far = swap(normed_mid, "yl")
    mids = [normed_mid, mid_far, swap(normed_mid, "c"), swap(mid_far, "c")]
    inner, gu_grad, down_t = mlp(mids, grads, mlp_all)
    gu_parts = gu_wgrad(mids, gu_grad)
    gu_sum = lax.psum_scatter(gu_parts, "z", scatter_dimension=0, tiled=True)
    gu_grad, gu_parts = lax.optimization_barrier((gu_grad, gu_parts))
    mid_keep, mid_give = mid(gu_grad, mlp_all)

    def group_sum(keep, come):
        far = keep[rows:].astype(F32) + come[rows:].astype(F32)
        away = swap(far.astype(BF), "yl")
        return keep[:rows].astype(F32) + come[:rows].astype(F32) + away.astype(F32)

    mid_come = swap(mid_give, "c")
    mid_grad = group_sum(mid_keep, mid_come)

    inner, mid_come = lax.optimization_barrier((inner, mid_come))
    down_parts = down_wgrad(inner, grads)
    mid_grad, down_parts = lax.optimization_barrier((mid_grad, down_parts))

    gain_two_grad = jnp.sum(mid_grad * normed_two, axis=0, keepdims=True)
    hidden_grad = out_grad.astype(F32) + norm_back(mid_grad * gain_two, normed_two, inverse_two)
    branch_grad = lax.all_gather(hidden_grad.astype(BF), "c", axis=0, tiled=True)
    down_pieces = lax.all_to_all(down_parts.reshape(4, 320, D), "x", 0, 0, tiled=True)
    query_grad, kv_keep, kv_give = attend_back(
        chip, query, kv, out_half, total, branch_grad, cosine, sine
    )
    kv_come = swap(kv_give, "yl")
    out_keep, out_give = out_wgrad(core, attn, branch_grad)
    out_come = swap(out_give, "c")
    qkv_wgrad, in_parts = project_back(
        core,
        query_grad,
        kv_keep,
        kv_come,
        normed_in,
        tok_two,
        packed,
        gain_two_grad,
        out_keep,
        out_come,
        cosine,
        sine,
    )

    gu_sum = after(gu_sum, kv_give).reshape(4, 56, 2 * FFP)
    gu_sum = lax.psum_scatter(gu_sum, "x", scatter_dimension=0, tiled=True)
    qkv_wgrad, down_pieces = lax.optimization_barrier((qkv_wgrad, down_pieces))
    qkv_wparts = lax.all_to_all(qkv_wgrad, ("z", "x"), 0, 0, tiled=True)
    down_sum = jnp.sum(down_pieces.astype(F32), axis=0).astype(BF).reshape(4, 80, D)
    inner, down_sum = lax.optimization_barrier((inner, down_sum))
    down_pieces = spread4(down_sum, "z", z)
    out_parts = dot(inner, down_t).astype(BF)
    in_parts = after(in_parts, out_parts)
    out_keep, out_give = out_parts[: 2 * rows], out_parts[2 * rows :]
    out_come = swap(out_give, "c")
    out_far = (out_keep[rows:].astype(F32) + out_come[rows:].astype(F32)).astype(BF)
    in_grad = chip_sum(in_parts)
    inverse_one = lax.rsqrt(jnp.mean(inputs * inputs, axis=-1, keepdims=True) + EPSILON)
    normed_one = inputs * inverse_one
    input_grad = hidden_grad + norm_back(in_grad * gain_one, normed_one, inverse_one)
    gu_sum = after(gu_sum, input_grad)
    gu_sum = scatter2(gu_sum.reshape(2, 28, 2 * FFP), "yh", yh)
    packed_sum = part_sum(qkv_wparts)
    packed_sum, gu_sum, out_far, input_grad, *down_pieces = lax.optimization_barrier(
        (packed_sum, gu_sum, out_far, input_grad, *down_pieces)
    )
    out_away = swap(out_far, "yl")
    mixed = hidden + out_keep[:rows].astype(F32) + out_come[:rows].astype(F32)
    mixed = (mixed + out_away.astype(F32)).astype(BF)
    down_sum = total4(down_pieces)
    packed_sum = lax.all_to_all(packed_sum, ("yl", "c", "yh"), 0, 0, tiled=True)
    packed_sum, mixed = lax.optimization_barrier((packed_sum, mixed))
    qkv_own, out_own, vec_own = finish(packed_sum)

    def own_vector(row, size):
        return lax.dynamic_slice_in_dim(vec_own[row], yh * size, size, 0)

    down_sum = (down_sum.astype(F32) + swap(down_sum, "yh").astype(F32)).astype(BF)[:76]
    down_far = lax.ppermute(down_sum, ("yl", "yh"), [(0, 2), (3, 1)])
    down_own = jnp.where(yl == yh, down_sum, down_far)
    down_own = lax.all_gather(down_own, "c", axis=0, tiled=True).astype(F32)

    gu_pair = jnp.stack(ordered(gu_sum, swap(gu_sum, "yl"), yl))
    gu_all = jnp.swapaxes(lax.all_gather(gu_pair, "c", axis=0), 0, 1)
    gate_own, up_own = deal(gu_all.reshape(4, 28, 2 * FFP))

    return (
        mixed.reshape(tokens.shape),
        input_grad.reshape(tokens.shape),
        own_vector(0, 28),
        qkv_own,
        own_vector(2, 32),
        own_vector(3, 4),
        out_own,
        own_vector(1, 28),
        gate_own,
        up_own,
        down_own,
    )


def solution(mesh):
    devices = mesh.devices.reshape(2, 2, 4, 4, 2)
    split = Mesh(devices, AXES)
    ctx, fsdp = ("yl", "c"), ("z", "x", "yh")
    rows = P(fsdp, None, ctx, None, None)
    in_specs = (
        rows,
        P(fsdp),
        P(fsdp, None),
        P(fsdp),
        P(fsdp),
        P(fsdp, None),
        P(fsdp),
        P(fsdp, None),
        P(fsdp, None),
        P(fsdp, None),
        rows,
    )
    out_specs = (
        rows,
        rows,
        P(fsdp),
        P(fsdp, None),
        P(fsdp),
        P(fsdp),
        P(fsdp, None),
        P(fsdp),
        P(fsdp, None),
        P(fsdp, None),
        P(fsdp, None),
    )
    return jax.shard_map(
        shards, mesh=split, in_specs=in_specs, out_specs=out_specs, check_vma=False
    )
```

```python
import jax
import jax.numpy as jnp
from jax import lax
from jax.experimental import pallas as pl
from jax.experimental.pallas import tpu as pltpu
from jax.sharding import Mesh, PartitionSpec as P

KVH = 2
HD = 64
REP = 7
D = 896
FF = 4864
FFT = FF // 4
CH = 256
CHUNKS = 5
FFP = CH * CHUNKS
VMEM_BYTES = 60 * 2**20
QC = REP * HD
STACK = REP * 128
PC = QC + 2 * HD
PACK = PC + QC
BLK = 128
EPSILON = 1e-06
THETA = 1000000.0
AXES = ("yl", "c", "z", "x", "yh")
BF = jnp.bfloat16
F32 = jnp.float32


def shift(value, axis, size, step):
    return lax.ppermute(value, axis, [(i, (i + step) % size) for i in range(size)])


def swap(value, axis):
    return shift(value, axis, 2, 1)


def angles(positions):
    freqs = THETA ** (-(jnp.arange(HD // 2, dtype=F32) * 2.0 / HD))
    return positions.astype(F32)[:, None] * freqs[None, :]


def rows_inner(left, right):
    return lax.dot_general(left, right, (((0,), (0,)), ((), ())), preferred_element_type=F32)


def cols_inner(left, right):
    return lax.dot_general(left, right, (((1,), (1,)), ((), ())), preferred_element_type=F32)


def dot(left, right):
    return jnp.dot(left, right, preferred_element_type=F32)


def norm_back(grad_normed, normed, inverse):
    return inverse * (grad_normed - normed * jnp.mean(grad_normed * normed, axis=-1, keepdims=True))


def ordered(own, other, place):
    first = jnp.where(place == 0, own, other)
    second = jnp.where(place == 0, other, own)
    return first, second


def spread4(parts, axis, place):
    def part(step):
        return lax.dynamic_index_in_dim(parts, (place + step) % 4, 0, keepdims=False)

    return [
        part(0),
        shift(part(1), axis, 4, 1),
        shift(part(3), axis, 4, 3),
        shift(part(2), axis, 4, 2),
    ]


def total4(pieces):
    return sum(piece.astype(F32) for piece in pieces).astype(BF)


def scatter2(parts, axis, place):
    keep = lax.dynamic_index_in_dim(parts, place, 0, keepdims=False)
    give = lax.dynamic_index_in_dim(parts, 1 - place, 0, keepdims=False)
    return (keep.astype(F32) + swap(give, axis).astype(F32)).astype(BF)


def after(value, *others):
    return lax.optimization_barrier((value,) + others)[0]


def quarter_kernel(ctx_ref, gate_ref, up_ref, down_ref, gu_out_ref, down_out_ref):
    gu_out_ref[...] = jnp.zeros_like(gu_out_ref)
    down_out_ref[...] = jnp.zeros_like(down_out_ref)
    for t in range(4):

        @pl.when(ctx_ref[0] == t)
        def _():
            down_out_ref[:38, :] = down_ref[38 * t : 38 * t + 38, :]
            for which, ref in enumerate((gate_ref, up_ref)):
                for run in range(32):
                    source, place, left = 152 * run + 38 * t, 40 * run, 38
                    while left:
                        size = min(left, CH - place % CH)
                        target = place // CH * 2 * CH + which * CH + place % CH
                        gu_out_ref[:, target : target + size] = ref[:, source : source + size]
                        source, place, left = source + size, place + size, left - size


def quarter(ctx, gate, up, down):
    smem = pl.BlockSpec(memory_space=pltpu.SMEM)
    vmem = pl.BlockSpec(memory_space=pltpu.VMEM)
    return pl.pallas_call(
        quarter_kernel,
        in_specs=[smem, vmem, vmem, vmem],
        out_shape=[
            jax.ShapeDtypeStruct((gate.shape[0], 2 * FFP), BF),
            jax.ShapeDtypeStruct((40, D), BF),
        ],
        compiler_params=pltpu.CompilerParams(vmem_limit_bytes=VMEM_BYTES),
        cost_estimate=pl.CostEstimate(flops=0, bytes_accessed=0, transcendentals=0),
        name="quarter",
    )(ctx, gate, up, down)


def tiles_down(part):
    return part.reshape(10, 8, 7, 128).transpose(2, 1, 0, 3).reshape(56, FFP)


PARTS = 4


def mlp_kernel(*refs):
    rows_refs, grads_refs = refs[:PARTS], refs[PARTS : 2 * PARTS]
    gu_ref, tiles_ref, inner_ref, gu_grad_ref, down_ref, wgrad_ref, turned_rows = refs[2 * PARTS :]
    step = pl.program_id(0)
    size = rows_refs[0].shape[0]

    @pl.when(step == 0)
    def _():
        for p in range(PARTS):
            turned_rows[:, p * size : (p + 1) * size] = jnp.transpose(rows_refs[p][...])

        for s in range(16):
            for pair in range(5):
                for lane in range(7):
                    rows = slice(56 * s + 8 * lane, 56 * s + 8 * lane + 8)
                    first = tiles_ref[rows, 256 * pair : 256 * pair + 128]
                    second = tiles_ref[rows, 256 * pair + 128 : 256 * pair + 256]
                    target = slice(80 * s + 16 * pair, 80 * s + 16 * pair + 16)
                    down_ref[target, 128 * lane : 128 * lane + 128] = jnp.concatenate(
                        [first, second], axis=0
                    )

    gate_w, up_w = gu_ref[:, :CH], gu_ref[:, CH:]
    down_w = down_ref[pl.ds(pl.multiple_of(step * CH, CH), CH), :]
    for p in range(PARTS):
        span = slice(p * size, (p + 1) * size)
        gate = dot(rows_refs[p][...], gate_w)
        up = dot(rows_refs[p][...], up_w)
        inner_grad = cols_inner(grads_refs[p][...], down_w)
        sigma = 0.5 + 0.5 * jnp.tanh(0.5 * gate)
        silu = gate * sigma
        slope = sigma + silu - silu * sigma
        inner_ref[span, :] = (silu * up).astype(BF)
        gu_grad_ref[span, :CH] = (inner_grad * up * slope).astype(BF)
        gu_grad_ref[span, CH:] = (inner_grad * silu).astype(BF)
    wgrad = dot(turned_rows[...], gu_grad_ref[...])
    wgrad_ref[...] = wgrad.astype(BF).reshape(wgrad_ref.shape)


def mlp(rows, grads, weights):
    size = rows[0].shape[0]
    count = PARTS * size
    whole = pl.BlockSpec((size, D), lambda j: (0, 0))
    return pl.pallas_call(
        mlp_kernel,
        grid=(CHUNKS,),
        in_specs=[
            *[whole] * (2 * PARTS),
            pl.BlockSpec((D, 2 * CH), lambda j: (0, j)),
            pl.BlockSpec((D, FFP), lambda j: (0, 2)),
        ],
        out_specs=[
            pl.BlockSpec((count, CH), lambda j: (0, j)),
            pl.BlockSpec((count, 2 * CH), lambda j: (0, j)),
            pl.BlockSpec((FFP, D), lambda j: (0, 0)),
            pl.BlockSpec((4, D // 4, 2 * CH), lambda j: (0, 0, j)),
        ],
        out_shape=[
            jax.ShapeDtypeStruct((count, FFP), BF),
            jax.ShapeDtypeStruct((count, 2 * FFP), BF),
            jax.ShapeDtypeStruct((FFP, D), BF),
            jax.ShapeDtypeStruct((4, D // 4, 2 * FFP), BF),
        ],
        scratch_shapes=[pltpu.VMEM((D, count), BF)],
        compiler_params=pltpu.CompilerParams(vmem_limit_bytes=VMEM_BYTES),
        cost_estimate=pl.CostEstimate(
            flops=10 * count * D * FFP, bytes_accessed=24 * 2**20, transcendentals=count * FFP
        ),
        name="mlp",
    )(*rows, *grads, weights, weights)


def mid_kernel(gu_grad_ref, gu_ref, keep_ref, give_ref):
    part = cols_inner(gu_grad_ref[...], gu_ref[...]).astype(BF)
    step = pl.program_id(0)

    @pl.when(step < PARTS // 2)
    def _():
        keep_ref[...] = part

    @pl.when(step >= PARTS // 2)
    def _():
        give_ref[...] = part


def mid(gu_grad, weights):
    count = gu_grad.shape[0]
    return pl.pallas_call(
        mid_kernel,
        grid=(PARTS,),
        in_specs=[
            pl.BlockSpec((count // PARTS, 2 * FFP), lambda j: (j, 0)),
            pl.BlockSpec((D, 2 * FFP), lambda j: (0, 0)),
        ],
        out_specs=[
            pl.BlockSpec((count // PARTS, D), lambda j: (jnp.minimum(j, PARTS // 2 - 1), 0)),
            pl.BlockSpec((count // PARTS, D), lambda j: (jnp.maximum(j - PARTS // 2, 0), 0)),
        ],
        out_shape=[jax.ShapeDtypeStruct((count // 2, D), BF)] * 2,
        compiler_params=pltpu.CompilerParams(vmem_limit_bytes=VMEM_BYTES),
        cost_estimate=pl.CostEstimate(
            flops=4 * count * D * FFP, bytes_accessed=12 * 2**20, transcendentals=0
        ),
        name="mid",
    )(gu_grad, weights)


def mlp_out_kernel(inner_ref, down_ref, keep_ref, give_ref):
    half = keep_ref.shape[0]
    keep_ref[...] = dot(inner_ref[:half, :], down_ref[...]).astype(BF)
    give_ref[...] = dot(inner_ref[half:, :], down_ref[...]).astype(BF)


def mlp_out(inner, down):
    count = inner.shape[0]
    return pl.pallas_call(
        mlp_out_kernel,
        out_shape=[jax.ShapeDtypeStruct((count // 2, D), BF)] * 2,
        compiler_params=pltpu.CompilerParams(vmem_limit_bytes=VMEM_BYTES),
        cost_estimate=pl.CostEstimate(flops=0, bytes_accessed=0, transcendentals=0),
        name="mlp_out",
    )(inner, down)


def down_wgrad_kernel(inner_ref, *refs):
    grads = jnp.concatenate([ref[...] for ref in refs[:PARTS]], axis=0)
    part = rows_inner(inner_ref[...], grads).astype(BF)
    for j in range(CHUNKS):

        @pl.when(pl.program_id(0) == j)
        def _():
            place = CH * j
            while place < CH * (j + 1):
                run, start = place // 80, place % 80
                size = min(80 - start, CH * (j + 1) - place)
                rows = part[place - CH * j : place - CH * j + size]
                refs[PARTS][run % 4, run // 4, start : start + size, :] = rows
                place += size


def down_wgrad(inner, grads):
    count = inner.shape[0]
    return pl.pallas_call(
        down_wgrad_kernel,
        grid=(CHUNKS,),
        in_specs=[
            pl.BlockSpec((count, CH), lambda j: (0, j)),
            *[pl.BlockSpec((count // PARTS, D), lambda j: (0, 0))] * PARTS,
        ],
        out_specs=pl.BlockSpec((4, 4, 80, D), lambda j: (0, 0, 0, 0)),
        out_shape=jax.ShapeDtypeStruct((4, 4, 80, D), BF),
        compiler_params=pltpu.CompilerParams(vmem_limit_bytes=VMEM_BYTES),
        cost_estimate=pl.CostEstimate(flops=0, bytes_accessed=0, transcendentals=0),
        name="down_wgrad",
    )(inner, *grads)


ORDER = (0, 7, 1, 6, 2, 5, 3, 4)
LENGTHS = {1: (0, 0), 8: (1, 0), 2: (2, 0), 7: (3, 0), 3: (0, 1), 6: (1, 1), 4: (2, 1), 5: (3, 1)}


def turned(value, cosine, sine):
    first, second = value[: HD // 2], value[HD // 2 :]
    return jnp.concatenate(
        [first * cosine - second * sine, second * cosine + first * sine], axis=0
    )


def project_kernel(
    core_ref,
    tok_ref,
    packed_ref,
    cos_ref,
    sin_ref,
    rows_ref,
    query_ref,
    kv_ref,
    gain_two_ref,
    weight,
    gain,
    bias,
):
    for s in range(16):
        weight[56 * s : 56 * s + 56, :] = packed_ref[s, :56, :PC]
        for h in range(2):
            vector = packed_ref[s, 56 + 4 * h : 57 + 4 * h, :128].astype(F32)
            k = 2 * s + h
            gain[:, 28 * k : 28 * k + 28] = vector[:, :28]
            gain_two_ref[:, 28 * k : 28 * k + 28] = vector[:, 28:56]
            group, start = (k // 14, 32 * (k % 14)) if k < 28 else (k // 2 - 14, QC + 32 * (k % 2))

            @pl.when(core_ref[0] == group)
            def _():
                bias[:, start : start + 32] = vector[:, 56:88]

            start = QC + HD + 4 * (k % 16)

            @pl.when(core_ref[0] == k // 16)
            def _():
                bias[:, start : start + 4] = vector[:, 88:92]

    inputs = tok_ref[...].astype(F32)
    inverse = lax.rsqrt(jnp.mean(inputs * inputs, axis=-1, keepdims=True) + EPSILON)
    rows = (inputs * inverse * gain[...]).astype(BF)
    rows_ref[...] = rows
    projected = dot(rows, weight[...]) + bias[...]
    for b in range(4):
        cosine, sine = cos_ref[b], sin_ref[b]
        block = projected[b * BLK : (b + 1) * BLK]
        for pair in range(4):
            both = jnp.transpose(block[:, 2 * HD * pair : 2 * HD * (pair + 1)])
            head = turned(both[:HD], cosine, sine).astype(BF)
            query_ref[b, :, 2 * pair * BLK : (2 * pair + 1) * BLK] = head
            other = turned(both[HD:], cosine, sine)
            if pair < 3:
                query_ref[b, :, (2 * pair + 1) * BLK : (2 * pair + 2) * BLK] = other.astype(BF)
            else:
                value = block[:, QC + HD :]
                kv_ref[b * BLK : (b + 1) * BLK, :] = jnp.concatenate(
                    [jnp.transpose(other), value], axis=1
                ).astype(BF)


def project(core, tok, packed, cosine, sine):
    smem = pl.BlockSpec(memory_space=pltpu.SMEM)
    vmem = pl.BlockSpec(memory_space=pltpu.VMEM)
    return pl.pallas_call(
        project_kernel,
        in_specs=[smem] + [vmem] * 4,
        out_shape=[
            jax.ShapeDtypeStruct((4 * BLK, D), BF),
            jax.ShapeDtypeStruct((4, HD, STACK), BF),
            jax.ShapeDtypeStruct((4 * BLK, 2 * HD), BF),
            jax.ShapeDtypeStruct((1, D), F32),
            jax.ShapeDtypeStruct((D, PC), BF),
        ],
        scratch_shapes=[
            pltpu.VMEM((1, D), F32),
            pltpu.VMEM((1, PC), F32),
        ],
        compiler_params=pltpu.CompilerParams(vmem_limit_bytes=VMEM_BYTES),
        cost_estimate=pl.CostEstimate(
            flops=2 * 4 * BLK * D * PC, bytes_accessed=6 * 2**20, transcendentals=0
        ),
        name="project",
    )(core, tok, packed, cosine, sine)


def split_kv(kv_ref, keys, values):
    for place, block in enumerate(ORDER):
        rows = kv_ref[place * BLK : (place + 1) * BLK, :]
        keys[block * BLK : (block + 1) * BLK, :] = rows[:, :HD]
        values[block * BLK : (block + 1) * BLK, :] = rows[:, HD:]


def masked_scores(keys, query, length):
    scores = dot(keys[: length * BLK, :], query) * HD ** (-0.5)
    key = lax.broadcasted_iota(jnp.int32, (BLK, STACK), 0)
    token = lax.rem(lax.broadcasted_iota(jnp.int32, (BLK, STACK), 1), BLK)
    last = jnp.where(key <= token, scores[(length - 1) * BLK :], -1e30)
    if length == 1:
        return last
    return jnp.concatenate([scores[: (length - 1) * BLK], last], axis=0)


def heads_out(stacked, ref, block):
    rows = slice(block * BLK, (block + 1) * BLK)
    for pair in range(3):
        first = stacked[:, 2 * pair * BLK : (2 * pair + 1) * BLK]
        second = stacked[:, (2 * pair + 1) * BLK : (2 * pair + 2) * BLK]
        both = jnp.transpose(jnp.concatenate([first, second], axis=0))
        ref[rows, 2 * HD * pair : 2 * HD * (pair + 1)] = both.astype(ref.dtype)
    ref[rows, 6 * HD :] = jnp.transpose(stacked[:, 6 * BLK :]).astype(ref.dtype)


def attend_kernel(chip_ref, query_ref, kv_ref, attn_ref, total_ref, keys, values):
    split_kv(kv_ref, keys, values)
    for length, (block, chip) in LENGTHS.items():

        @pl.when(chip_ref[0] == chip)
        def _():
            scores = masked_scores(keys, query_ref[block], length)
            top = jnp.max(scores, axis=0, keepdims=True)
            prob = jnp.exp(scores - top)
            total = jnp.sum(prob, axis=0, keepdims=True)
            total_ref[block] = top + jnp.log(total)
            attn = rows_inner(values[: length * BLK, :], prob.astype(BF)) / total
            heads_out(attn, attn_ref, block)


def attend(chip, query, kv):
    smem = pl.BlockSpec(memory_space=pltpu.SMEM)
    vmem = pl.BlockSpec(memory_space=pltpu.VMEM)
    return pl.pallas_call(
        attend_kernel,
        in_specs=[smem, vmem, vmem],
        out_shape=[
            jax.ShapeDtypeStruct((4 * BLK, QC), BF),
            jax.ShapeDtypeStruct((4, 1, STACK), F32),
        ],
        scratch_shapes=[pltpu.VMEM((8 * BLK, HD), BF), pltpu.VMEM((8 * BLK, HD), BF)],
        compiler_params=pltpu.CompilerParams(vmem_limit_bytes=VMEM_BYTES),
        cost_estimate=pl.CostEstimate(
            flops=2 * 18 * BLK * STACK * HD * 8, bytes_accessed=4 * 2**20, transcendentals=2**21
        ),
        name="attend",
    )(chip, query, kv)


def attend_back_kernel(
    chip_ref,
    query_ref,
    kv_ref,
    out_ref,
    total_ref,
    branch_ref,
    cos_ref,
    sin_ref,
    grad_ref,
    keep_ref,
    give_ref,
    keys,
    values,
    key_sum,
    value_sum,
    heads,
):
    split_kv(kv_ref, keys, values)
    key_sum[...] = jnp.zeros_like(key_sum)
    value_sum[...] = jnp.zeros_like(value_sum)
    attn_grad = cols_inner(branch_ref[...], out_ref[...])
    for b in range(4):
        part = attn_grad[b * BLK : (b + 1) * BLK]
        for pair in range(4):
            both = jnp.transpose(part[:, 2 * HD * pair : min(2 * HD * (pair + 1), QC)]).astype(BF)
            heads[b, :, 2 * pair * BLK : (2 * pair + 1) * BLK] = both[:HD]
            if pair < 3:
                heads[b, :, (2 * pair + 1) * BLK : (2 * pair + 2) * BLK] = both[HD:]
    for length, (block, chip) in LENGTHS.items():

        @pl.when(chip_ref[0] == chip)
        def _():
            span = length * BLK
            query = query_ref[block]
            grads = heads[block]
            prob = jnp.exp(masked_scores(keys, query, length) - total_ref[block])
            prob_grad = dot(values[:span, :], grads)
            weighted = jnp.sum(prob * prob_grad, axis=0, keepdims=True)
            score_grad = (prob * (prob_grad - weighted)).astype(BF)
            value_sum[:span, :] += cols_inner(prob.astype(BF), grads)
            key_sum[:span, :] += cols_inner(score_grad, query)
            query_grad = rows_inner(keys[:span, :], score_grad) * HD ** (-0.5)
            cosine = jnp.concatenate([cos_ref[block]] * REP, axis=1)
            sine = jnp.concatenate([sin_ref[block]] * REP, axis=1)
            heads_out(turned(query_grad, cosine, -sine), grad_ref, block)

    for place, block in enumerate(ORDER):
        span = slice(block * BLK, (block + 1) * BLK)
        both = jnp.concatenate([key_sum[span, :] * HD ** (-0.5), value_sum[span, :]], axis=1)
        rows = slice(place % 4 * BLK, (place % 4 + 1) * BLK)

        @pl.when(chip_ref[0] == place // 4)
        def _():
            keep_ref[rows, :] = both

        @pl.when(chip_ref[0] != place // 4)
        def _():
            give_ref[rows, :] = both.astype(BF)


def attend_back(chip, query, kv, out_half, total, branch_grad, cosine, sine):
    smem = pl.BlockSpec(memory_space=pltpu.SMEM)
    vmem = pl.BlockSpec(memory_space=pltpu.VMEM)
    return pl.pallas_call(
        attend_back_kernel,
        in_specs=[smem] + [vmem] * 7,
        out_shape=[
            jax.ShapeDtypeStruct((4 * BLK, QC), BF),
            jax.ShapeDtypeStruct((4 * BLK, 2 * HD), F32),
            jax.ShapeDtypeStruct((4 * BLK, 2 * HD), BF),
        ],
        scratch_shapes=[
            pltpu.VMEM((8 * BLK, HD), BF),
            pltpu.VMEM((8 * BLK, HD), BF),
            pltpu.VMEM((8 * BLK, HD), F32),
            pltpu.VMEM((8 * BLK, HD), F32),
            pltpu.VMEM((4, HD, STACK), BF),
        ],
        compiler_params=pltpu.CompilerParams(vmem_limit_bytes=VMEM_BYTES),
        cost_estimate=pl.CostEstimate(
            flops=2 * 18 * BLK * STACK * HD * 20, bytes_accessed=6 * 2**20, transcendentals=2**21
        ),
        name="attend_back",
    )(chip, query, kv, out_half, total, branch_grad, cosine, sine)


def project_back_kernel(
    core_ref,
    grad_ref,
    keep_ref,
    come_ref,
    rows_ref,
    tok_ref,
    weight_ref,
    gain_two_ref,
    out_keep_ref,
    out_come_ref,
    cos_ref,
    sin_ref,
    wgrad_ref,
    in_ref,
):
    kv_grad = keep_ref[...] + come_ref[...].astype(F32)
    keys = []
    for b in range(4):
        key = jnp.transpose(kv_grad[b * BLK : (b + 1) * BLK, :HD])
        keys.append(jnp.transpose(turned(key, cos_ref[b], -sin_ref[b])))
    key_back = jnp.concatenate(keys, axis=0)
    grads = jnp.concatenate(
        [grad_ref[...], key_back.astype(BF), kv_grad[:, HD:].astype(BF)], axis=1
    )
    wgrad = rows_inner(rows_ref[...], grads).astype(BF)
    in_part = cols_inner(grads, weight_ref[...])
    in_ref[...] = in_part.astype(BF)
    inputs = tok_ref[...].astype(F32)
    inverse = lax.rsqrt(jnp.mean(inputs * inputs, axis=-1, keepdims=True) + EPSILON)
    gain_one = jnp.sum(in_part * inputs * inverse, axis=0, keepdims=True)
    gain_two = gain_two_ref[...]
    bias = jnp.sum(grads.astype(F32), axis=0, keepdims=True)
    core = core_ref[0]
    wgrad_ref[:, 56:, :] = jnp.zeros((16, 8, PACK), BF)
    for group in range(2):

        @pl.when(core == group)
        def _():
            for s in range(8):
                span = slice(56 * s, 56 * s + 56)
                wgrad_ref[8 * group + s, :56, PC:] = out_keep_ref[span, :]
                wgrad_ref[8 * (1 - group) + s, :56, PC:] = out_come_ref[span, :]

    for s in range(16):
        wgrad_ref[s, :56, :PC] = wgrad[56 * s : 56 * s + 56]
        group, start = (s // 7, HD * (s % 7)) if s < 14 else (s - 14, QC)
        qk = jnp.where(core == group, bias[:, start : start + HD], 0.0)
        start = QC + HD + 8 * (s % 8)
        value = jnp.where(core == s // 8, bias[:, start : start + 8], 0.0)
        wgrad_ref[s, 56:57, :56] = gain_one[:, 56 * s : 56 * s + 56].astype(BF)
        wgrad_ref[s, 57:58, :56] = gain_two[:, 56 * s : 56 * s + 56].astype(BF)
        wgrad_ref[s, 58:59, :HD] = qk.astype(BF)
        wgrad_ref[s, 59:60, :8] = value.astype(BF)


def project_back(
    core, grad, keep, come, rows, tok, weight, gain_two, out_keep, out_come, cosine, sine
):
    smem = pl.BlockSpec(memory_space=pltpu.SMEM)
    vmem = pl.BlockSpec(memory_space=pltpu.VMEM)
    return pl.pallas_call(
        project_back_kernel,
        in_specs=[smem] + [vmem] * 11,
        out_shape=[
            jax.ShapeDtypeStruct((16, 64, PACK), BF),
            jax.ShapeDtypeStruct((4 * BLK, D), BF),
        ],
        compiler_params=pltpu.CompilerParams(vmem_limit_bytes=VMEM_BYTES),
        cost_estimate=pl.CostEstimate(
            flops=4 * 4 * BLK * D * PC, bytes_accessed=10 * 2**20, transcendentals=0
        ),
        name="project_back",
    )(core, grad, keep, come, rows, tok, weight, gain_two, out_keep, out_come, cosine, sine)


def sum4_kernel(parts_ref, out_ref):
    total = parts_ref[0].astype(F32)
    for s in range(1, 4):
        total += parts_ref[s].astype(F32)
    out_ref[...] = total.astype(BF)


def sum4(parts):
    _, count, width = parts.shape
    return pl.pallas_call(
        sum4_kernel,
        out_shape=jax.ShapeDtypeStruct((count, width), BF),
        compiler_params=pltpu.CompilerParams(vmem_limit_bytes=VMEM_BYTES),
        cost_estimate=pl.CostEstimate(flops=0, bytes_accessed=0, transcendentals=0),
        name="sum4",
    )(parts)


def small(kernel, shapes, *operands, name):
    vmem = pl.BlockSpec(memory_space=pltpu.VMEM)
    smem = pl.BlockSpec(memory_space=pltpu.SMEM)
    return pl.pallas_call(
        kernel,
        in_specs=[smem if value.dtype == jnp.int32 else vmem for value in operands],
        out_shape=shapes,
        compiler_params=pltpu.CompilerParams(vmem_limit_bytes=VMEM_BYTES),
        cost_estimate=pl.CostEstimate(flops=0, bytes_accessed=0, transcendentals=0),
        name=name,
    )(*operands)


def far_kernel(keep_ref, come_ref, out_ref):
    half = out_ref.shape[0]
    total = keep_ref[half:, :].astype(F32) + come_ref[half:, :].astype(F32)
    out_ref[...] = total.astype(BF)


def far_rows(keep, come):
    shape = jax.ShapeDtypeStruct((keep.shape[0] // 2, keep.shape[1]), BF)
    return small(far_kernel, shape, keep, come, name="far_rows")


def halves_kernel(place_ref, gu_ref, *refs):
    keep_ref, give_ref, total_ref = refs[4:]
    total_ref[...] = sum(ref[...].astype(F32) for ref in refs[:4])
    for place in range(2):

        @pl.when(place_ref[0] == place)
        def _():
            for ref, half in ((keep_ref, place), (give_ref, 1 - place)):
                ref[:, : 2 * FFP] = gu_ref[28 * half : 28 * half + 28, :]
                for piece in range(70):
                    row, lane = 40 * half + 4 * (piece // 7), 128 * (piece % 7)
                    part = total_ref[row : row + 4, lane : lane + 128].astype(BF)
                    row, lane = 4 * (piece // 10), 2 * FFP + 128 * (piece % 10)
                    ref[row : row + 4, lane : lane + 128] = part


def halves(place, gu, down_pieces):
    shape = jax.ShapeDtypeStruct((28, 3 * FFP), BF)
    vmem = pl.BlockSpec(memory_space=pltpu.VMEM)
    return pl.pallas_call(
        halves_kernel,
        in_specs=[pl.BlockSpec(memory_space=pltpu.SMEM)] + [vmem] * 5,
        out_shape=[shape, shape],
        scratch_shapes=[pltpu.VMEM((80, D), F32)],
        compiler_params=pltpu.CompilerParams(vmem_limit_bytes=VMEM_BYTES),
        cost_estimate=pl.CostEstimate(flops=0, bytes_accessed=0, transcendentals=0),
        name="halves",
    )(place, gu, *down_pieces)


def input_kernel(core_ref, grad_ref, parts_ref, come_ref, tok_ref, gain_ref, out_ref):
    size = come_ref.shape[0]
    for core in range(2):

        @pl.when(core_ref[0] == core)
        def _():
            part = parts_ref[core * size : (core + 1) * size, :].astype(F32)
            scaled = (part + come_ref[...].astype(F32)) * gain_ref[...]
            inputs = tok_ref[...].astype(F32)
            inverse = lax.rsqrt(jnp.mean(inputs * inputs, axis=-1, keepdims=True) + EPSILON)
            out_ref[...] = grad_ref[...] + norm_back(scaled, inputs * inverse, inverse)


def input_back(core, grad, parts, come, tok, gain):
    shape = jax.ShapeDtypeStruct(grad.shape, F32)
    return small(input_kernel, shape, core, grad, parts, come, tok, gain, name="input_back")


def part_sum_kernel(parts_ref, out_ref):
    total = parts_ref[0].astype(F32)
    for s in range(1, 16):
        total += parts_ref[s].astype(F32)
    total = total.astype(BF)
    for place in range(8):
        half = 28 * (place % 2)
        out_ref[place, :28, :] = total[half : half + 28]
        out_ref[place, 28:, :] = total[56:60]


def part_sum(parts):
    return pl.pallas_call(
        part_sum_kernel,
        out_shape=jax.ShapeDtypeStruct((8, 32, PACK), BF),
        compiler_params=pltpu.CompilerParams(vmem_limit_bytes=VMEM_BYTES),
        cost_estimate=pl.CostEstimate(flops=0, bytes_accessed=3 * 2**20, transcendentals=0),
        name="part_sum",
    )(parts)


def finish_kernel(parts_ref, qkv_ref, out_ref, vec_ref):
    vectors = 0.0
    for group in range(2):
        total = 0.0
        for place in (0, 1, 4, 5):
            total += parts_ref[2 * group + place].astype(F32)
        rows = total[:28]
        vectors += total[28:, :128]
        qkv_ref[:, QC * group : QC * (group + 1)] = rows[:, :QC]
        qkv_ref[:, D + HD * group : D + HD * (group + 1)] = rows[:, QC : QC + HD]
        start = D + HD * (KVH + group)
        qkv_ref[:, start : start + HD] = rows[:, QC + HD : PC]
        out_ref[:, QC * group : QC * (group + 1)] = rows[:, PC:]
    vec_ref[...] = vectors


def finish(parts):
    return pl.pallas_call(
        finish_kernel,
        out_shape=[
            jax.ShapeDtypeStruct((28, D + 2 * KVH * HD), F32),
            jax.ShapeDtypeStruct((28, D), F32),
            jax.ShapeDtypeStruct((4, 128), F32),
        ],
        compiler_params=pltpu.CompilerParams(vmem_limit_bytes=VMEM_BYTES),
        cost_estimate=pl.CostEstimate(flops=0, bytes_accessed=2**20, transcendentals=0),
        name="finish",
    )(parts)


def out_wgrad_kernel(core_ref, attn_ref, branch_ref, keep_ref, give_ref):
    wgrad = rows_inner(attn_ref[...], branch_ref[...]).astype(BF)
    for group in range(2):

        @pl.when(core_ref[0] == group)
        def _():
            keep_ref[...] = wgrad[:, QC * group : QC * (group + 1)]
            give_ref[...] = wgrad[:, QC * (1 - group) : QC * (2 - group)]


def out_wgrad(core, attn, branch_grad):
    smem = pl.BlockSpec(memory_space=pltpu.SMEM)
    vmem = pl.BlockSpec(memory_space=pltpu.VMEM)
    return pl.pallas_call(
        out_wgrad_kernel,
        in_specs=[smem, vmem, vmem],
        out_shape=[jax.ShapeDtypeStruct((QC, QC), BF)] * 2,
        compiler_params=pltpu.CompilerParams(vmem_limit_bytes=VMEM_BYTES),
        cost_estimate=pl.CostEstimate(flops=0, bytes_accessed=0, transcendentals=0),
        name="out_wgrad",
    )(core, attn, branch_grad)


def deal_kernel(parts_ref, gate_ref, up_ref, down_ref, rows_ref):
    for t in range(4):
        source_ref = parts_ref.at[t % 2 * 2 + t // 2]
        for which, ref in enumerate((gate_ref, up_ref)):
            for run in range(32):
                target, place, left = 152 * run + 38 * t, 40 * run, 38
                while left:
                    size = min(left, CH - place % CH)
                    source = place // CH * 2 * CH + which * CH + place % CH
                    part = source_ref[:, source : source + size]
                    ref[:, target : target + size] = part.astype(F32)
                    target, place, left = target + size, place + size, left - size
        for piece in range(70):
            row, lane = 4 * (piece // 10), 2 * FFP + 128 * (piece % 10)
            part = source_ref[row : row + 4, lane : lane + 128].astype(F32)
            row, lane = 4 * (piece // 7), 128 * (piece % 7)
            rows_ref[row : row + 4, lane : lane + 128] = part
        down_ref[38 * t : 38 * t + 38, :] = rows_ref[:38, :]


def deal(parts):
    return pl.pallas_call(
        deal_kernel,
        out_shape=[
            jax.ShapeDtypeStruct((28, FF), F32),
            jax.ShapeDtypeStruct((28, FF), F32),
            jax.ShapeDtypeStruct((152, D), F32),
        ],
        scratch_shapes=[pltpu.VMEM((40, D), F32)],
        compiler_params=pltpu.CompilerParams(vmem_limit_bytes=VMEM_BYTES),
        cost_estimate=pl.CostEstimate(flops=0, bytes_accessed=0, transcendentals=0),
        name="deal",
    )(parts)


def shards(
    tokens,
    attn_gain,
    qkv_weight,
    qk_bias,
    value_bias,
    out_weight,
    mlp_gain,
    gate_weight,
    up_weight,
    down_weight,
    cotangent,
):
    yl, c, z, x, yh = [lax.axis_index(name) for name in AXES]
    ctx = yl * 2 + c
    rows = 2 * BLK

    tok = tokens.reshape(rows, D)
    out_grad = cotangent.reshape(rows, D)
    chip = jnp.stack([yl])
    core = jnp.stack([c])

    vectors = jnp.concatenate([attn_gain, mlp_gain, qk_bias, value_bias])
    vec_count = vectors.shape[0]
    packed = jnp.concatenate(
        [
            lax.dynamic_slice_in_dim(qkv_weight, c * QC, QC, 1),
            lax.dynamic_slice_in_dim(qkv_weight, D + c * HD, HD, 1),
            lax.dynamic_slice_in_dim(qkv_weight, D + KVH * HD + c * HD, HD, 1),
            lax.dynamic_slice_in_dim(out_weight, c * QC, QC, 1),
        ],
        axis=1,
    )
    vec_rows = jnp.zeros((4, PACK), BF).at[0, :vec_count].set(vectors)
    packed = jnp.concatenate([packed, vec_rows], axis=0)
    packed, gate_weight, up_weight, down_weight = lax.optimization_barrier(
        (packed, gate_weight, up_weight, down_weight)
    )
    low, high = ordered(packed, swap(packed, "yh"), yh)
    packed = jnp.concatenate([low[:28], high[:28], low[28:], high[28:]], axis=0)
    packed = jnp.broadcast_to(packed, (16, 64, PACK))

    tok_two = lax.all_gather(tok, "c", axis=0, tiled=True)
    gu_part, down_part = quarter(jnp.stack([ctx]), gate_weight, up_weight, down_weight)
    gu_part = jnp.concatenate(ordered(gu_part, swap(gu_part, "yh"), yh), axis=0)
    down_part = jnp.concatenate(ordered(down_part, swap(down_part, "yh"), yh), axis=0)
    grads_far = swap(out_grad, "yl")
    mlp_part = jnp.concatenate([gu_part, tiles_down(down_part)], axis=1)
    places = jnp.stack([2 * yl, 7 - 2 * yl, 2 * yl + 1, 6 - 2 * yl])
    positions = places[:, None] * BLK + jnp.arange(BLK, dtype=jnp.int32)[None, :]
    freqs = THETA ** (-(jnp.arange(HD // 2, dtype=F32) * 2.0 / HD))
    turns = positions.astype(F32)[:, None, :] * freqs[None, :, None]
    cosine, sine = jnp.cos(turns), jnp.sin(turns)
    mlp_part, packed = lax.optimization_barrier((mlp_part, packed))
    packed = lax.all_to_all(packed, ("z", "x"), 0, 0, tiled=True)
    mlp_all = lax.all_gather(mlp_part, ("z", "x"), axis=0, tiled=True)

    normed_in, query, kv_own, gain_two, qkv_half = project(core, tok_two, packed, cosine, sine)
    packed, kv_own, grads_far = lax.optimization_barrier((packed, kv_own, grads_far))
    gain_one = packed[:, 56::4, :28].reshape(1, D).astype(F32)
    out_cols = packed[:, :56, PC:].reshape(2, QC, QC)
    kv = lax.all_gather(kv_own, "yl", axis=0, tiled=True)

    attn, total = attend(chip, query, kv)
    out_give = lax.dynamic_index_in_dim(out_cols, 1 - c, 0, keepdims=False)
    out_keep = lax.dynamic_index_in_dim(out_cols, c, 0, keepdims=False)
    out_half = jnp.concatenate(ordered(out_keep, swap(out_give, "c"), c), axis=1)
    grads = [out_grad, grads_far, swap(out_grad, "c"), swap(grads_far, "c")]

    def own_rows(parts):
        return lax.dynamic_slice_in_dim(parts, c * rows, rows, 0)

    def chip_sum(parts):
        give = lax.dynamic_slice_in_dim(parts, (1 - c) * rows, rows, 0)
        return own_rows(parts).astype(F32) + swap(give, "c").astype(F32)

    attn_give = lax.dynamic_slice_in_dim(attn, (1 - c) * rows, rows, 0)
    branch_come = swap(dot(attn_give, out_half).astype(BF), "c")
    inputs = tok.astype(F32)
    hidden = inputs + dot(own_rows(attn), out_half) + branch_come.astype(F32)
    hidden, *grads = lax.optimization_barrier((hidden, *grads))

    inverse_two = lax.rsqrt(jnp.mean(hidden * hidden, axis=-1, keepdims=True) + EPSILON)
    normed_two = hidden * inverse_two
    normed_mid = (normed_two * gain_two).astype(BF)
    mid_far = swap(normed_mid, "yl")
    mids = [normed_mid, mid_far, swap(normed_mid, "c"), swap(mid_far, "c")]
    inner, gu_grad, down_t, gu_parts = mlp(mids, grads, mlp_all)
    gu_sum = lax.psum_scatter(gu_parts, "z", scatter_dimension=0, tiled=True)
    mid_keep, mid_give = mid(gu_grad, mlp_all)

    def group_sum(keep, come):
        far = keep[rows:].astype(F32) + come[rows:].astype(F32)
        away = swap(far.astype(BF), "yl")
        return keep[:rows].astype(F32) + come[:rows].astype(F32) + away.astype(F32)

    mid_come = swap(mid_give, "c")
    mid_grad = group_sum(mid_keep, mid_come)

    inner, mid_come = lax.optimization_barrier((inner, mid_come))
    down_parts = down_wgrad(inner, grads)
    mid_grad = after(mid_grad, down_parts)

    gain_two_grad = jnp.sum(mid_grad * normed_two, axis=0, keepdims=True)
    hidden_grad = out_grad.astype(F32) + norm_back(mid_grad * gain_two, normed_two, inverse_two)
    branch_grad = lax.all_gather(hidden_grad.astype(BF), "c", axis=0, tiled=True)
    down_pieces = lax.all_to_all(down_parts.reshape(4, 320, D), "x", 0, 0, tiled=True)
    query_grad, kv_keep, kv_give = attend_back(
        chip, query, kv, out_half, total, branch_grad, cosine, sine
    )
    kv_come = swap(kv_give, "yl")
    out_keep, out_give = out_wgrad(core, attn, after(branch_grad, kv_give))
    out_come = swap(out_give, "c")
    qkv_wgrad, in_parts = project_back(
        core,
        query_grad,
        kv_keep,
        kv_come,
        normed_in,
        tok_two,
        qkv_half,
        gain_two_grad,
        out_keep,
        out_come,
        cosine,
        sine,
    )

    gu_sum = after(gu_sum, kv_come).reshape(4, 56, 2 * FFP)
    gu_sum = lax.psum_scatter(gu_sum, "x", scatter_dimension=0, tiled=True)
    qkv_wparts = lax.all_to_all(qkv_wgrad, ("z", "x"), 0, 0, tiled=True)
    in_give = lax.dynamic_slice_in_dim(in_parts, (1 - c) * rows, rows, 0)
    in_come = swap(in_give, "c")
    down_pieces, in_come = lax.optimization_barrier((down_pieces, in_come))
    down_sum = sum4(down_pieces).reshape(4, 80, D)
    down_pieces = spread4(down_sum, "z", z)
    inner, down_sum = lax.optimization_barrier((inner, down_sum))
    out_keep, out_give = mlp_out(inner, down_t)
    out_come = swap(out_give, "c")
    out_far = far_rows(out_keep, out_come)
    input_grad = input_back(core, hidden_grad, in_parts, in_come, tok, gain_one)
    gu_sum, input_grad, out_far = lax.optimization_barrier((gu_sum, input_grad, out_far))
    keep, give = halves(jnp.stack([yh]), gu_sum.reshape(56, 2 * FFP), down_pieces)
    out_away = swap(out_far, "yl")
    qkv_wparts, give, out_away, input_grad = lax.optimization_barrier(
        (qkv_wparts, give, out_away, input_grad)
    )
    packed_sum = part_sum(qkv_wparts)
    packed_sum, give = lax.optimization_barrier((packed_sum, give))
    mixed = hidden + out_keep[:rows].astype(F32) + out_come[:rows].astype(F32)
    mixed = (mixed + out_away.astype(F32)).astype(BF)
    packed_sum = lax.all_to_all(packed_sum, ("yl", "c", "yh"), 0, 0, tiled=True)

    mlp_sum = (keep.astype(F32) + swap(give, "yh").astype(F32)).astype(BF)
    mlp_pair = jnp.stack(ordered(mlp_sum, swap(mlp_sum, "yl"), yl))
    mlp_pair = lax.all_gather(mlp_pair, "c", axis=0).reshape(4, 28, 3 * FFP)
    qkv_own, out_own, vec_own = finish(packed_sum)
    mlp_pair, qkv_own, mixed = lax.optimization_barrier((mlp_pair, qkv_own, mixed))
    gate_own, up_own, down_own = deal(mlp_pair)

    def own_vector(row, size):
        return lax.dynamic_slice_in_dim(vec_own[row], yh * size, size, 0)

    return (
        mixed.reshape(tokens.shape),
        input_grad.reshape(tokens.shape),
        own_vector(0, 28),
        qkv_own,
        own_vector(2, 32),
        own_vector(3, 4),
        out_own,
        own_vector(1, 28),
        gate_own,
        up_own,
        down_own,
    )


def solution(mesh):
    devices = mesh.devices.reshape(2, 2, 4, 4, 2)
    split = Mesh(devices, AXES)
    ctx, fsdp = ("yl", "c"), ("z", "x", "yh")
    rows = P(fsdp, None, ctx, None, None)
    in_specs = (
        rows,
        P(fsdp),
        P(fsdp, None),
        P(fsdp),
        P(fsdp),
        P(fsdp, None),
        P(fsdp),
        P(fsdp, None),
        P(fsdp, None),
        P(fsdp, None),
        rows,
    )
    out_specs = (
        rows,
        rows,
        P(fsdp),
        P(fsdp, None),
        P(fsdp),
        P(fsdp),
        P(fsdp, None),
        P(fsdp),
        P(fsdp, None),
        P(fsdp, None),
        P(fsdp, None),
    )
    return jax.shard_map(
        shards, mesh=split, in_specs=in_specs, out_specs=out_specs, check_vma=False
    )
```

```python
import jax
import jax.numpy as jnp
from jax import lax
from jax.experimental import pallas as pl
from jax.experimental.pallas import tpu as pltpu
from jax.sharding import Mesh, PartitionSpec as P

KVH = 2
HD = 64
REP = 7
D = 896
FF = 4864
FFT = FF // 4
CH = 256
CHUNKS = 5
FFP = CH * CHUNKS
VMEM_BYTES = 60 * 2**20
QC = REP * HD
STACK = REP * 128
PC = QC + 2 * HD
PACK = PC + QC
BLK = 128
EPSILON = 1e-06
THETA = 1000000.0
AXES = ("yl", "c", "z", "x", "yh")
BF = jnp.bfloat16
F32 = jnp.float32


def shift(value, axis, size, step):
    return lax.ppermute(value, axis, [(i, (i + step) % size) for i in range(size)])


def swap(value, axis):
    return shift(value, axis, 2, 1)


def angles(positions):
    freqs = THETA ** (-(jnp.arange(HD // 2, dtype=F32) * 2.0 / HD))
    return positions.astype(F32)[:, None] * freqs[None, :]


def rows_inner(left, right):
    return lax.dot_general(left, right, (((0,), (0,)), ((), ())), preferred_element_type=F32)


def cols_inner(left, right):
    return lax.dot_general(left, right, (((1,), (1,)), ((), ())), preferred_element_type=F32)


def dot(left, right):
    return jnp.dot(left, right, preferred_element_type=F32)


def norm_back(grad_normed, normed, inverse):
    return inverse * (grad_normed - normed * jnp.mean(grad_normed * normed, axis=-1, keepdims=True))


def ordered(own, other, place):
    first = jnp.where(place == 0, own, other)
    second = jnp.where(place == 0, other, own)
    return first, second


def spread4(parts, axis, place):
    def part(step):
        return lax.dynamic_index_in_dim(parts, (place + step) % 4, 0, keepdims=False)

    return [
        part(0),
        shift(part(1), axis, 4, 1),
        shift(part(3), axis, 4, 3),
        shift(part(2), axis, 4, 2),
    ]


def total4(pieces):
    return sum(piece.astype(F32) for piece in pieces).astype(BF)


def scatter2(parts, axis, place):
    keep = lax.dynamic_index_in_dim(parts, place, 0, keepdims=False)
    give = lax.dynamic_index_in_dim(parts, 1 - place, 0, keepdims=False)
    return (keep.astype(F32) + swap(give, axis).astype(F32)).astype(BF)


def after(value, *others):
    return lax.optimization_barrier((value,) + others)[0]


def quarter_kernel(ctx_ref, gate_ref, up_ref, down_ref, gu_out_ref, down_out_ref):
    gu_out_ref[...] = jnp.zeros_like(gu_out_ref)
    down_out_ref[...] = jnp.zeros_like(down_out_ref)
    for t in range(4):

        @pl.when(ctx_ref[0] == t)
        def _():
            down_out_ref[:38, :] = down_ref[38 * t : 38 * t + 38, :]
            for which, ref in enumerate((gate_ref, up_ref)):
                for run in range(32):
                    source, place, left = 152 * run + 38 * t, 40 * run, 38
                    while left:
                        size = min(left, CH - place % CH)
                        target = place // CH * 2 * CH + which * CH + place % CH
                        gu_out_ref[:, target : target + size] = ref[:, source : source + size]
                        source, place, left = source + size, place + size, left - size


def quarter(ctx, gate, up, down):
    smem = pl.BlockSpec(memory_space=pltpu.SMEM)
    vmem = pl.BlockSpec(memory_space=pltpu.VMEM)
    return pl.pallas_call(
        quarter_kernel,
        in_specs=[smem, vmem, vmem, vmem],
        out_shape=[
            jax.ShapeDtypeStruct((gate.shape[0], 2 * FFP), BF),
            jax.ShapeDtypeStruct((40, D), BF),
        ],
        compiler_params=pltpu.CompilerParams(vmem_limit_bytes=16 * 2**20),
        cost_estimate=pl.CostEstimate(flops=0, bytes_accessed=0, transcendentals=0),
        name="quarter",
    )(ctx, gate, up, down)


def tiles_down(part):
    return part.reshape(10, 8, 7, 128).transpose(2, 1, 0, 3).reshape(56, FFP)


PARTS = 4


def mlp_kernel(*refs):
    rows_refs, grads_refs = refs[:PARTS], refs[PARTS : 2 * PARTS]
    gu_ref, tiles_ref, inner_ref, gu_grad_ref, down_ref, wgrad_ref, turned_rows = refs[2 * PARTS :]
    step = pl.program_id(0)
    size = rows_refs[0].shape[0]

    @pl.when(step == 0)
    def _():
        for p in range(PARTS):
            turned_rows[:, p * size : (p + 1) * size] = jnp.transpose(rows_refs[p][...])

        for s in range(16):
            for pair in range(5):
                for lane in range(7):
                    rows = slice(56 * s + 8 * lane, 56 * s + 8 * lane + 8)
                    first = tiles_ref[rows, 256 * pair : 256 * pair + 128]
                    second = tiles_ref[rows, 256 * pair + 128 : 256 * pair + 256]
                    target = slice(80 * s + 16 * pair, 80 * s + 16 * pair + 16)
                    down_ref[target, 128 * lane : 128 * lane + 128] = jnp.concatenate(
                        [first, second], axis=0
                    )

    gate_w, up_w = gu_ref[:, :CH], gu_ref[:, CH:]
    down_w = down_ref[pl.ds(pl.multiple_of(step * CH, CH), CH), :]
    for p in range(PARTS):
        span = slice(p * size, (p + 1) * size)
        gate = dot(rows_refs[p][...], gate_w)
        up = dot(rows_refs[p][...], up_w)
        inner_grad = cols_inner(grads_refs[p][...], down_w)
        sigma = 0.5 + 0.5 * jnp.tanh(0.5 * gate)
        silu = gate * sigma
        slope = sigma + silu - silu * sigma
        inner_ref[span, :] = (silu * up).astype(BF)
        gu_grad_ref[span, :CH] = (inner_grad * up * slope).astype(BF)
        gu_grad_ref[span, CH:] = (inner_grad * silu).astype(BF)
    wgrad = dot(turned_rows[...], gu_grad_ref[...])
    wgrad_ref[...] = wgrad.astype(BF).reshape(wgrad_ref.shape)


def mlp(rows, grads, weights):
    size = rows[0].shape[0]
    count = PARTS * size
    whole = pl.BlockSpec((size, D), lambda j: (0, 0))
    return pl.pallas_call(
        mlp_kernel,
        grid=(CHUNKS,),
        in_specs=[
            *[whole] * (2 * PARTS),
            pl.BlockSpec((D, 2 * CH), lambda j: (0, j)),
            pl.BlockSpec((D, FFP), lambda j: (0, 2)),
        ],
        out_specs=[
            pl.BlockSpec((count, CH), lambda j: (0, j)),
            pl.BlockSpec((count, 2 * CH), lambda j: (0, j)),
            pl.BlockSpec((FFP, D), lambda j: (0, 0)),
            pl.BlockSpec((4, D // 4, 2 * CH), lambda j: (0, 0, j)),
        ],
        out_shape=[
            jax.ShapeDtypeStruct((count, FFP), BF),
            jax.ShapeDtypeStruct((count, 2 * FFP), BF),
            jax.ShapeDtypeStruct((FFP, D), BF),
            jax.ShapeDtypeStruct((4, D // 4, 2 * FFP), BF),
        ],
        scratch_shapes=[pltpu.VMEM((D, count), BF)],
        compiler_params=pltpu.CompilerParams(vmem_limit_bytes=VMEM_BYTES),
        cost_estimate=pl.CostEstimate(
            flops=10 * count * D * FFP, bytes_accessed=24 * 2**20, transcendentals=count * FFP
        ),
        name="mlp",
    )(*rows, *grads, weights, weights)


def mid_kernel(gu_grad_ref, gu_ref, keep_ref, give_ref):
    part = cols_inner(gu_grad_ref[...], gu_ref[...]).astype(BF)
    step = pl.program_id(0)

    @pl.when(step < PARTS // 2)
    def _():
        keep_ref[...] = part

    @pl.when(step >= PARTS // 2)
    def _():
        give_ref[...] = part


def mid(gu_grad, weights):
    count = gu_grad.shape[0]
    return pl.pallas_call(
        mid_kernel,
        grid=(PARTS,),
        in_specs=[
            pl.BlockSpec((count // PARTS, 2 * FFP), lambda j: (j, 0)),
            pl.BlockSpec((D, 2 * FFP), lambda j: (0, 0)),
        ],
        out_specs=[
            pl.BlockSpec((count // PARTS, D), lambda j: (jnp.minimum(j, PARTS // 2 - 1), 0)),
            pl.BlockSpec((count // PARTS, D), lambda j: (jnp.maximum(j - PARTS // 2, 0), 0)),
        ],
        out_shape=[jax.ShapeDtypeStruct((count // 2, D), BF)] * 2,
        compiler_params=pltpu.CompilerParams(vmem_limit_bytes=60 * 2**20),
        cost_estimate=pl.CostEstimate(
            flops=4 * count * D * FFP, bytes_accessed=12 * 2**20, transcendentals=0
        ),
        name="mid",
    )(gu_grad, weights)


def mlp_out_kernel(inner_ref, down_ref, keep_ref, give_ref):
    half = keep_ref.shape[0]
    keep_ref[...] = dot(inner_ref[:half, :], down_ref[...]).astype(BF)
    give_ref[...] = dot(inner_ref[half:, :], down_ref[...]).astype(BF)


def mlp_out(inner, down):
    count = inner.shape[0]
    return pl.pallas_call(
        mlp_out_kernel,
        out_shape=[jax.ShapeDtypeStruct((count // 2, D), BF)] * 2,
        compiler_params=pltpu.CompilerParams(vmem_limit_bytes=24 * 2**20),
        cost_estimate=pl.CostEstimate(flops=0, bytes_accessed=0, transcendentals=0),
        name="mlp_out",
    )(inner, down)


def down_wgrad_kernel(inner_ref, *refs):
    grads = jnp.concatenate([ref[...] for ref in refs[:PARTS]], axis=0)
    part = rows_inner(inner_ref[...], grads).astype(BF)
    for j in range(CHUNKS):

        @pl.when(pl.program_id(0) == j)
        def _():
            place = CH * j
            while place < CH * (j + 1):
                run, start = place // 80, place % 80
                size = min(80 - start, CH * (j + 1) - place)
                rows = part[place - CH * j : place - CH * j + size]
                refs[PARTS][run % 4, run // 4, start : start + size, :] = rows
                place += size


def down_wgrad(inner, grads):
    count = inner.shape[0]
    return pl.pallas_call(
        down_wgrad_kernel,
        grid=(CHUNKS,),
        in_specs=[
            pl.BlockSpec((count, CH), lambda j: (0, j)),
            *[pl.BlockSpec((count // PARTS, D), lambda j: (0, 0))] * PARTS,
        ],
        out_specs=pl.BlockSpec((4, 4, 80, D), lambda j: (0, 0, 0, 0)),
        out_shape=jax.ShapeDtypeStruct((4, 4, 80, D), BF),
        compiler_params=pltpu.CompilerParams(vmem_limit_bytes=24 * 2**20),
        cost_estimate=pl.CostEstimate(flops=0, bytes_accessed=0, transcendentals=0),
        name="down_wgrad",
    )(inner, *grads)


ORDER = (0, 7, 1, 6, 2, 5, 3, 4)
LENGTHS = {1: (0, 0), 8: (1, 0), 2: (2, 0), 7: (3, 0), 3: (0, 1), 6: (1, 1), 4: (2, 1), 5: (3, 1)}


def turned(value, cosine, sine):
    first, second = value[: HD // 2], value[HD // 2 :]
    return jnp.concatenate(
        [first * cosine - second * sine, second * cosine + first * sine], axis=0
    )


def project_kernel(
    core_ref,
    tok_ref,
    packed_ref,
    cos_ref,
    sin_ref,
    rows_ref,
    query_ref,
    kv_ref,
    gain,
    gain_two_ref,
    weight,
    out_ref,
    bias,
):
    for s in range(16):
        span = slice(56 * s, 56 * s + 56)
        weight[span, :] = packed_ref[s, :56, :PC]
        out_ref[s // 8, 56 * (s % 8) : 56 * (s % 8) + 56, :] = packed_ref[s, :56, PC:]
        gain[:, span] = packed_ref[s, 56:57, :56].astype(F32)
        gain_two_ref[:, span] = packed_ref[s, 57:58, :56].astype(F32)
    for group in range(2):

        @pl.when(core_ref[0] == group)
        def _():
            for head in range(REP):
                part = packed_ref[REP * group + head, 58:59, :HD]
                bias[:, HD * head : HD * (head + 1)] = part.astype(F32)
            bias[:, QC : QC + HD] = packed_ref[14 + group, 58:59, :HD].astype(F32)
            for run in range(8):
                part = packed_ref[8 * group + run, 59:60, :8]
                bias[:, QC + HD + 8 * run : QC + HD + 8 * run + 8] = part.astype(F32)

    inputs = tok_ref[...].astype(F32)
    inverse = lax.rsqrt(jnp.mean(inputs * inputs, axis=-1, keepdims=True) + EPSILON)
    rows = (inputs * inverse * gain[...]).astype(BF)
    rows_ref[...] = rows
    projected = dot(rows, weight[...]) + bias[...]
    for b in range(4):
        cosine, sine = cos_ref[b], sin_ref[b]
        block = projected[b * BLK : (b + 1) * BLK]
        for pair in range(4):
            both = jnp.transpose(block[:, 2 * HD * pair : 2 * HD * (pair + 1)])
            head = turned(both[:HD], cosine, sine).astype(BF)
            query_ref[b, :, 2 * pair * BLK : (2 * pair + 1) * BLK] = head
            other = turned(both[HD:], cosine, sine)
            if pair < 3:
                query_ref[b, :, (2 * pair + 1) * BLK : (2 * pair + 2) * BLK] = other.astype(BF)
            else:
                value = block[:, QC + HD :]
                kv_ref[b * BLK : (b + 1) * BLK, :] = jnp.concatenate(
                    [jnp.transpose(other), value], axis=1
                ).astype(BF)


def project(core, tok, packed, cosine, sine):
    smem = pl.BlockSpec(memory_space=pltpu.SMEM)
    vmem = pl.BlockSpec(memory_space=pltpu.VMEM)
    return pl.pallas_call(
        project_kernel,
        in_specs=[smem] + [vmem] * 4,
        out_shape=[
            jax.ShapeDtypeStruct((4 * BLK, D), BF),
            jax.ShapeDtypeStruct((4, HD, STACK), BF),
            jax.ShapeDtypeStruct((4 * BLK, 2 * HD), BF),
            jax.ShapeDtypeStruct((1, D), F32),
            jax.ShapeDtypeStruct((1, D), F32),
            jax.ShapeDtypeStruct((D, PC), BF),
            jax.ShapeDtypeStruct((2, QC, QC), BF),
        ],
        scratch_shapes=[pltpu.VMEM((1, PC), F32)],
        compiler_params=pltpu.CompilerParams(vmem_limit_bytes=32 * 2**20),
        cost_estimate=pl.CostEstimate(
            flops=2 * 4 * BLK * D * PC, bytes_accessed=6 * 2**20, transcendentals=0
        ),
        name="project",
    )(core, tok, packed, cosine, sine)


def split_kv(kv_ref, keys, values):
    for place, block in enumerate(ORDER):
        rows = kv_ref[place * BLK : (place + 1) * BLK, :]
        keys[block * BLK : (block + 1) * BLK, :] = rows[:, :HD]
        values[block * BLK : (block + 1) * BLK, :] = rows[:, HD:]


def masked_scores(keys, query, length):
    scores = dot(keys[: length * BLK, :], query) * HD ** (-0.5)
    key = lax.broadcasted_iota(jnp.int32, (BLK, STACK), 0)
    token = lax.rem(lax.broadcasted_iota(jnp.int32, (BLK, STACK), 1), BLK)
    last = jnp.where(key <= token, scores[(length - 1) * BLK :], -1e30)
    if length == 1:
        return last
    return jnp.concatenate([scores[: (length - 1) * BLK], last], axis=0)


def heads_out(stacked, ref, block):
    rows = slice(block * BLK, (block + 1) * BLK)
    for pair in range(3):
        first = stacked[:, 2 * pair * BLK : (2 * pair + 1) * BLK]
        second = stacked[:, (2 * pair + 1) * BLK : (2 * pair + 2) * BLK]
        both = jnp.transpose(jnp.concatenate([first, second], axis=0))
        ref[rows, 2 * HD * pair : 2 * HD * (pair + 1)] = both.astype(ref.dtype)
    ref[rows, 6 * HD :] = jnp.transpose(stacked[:, 6 * BLK :]).astype(ref.dtype)


def attend_kernel(chip_ref, query_ref, kv_ref, attn_ref, total_ref, keys, values):
    split_kv(kv_ref, keys, values)
    for length, (block, chip) in LENGTHS.items():

        @pl.when(chip_ref[0] == chip)
        def _():
            scores = masked_scores(keys, query_ref[block], length)
            top = jnp.max(scores, axis=0, keepdims=True)
            prob = jnp.exp(scores - top)
            total = jnp.sum(prob, axis=0, keepdims=True)
            total_ref[block] = top + jnp.log(total)
            attn = rows_inner(values[: length * BLK, :], prob.astype(BF)) / total
            heads_out(attn, attn_ref, block)


def attend(chip, query, kv):
    smem = pl.BlockSpec(memory_space=pltpu.SMEM)
    vmem = pl.BlockSpec(memory_space=pltpu.VMEM)
    return pl.pallas_call(
        attend_kernel,
        in_specs=[smem, vmem, vmem],
        out_shape=[
            jax.ShapeDtypeStruct((4 * BLK, QC), BF),
            jax.ShapeDtypeStruct((4, 1, STACK), F32),
        ],
        scratch_shapes=[pltpu.VMEM((8 * BLK, HD), BF), pltpu.VMEM((8 * BLK, HD), BF)],
        compiler_params=pltpu.CompilerParams(vmem_limit_bytes=32 * 2**20),
        cost_estimate=pl.CostEstimate(
            flops=2 * 18 * BLK * STACK * HD * 8, bytes_accessed=4 * 2**20, transcendentals=2**21
        ),
        name="attend",
    )(chip, query, kv)


def attend_back_kernel(
    chip_ref,
    query_ref,
    kv_ref,
    out_ref,
    total_ref,
    branch_ref,
    cos_ref,
    sin_ref,
    grad_ref,
    keep_ref,
    give_ref,
    keys,
    values,
    key_sum,
    value_sum,
    heads,
):
    split_kv(kv_ref, keys, values)
    key_sum[...] = jnp.zeros_like(key_sum)
    value_sum[...] = jnp.zeros_like(value_sum)
    attn_grad = cols_inner(branch_ref[...], out_ref[...])
    for b in range(4):
        part = attn_grad[b * BLK : (b + 1) * BLK]
        for pair in range(4):
            both = jnp.transpose(part[:, 2 * HD * pair : min(2 * HD * (pair + 1), QC)]).astype(BF)
            heads[b, :, 2 * pair * BLK : (2 * pair + 1) * BLK] = both[:HD]
            if pair < 3:
                heads[b, :, (2 * pair + 1) * BLK : (2 * pair + 2) * BLK] = both[HD:]
    for length, (block, chip) in LENGTHS.items():

        @pl.when(chip_ref[0] == chip)
        def _():
            span = length * BLK
            query = query_ref[block]
            grads = heads[block]
            prob = jnp.exp(masked_scores(keys, query, length) - total_ref[block])
            prob_grad = dot(values[:span, :], grads)
            weighted = jnp.sum(prob * prob_grad, axis=0, keepdims=True)
            score_grad = (prob * (prob_grad - weighted)).astype(BF)
            value_sum[:span, :] += cols_inner(prob.astype(BF), grads)
            key_sum[:span, :] += cols_inner(score_grad, query)
            query_grad = rows_inner(keys[:span, :], score_grad) * HD ** (-0.5)
            cosine = jnp.concatenate([cos_ref[block]] * REP, axis=1)
            sine = jnp.concatenate([sin_ref[block]] * REP, axis=1)
            heads_out(turned(query_grad, cosine, -sine), grad_ref, block)

    for place, block in enumerate(ORDER):
        span = slice(block * BLK, (block + 1) * BLK)
        both = jnp.concatenate([key_sum[span, :] * HD ** (-0.5), value_sum[span, :]], axis=1)
        rows = slice(place % 4 * BLK, (place % 4 + 1) * BLK)

        @pl.when(chip_ref[0] == place // 4)
        def _():
            keep_ref[rows, :] = both

        @pl.when(chip_ref[0] != place // 4)
        def _():
            give_ref[rows, :] = both.astype(BF)


def attend_back(chip, query, kv, out_half, total, branch_grad, cosine, sine):
    smem = pl.BlockSpec(memory_space=pltpu.SMEM)
    vmem = pl.BlockSpec(memory_space=pltpu.VMEM)
    return pl.pallas_call(
        attend_back_kernel,
        in_specs=[smem] + [vmem] * 7,
        out_shape=[
            jax.ShapeDtypeStruct((4 * BLK, QC), BF),
            jax.ShapeDtypeStruct((4 * BLK, 2 * HD), F32),
            jax.ShapeDtypeStruct((4 * BLK, 2 * HD), BF),
        ],
        scratch_shapes=[
            pltpu.VMEM((8 * BLK, HD), BF),
            pltpu.VMEM((8 * BLK, HD), BF),
            pltpu.VMEM((8 * BLK, HD), F32),
            pltpu.VMEM((8 * BLK, HD), F32),
            pltpu.VMEM((4, HD, STACK), BF),
        ],
        compiler_params=pltpu.CompilerParams(vmem_limit_bytes=40 * 2**20),
        cost_estimate=pl.CostEstimate(
            flops=2 * 18 * BLK * STACK * HD * 20, bytes_accessed=6 * 2**20, transcendentals=2**21
        ),
        name="attend_back",
    )(chip, query, kv, out_half, total, branch_grad, cosine, sine)


def project_back_kernel(
    core_ref,
    grad_ref,
    keep_ref,
    come_ref,
    rows_ref,
    tok_ref,
    weight_ref,
    gain_two_ref,
    out_keep_ref,
    out_come_ref,
    cos_ref,
    sin_ref,
    wgrad_ref,
    in_ref,
):
    kv_grad = keep_ref[...] + come_ref[...].astype(F32)
    keys = []
    for b in range(4):
        key = jnp.transpose(kv_grad[b * BLK : (b + 1) * BLK, :HD])
        keys.append(jnp.transpose(turned(key, cos_ref[b], -sin_ref[b])))
    key_back = jnp.concatenate(keys, axis=0)
    grads = jnp.concatenate(
        [grad_ref[...], key_back.astype(BF), kv_grad[:, HD:].astype(BF)], axis=1
    )
    wgrad = rows_inner(rows_ref[...], grads).astype(BF)
    in_part = cols_inner(grads, weight_ref[...])
    in_ref[...] = in_part.astype(BF)
    inputs = tok_ref[...].astype(F32)
    inverse = lax.rsqrt(jnp.mean(inputs * inputs, axis=-1, keepdims=True) + EPSILON)
    gain_one = jnp.sum(in_part * inputs * inverse, axis=0, keepdims=True)
    gain_two = gain_two_ref[...]
    bias = jnp.sum(grads.astype(F32), axis=0, keepdims=True)
    core = core_ref[0]
    wgrad_ref[:, 56:, :] = jnp.zeros((16, 8, PACK), BF)
    for group in range(2):

        @pl.when(core == group)
        def _():
            for s in range(8):
                span = slice(56 * s, 56 * s + 56)
                wgrad_ref[8 * group + s, :56, PC:] = out_keep_ref[span, :]
                wgrad_ref[8 * (1 - group) + s, :56, PC:] = out_come_ref[span, :]

    for s in range(16):
        wgrad_ref[s, :56, :PC] = wgrad[56 * s : 56 * s + 56]
        group, start = (s // 7, HD * (s % 7)) if s < 14 else (s - 14, QC)
        qk = jnp.where(core == group, bias[:, start : start + HD], 0.0)
        start = QC + HD + 8 * (s % 8)
        value = jnp.where(core == s // 8, bias[:, start : start + 8], 0.0)
        wgrad_ref[s, 56:57, :56] = gain_one[:, 56 * s : 56 * s + 56].astype(BF)
        wgrad_ref[s, 57:58, :56] = gain_two[:, 56 * s : 56 * s + 56].astype(BF)
        wgrad_ref[s, 58:59, :HD] = qk.astype(BF)
        wgrad_ref[s, 59:60, :8] = value.astype(BF)


def project_back(
    core, grad, keep, come, rows, tok, weight, gain_two, out_keep, out_come, cosine, sine
):
    smem = pl.BlockSpec(memory_space=pltpu.SMEM)
    vmem = pl.BlockSpec(memory_space=pltpu.VMEM)
    return pl.pallas_call(
        project_back_kernel,
        in_specs=[smem] + [vmem] * 11,
        out_shape=[
            jax.ShapeDtypeStruct((16, 64, PACK), BF),
            jax.ShapeDtypeStruct((4 * BLK, D), BF),
        ],
        compiler_params=pltpu.CompilerParams(vmem_limit_bytes=60 * 2**20),
        cost_estimate=pl.CostEstimate(
            flops=4 * 4 * BLK * D * PC, bytes_accessed=10 * 2**20, transcendentals=0
        ),
        name="project_back",
    )(core, grad, keep, come, rows, tok, weight, gain_two, out_keep, out_come, cosine, sine)


def sum4_kernel(parts_ref, out_ref):
    total = parts_ref[0].astype(F32)
    for s in range(1, 4):
        total += parts_ref[s].astype(F32)
    out_ref[...] = total.astype(BF)


def sum4(parts):
    _, count, width = parts.shape
    return pl.pallas_call(
        sum4_kernel,
        out_shape=jax.ShapeDtypeStruct((count, width), BF),
        compiler_params=pltpu.CompilerParams(vmem_limit_bytes=24 * 2**20),
        cost_estimate=pl.CostEstimate(flops=0, bytes_accessed=0, transcendentals=0),
        name="sum4",
    )(parts)


def small(kernel, shapes, *operands, name):
    vmem = pl.BlockSpec(memory_space=pltpu.VMEM)
    smem = pl.BlockSpec(memory_space=pltpu.SMEM)
    return pl.pallas_call(
        kernel,
        in_specs=[smem if value.dtype == jnp.int32 else vmem for value in operands],
        out_shape=shapes,
        compiler_params=pltpu.CompilerParams(vmem_limit_bytes=16 * 2**20),
        cost_estimate=pl.CostEstimate(flops=0, bytes_accessed=0, transcendentals=0),
        name=name,
    )(*operands)


def far_kernel(keep_ref, come_ref, out_ref):
    half = out_ref.shape[0]
    total = keep_ref[half:, :].astype(F32) + come_ref[half:, :].astype(F32)
    out_ref[...] = total.astype(BF)


def far_rows(keep, come):
    shape = jax.ShapeDtypeStruct((keep.shape[0] // 2, keep.shape[1]), BF)
    return small(far_kernel, shape, keep, come, name="far_rows")


def halves_kernel(place_ref, gu_ref, *refs):
    keep_ref, give_ref, total_ref = refs[4:]
    total_ref[...] = sum(ref[...].astype(F32) for ref in refs[:4])
    for place in range(2):

        @pl.when(place_ref[0] == place)
        def _():
            for ref, half in ((keep_ref, place), (give_ref, 1 - place)):
                ref[:, : 2 * FFP] = gu_ref[28 * half : 28 * half + 28, :]
                for piece in range(70):
                    row, lane = 40 * half + 4 * (piece // 7), 128 * (piece % 7)
                    part = total_ref[row : row + 4, lane : lane + 128].astype(BF)
                    row, lane = 4 * (piece // 10), 2 * FFP + 128 * (piece % 10)
                    ref[row : row + 4, lane : lane + 128] = part


def halves(place, gu, down_pieces):
    shape = jax.ShapeDtypeStruct((28, 3 * FFP), BF)
    vmem = pl.BlockSpec(memory_space=pltpu.VMEM)
    return pl.pallas_call(
        halves_kernel,
        in_specs=[pl.BlockSpec(memory_space=pltpu.SMEM)] + [vmem] * 5,
        out_shape=[shape, shape],
        scratch_shapes=[pltpu.VMEM((80, D), F32)],
        compiler_params=pltpu.CompilerParams(vmem_limit_bytes=24 * 2**20),
        cost_estimate=pl.CostEstimate(flops=0, bytes_accessed=0, transcendentals=0),
        name="halves",
    )(place, gu, *down_pieces)


def input_kernel(core_ref, grad_ref, parts_ref, come_ref, tok_ref, gain_ref, out_ref):
    size = come_ref.shape[0]
    for core in range(2):

        @pl.when(core_ref[0] == core)
        def _():
            part = parts_ref[core * size : (core + 1) * size, :].astype(F32)
            scaled = (part + come_ref[...].astype(F32)) * gain_ref[...]
            inputs = tok_ref[...].astype(F32)
            inverse = lax.rsqrt(jnp.mean(inputs * inputs, axis=-1, keepdims=True) + EPSILON)
            out_ref[...] = grad_ref[...] + norm_back(scaled, inputs * inverse, inverse)


def input_back(core, grad, parts, come, tok, gain):
    shape = jax.ShapeDtypeStruct(grad.shape, F32)
    return small(input_kernel, shape, core, grad, parts, come, tok, gain, name="input_back")


def part_sum_kernel(parts_ref, out_ref):
    total = parts_ref[0].astype(F32)
    for s in range(1, 16):
        total += parts_ref[s].astype(F32)
    total = total.astype(BF)
    for place in range(8):
        half = place % 2
        out_ref[place, :28, :] = total[28 * half : 28 * half + 28]
        out_ref[place, 28:, :] = jnp.zeros((4, PACK), BF)
        for row, size in enumerate((28, 28, 32, 4)):
            part = total[56 + row : 57 + row, size * half : size * (half + 1)]
            out_ref[place, 28 + row : 29 + row, :size] = part


def part_sum(parts):
    return pl.pallas_call(
        part_sum_kernel,
        out_shape=jax.ShapeDtypeStruct((8, 32, PACK), BF),
        compiler_params=pltpu.CompilerParams(vmem_limit_bytes=24 * 2**20),
        cost_estimate=pl.CostEstimate(flops=0, bytes_accessed=3 * 2**20, transcendentals=0),
        name="part_sum",
    )(parts)


def finish_kernel(parts_ref, qkv_ref, out_ref, *vec_refs):
    vectors = 0.0
    for group in range(2):
        total = 0.0
        for place in (0, 1, 4, 5):
            total += parts_ref[2 * group + place].astype(F32)
        rows = total[:28]
        vectors += total[28:, :128]
        qkv_ref[:, QC * group : QC * (group + 1)] = rows[:, :QC]
        qkv_ref[:, D + HD * group : D + HD * (group + 1)] = rows[:, QC : QC + HD]
        start = D + HD * (KVH + group)
        qkv_ref[:, start : start + HD] = rows[:, QC + HD : PC]
        out_ref[:, QC * group : QC * (group + 1)] = rows[:, PC:]
    for row, ref in enumerate(vec_refs):
        ref[...] = vectors[row : row + 1, : ref.shape[1]]


def finish(parts):
    return pl.pallas_call(
        finish_kernel,
        out_shape=[
            jax.ShapeDtypeStruct((28, D + 2 * KVH * HD), F32),
            jax.ShapeDtypeStruct((28, D), F32),
            *[jax.ShapeDtypeStruct((1, size), F32) for size in (28, 28, 32, 4)],
        ],
        compiler_params=pltpu.CompilerParams(vmem_limit_bytes=24 * 2**20),
        cost_estimate=pl.CostEstimate(flops=0, bytes_accessed=2**20, transcendentals=0),
        name="finish",
    )(parts)


def out_wgrad_kernel(core_ref, attn_ref, branch_ref, keep_ref, give_ref):
    wgrad = rows_inner(attn_ref[...], branch_ref[...]).astype(BF)
    for group in range(2):

        @pl.when(core_ref[0] == group)
        def _():
            keep_ref[...] = wgrad[:, QC * group : QC * (group + 1)]
            give_ref[...] = wgrad[:, QC * (1 - group) : QC * (2 - group)]


def out_wgrad(core, attn, branch_grad):
    smem = pl.BlockSpec(memory_space=pltpu.SMEM)
    vmem = pl.BlockSpec(memory_space=pltpu.VMEM)
    return pl.pallas_call(
        out_wgrad_kernel,
        in_specs=[smem, vmem, vmem],
        out_shape=[jax.ShapeDtypeStruct((QC, QC), BF)] * 2,
        compiler_params=pltpu.CompilerParams(vmem_limit_bytes=VMEM_BYTES),
        cost_estimate=pl.CostEstimate(flops=0, bytes_accessed=0, transcendentals=0),
        name="out_wgrad",
    )(core, attn, branch_grad)


def deal_kernel(parts_ref, gate_ref, up_ref, down_ref, rows_ref):
    for t in range(4):
        source_ref = parts_ref.at[t % 2 * 2 + t // 2]
        for which, ref in enumerate((gate_ref, up_ref)):
            for run in range(32):
                target, place, left = 152 * run + 38 * t, 40 * run, 38
                while left:
                    size = min(left, CH - place % CH)
                    source = place // CH * 2 * CH + which * CH + place % CH
                    part = source_ref[:, source : source + size]
                    ref[:, target : target + size] = part.astype(F32)
                    target, place, left = target + size, place + size, left - size
        for piece in range(70):
            row, lane = 4 * (piece // 10), 2 * FFP + 128 * (piece % 10)
            part = source_ref[row : row + 4, lane : lane + 128].astype(F32)
            row, lane = 4 * (piece // 7), 128 * (piece % 7)
            rows_ref[row : row + 4, lane : lane + 128] = part
        down_ref[38 * t : 38 * t + 38, :] = rows_ref[:38, :]


def deal(parts):
    return pl.pallas_call(
        deal_kernel,
        out_shape=[
            jax.ShapeDtypeStruct((28, FF), F32),
            jax.ShapeDtypeStruct((28, FF), F32),
            jax.ShapeDtypeStruct((152, D), F32),
        ],
        scratch_shapes=[pltpu.VMEM((40, D), F32)],
        compiler_params=pltpu.CompilerParams(vmem_limit_bytes=24 * 2**20),
        cost_estimate=pl.CostEstimate(flops=0, bytes_accessed=0, transcendentals=0),
        name="deal",
    )(parts)


def shards(
    tokens,
    attn_gain,
    qkv_weight,
    qk_bias,
    value_bias,
    out_weight,
    mlp_gain,
    gate_weight,
    up_weight,
    down_weight,
    cotangent,
):
    yl, c, z, x, yh = [lax.axis_index(name) for name in AXES]
    ctx = yl * 2 + c
    rows = 2 * BLK

    tok = tokens.reshape(rows, D)
    out_grad = cotangent.reshape(rows, D)
    chip = jnp.stack([yl])
    core = jnp.stack([c])

    def spare(vector):
        size = vector.shape[0]
        row = jnp.pad(vector, (0, PACK - size))
        return jnp.where(yh == 0, row, jnp.pad(vector, (size, PACK - 2 * size)))

    packed = jnp.concatenate(
        [
            lax.dynamic_slice_in_dim(qkv_weight, c * QC, QC, 1),
            lax.dynamic_slice_in_dim(qkv_weight, D + c * HD, HD, 1),
            lax.dynamic_slice_in_dim(qkv_weight, D + KVH * HD + c * HD, HD, 1),
            lax.dynamic_slice_in_dim(out_weight, c * QC, QC, 1),
        ],
        axis=1,
    )
    vec_rows = jnp.stack([spare(vector) for vector in (attn_gain, mlp_gain, qk_bias, value_bias)])
    packed = jnp.concatenate([packed, vec_rows], axis=0)
    packed, gate_weight, up_weight, down_weight = lax.optimization_barrier(
        (packed, gate_weight, up_weight, down_weight)
    )
    low, high = ordered(packed, swap(packed, "yh"), yh)
    packed = jnp.concatenate([low[:28], high[:28], low[28:] + high[28:]], axis=0)
    packed = jnp.broadcast_to(jnp.pad(packed, ((0, 4), (0, 0))), (16, 64, PACK))

    tok_two = lax.all_gather(tok, "c", axis=0, tiled=True)
    gu_part, down_part = quarter(jnp.stack([ctx]), gate_weight, up_weight, down_weight)
    gu_part = jnp.concatenate(ordered(gu_part, swap(gu_part, "yh"), yh), axis=0)
    down_part = jnp.concatenate(ordered(down_part, swap(down_part, "yh"), yh), axis=0)
    grads_far = swap(out_grad, "yl")
    mlp_part = jnp.concatenate([gu_part, tiles_down(down_part)], axis=1)
    places = jnp.stack([2 * yl, 7 - 2 * yl, 2 * yl + 1, 6 - 2 * yl])
    positions = places[:, None] * BLK + jnp.arange(BLK, dtype=jnp.int32)[None, :]
    freqs = THETA ** (-(jnp.arange(HD // 2, dtype=F32) * 2.0 / HD))
    turns = positions.astype(F32)[:, None, :] * freqs[None, :, None]
    cosine, sine = jnp.cos(turns), jnp.sin(turns)
    mlp_part, packed = lax.optimization_barrier((mlp_part, packed))
    packed = lax.all_to_all(packed, ("z", "x"), 0, 0, tiled=True)
    mlp_all = lax.all_gather(mlp_part, ("z", "x"), axis=0, tiled=True)

    normed_in, query, kv_own, gain_one, gain_two, qkv_half, out_cols = project(
        core, tok_two, packed, cosine, sine
    )
    kv_own, grads_far = lax.optimization_barrier((kv_own, grads_far))
    kv = lax.all_gather(kv_own, "yl", axis=0, tiled=True)

    attn, total = attend(chip, query, kv)
    out_give = lax.dynamic_index_in_dim(out_cols, 1 - c, 0, keepdims=False)
    out_keep = lax.dynamic_index_in_dim(out_cols, c, 0, keepdims=False)
    out_half = jnp.concatenate(ordered(out_keep, swap(out_give, "c"), c), axis=1)
    grads = [out_grad, grads_far, swap(out_grad, "c"), swap(grads_far, "c")]

    def own_rows(parts):
        return lax.dynamic_slice_in_dim(parts, c * rows, rows, 0)

    def chip_sum(parts):
        give = lax.dynamic_slice_in_dim(parts, (1 - c) * rows, rows, 0)
        return own_rows(parts).astype(F32) + swap(give, "c").astype(F32)

    attn_give = lax.dynamic_slice_in_dim(attn, (1 - c) * rows, rows, 0)
    branch_come = swap(dot(attn_give, out_half).astype(BF), "c")
    inputs = tok.astype(F32)
    hidden = inputs + dot(own_rows(attn), out_half) + branch_come.astype(F32)
    hidden, *grads = lax.optimization_barrier((hidden, *grads))

    inverse_two = lax.rsqrt(jnp.mean(hidden * hidden, axis=-1, keepdims=True) + EPSILON)
    normed_two = hidden * inverse_two
    normed_mid = (normed_two * gain_two).astype(BF)
    mid_far = swap(normed_mid, "yl")
    mids = [normed_mid, mid_far, swap(normed_mid, "c"), swap(mid_far, "c")]
    inner, gu_grad, down_t, gu_parts = mlp(mids, grads, mlp_all)
    gu_sum = lax.psum_scatter(gu_parts, "z", scatter_dimension=0, tiled=True)
    mid_keep, mid_give = mid(gu_grad, mlp_all)

    def group_sum(keep, come):
        far = keep[rows:].astype(F32) + come[rows:].astype(F32)
        away = swap(far.astype(BF), "yl")
        return keep[:rows].astype(F32) + come[:rows].astype(F32) + away.astype(F32)

    mid_come = swap(mid_give, "c")
    mid_grad = group_sum(mid_keep, mid_come)

    inner, mid_come = lax.optimization_barrier((inner, mid_come))
    down_parts = down_wgrad(inner, grads)
    mid_grad = after(mid_grad, down_parts)

    gain_two_grad = jnp.sum(mid_grad * normed_two, axis=0, keepdims=True)
    hidden_grad = out_grad.astype(F32) + norm_back(mid_grad * gain_two, normed_two, inverse_two)
    branch_grad = lax.all_gather(hidden_grad.astype(BF), "c", axis=0, tiled=True)
    down_pieces = lax.all_to_all(down_parts.reshape(4, 320, D), "x", 0, 0, tiled=True)
    query_grad, kv_keep, kv_give = attend_back(
        chip, query, kv, out_half, total, branch_grad, cosine, sine
    )
    kv_come = swap(kv_give, "yl")
    out_keep, out_give = out_wgrad(core, attn, after(branch_grad, kv_give))
    out_come = swap(out_give, "c")
    qkv_wgrad, in_parts = project_back(
        core,
        query_grad,
        kv_keep,
        kv_come,
        normed_in,
        tok_two,
        qkv_half,
        gain_two_grad,
        out_keep,
        out_come,
        cosine,
        sine,
    )

    gu_sum = after(gu_sum, kv_come).reshape(4, 56, 2 * FFP)
    gu_sum = lax.psum_scatter(gu_sum, "x", scatter_dimension=0, tiled=True)
    qkv_wparts = lax.all_to_all(qkv_wgrad, ("z", "x"), 0, 0, tiled=True)
    in_give = lax.dynamic_slice_in_dim(in_parts, (1 - c) * rows, rows, 0)
    in_come = swap(in_give, "c")
    down_pieces, in_come = lax.optimization_barrier((down_pieces, in_come))
    down_sum = sum4(down_pieces).reshape(4, 80, D)
    down_pieces = spread4(down_sum, "z", z)
    inner, down_sum = lax.optimization_barrier((inner, down_sum))
    out_keep, out_give = mlp_out(inner, down_t)
    out_come = swap(out_give, "c")
    out_far = far_rows(out_keep, out_come)
    input_grad = input_back(core, hidden_grad, in_parts, in_come, tok, gain_one)
    gu_sum, input_grad, out_far = lax.optimization_barrier((gu_sum, input_grad, out_far))
    keep, give = halves(jnp.stack([yh]), gu_sum.reshape(56, 2 * FFP), down_pieces)
    out_away = swap(out_far, "yl")
    qkv_wparts, give, out_away, input_grad = lax.optimization_barrier(
        (qkv_wparts, give, out_away, input_grad)
    )
    packed_sum = part_sum(qkv_wparts)
    packed_sum, give = lax.optimization_barrier((packed_sum, give))
    mixed = hidden + out_keep[:rows].astype(F32) + out_come[:rows].astype(F32)
    mixed = (mixed + out_away.astype(F32)).astype(BF)
    packed_sum = lax.all_to_all(packed_sum, ("yl", "c", "yh"), 0, 0, tiled=True)

    mlp_sum = (keep.astype(F32) + swap(give, "yh").astype(F32)).astype(BF)
    mlp_pair = jnp.stack(ordered(mlp_sum, swap(mlp_sum, "yl"), yl))
    mlp_pair = lax.all_gather(mlp_pair, "c", axis=0).reshape(4, 28, 3 * FFP)
    qkv_own, out_own, *vec_own = finish(packed_sum)
    mlp_pair, qkv_own, mixed = lax.optimization_barrier((mlp_pair, qkv_own, mixed))
    gate_own, up_own, down_own = deal(mlp_pair)

    return (
        mixed.reshape(tokens.shape),
        input_grad.reshape(tokens.shape),
        vec_own[0].reshape(28),
        qkv_own,
        vec_own[2].reshape(32),
        vec_own[3].reshape(4),
        out_own,
        vec_own[1].reshape(28),
        gate_own,
        up_own,
        down_own,
    )


def solution(mesh):
    devices = mesh.devices.reshape(2, 2, 4, 4, 2)
    split = Mesh(devices, AXES)
    ctx, fsdp = ("yl", "c"), ("z", "x", "yh")
    rows = P(fsdp, None, ctx, None, None)
    in_specs = (
        rows,
        P(fsdp),
        P(fsdp, None),
        P(fsdp),
        P(fsdp),
        P(fsdp, None),
        P(fsdp),
        P(fsdp, None),
        P(fsdp, None),
        P(fsdp, None),
        rows,
    )
    out_specs = (
        rows,
        rows,
        P(fsdp),
        P(fsdp, None),
        P(fsdp),
        P(fsdp),
        P(fsdp, None),
        P(fsdp),
        P(fsdp, None),
        P(fsdp, None),
        P(fsdp, None),
    )
    return jax.shard_map(
        shards, mesh=split, in_specs=in_specs, out_specs=out_specs, check_vma=False
    )
```

```python
import jax
import jax.numpy as jnp
from jax import lax
from jax.experimental import pallas as pl
from jax.experimental.pallas import tpu as pltpu
from jax.sharding import Mesh, PartitionSpec as P

KVH = 2
HD = 64
REP = 7
D = 896
FF = 4864
FFT = FF // 4
CH = 256
CHUNKS = 5
FFP = CH * CHUNKS
VMEM_BYTES = 60 * 2**20
QC = REP * HD
STACK = REP * 128
PC = QC + 2 * HD
PACK = PC + QC
BLK = 128
EPSILON = 1e-06
THETA = 1000000.0
AXES = ("yl", "c", "z", "x", "yh")
BF = jnp.bfloat16
F32 = jnp.float32


def shift(value, axis, size, step):
    return lax.ppermute(value, axis, [(i, (i + step) % size) for i in range(size)])


def swap(value, axis):
    return shift(value, axis, 2, 1)


def angles(positions):
    freqs = THETA ** (-(jnp.arange(HD // 2, dtype=F32) * 2.0 / HD))
    return positions.astype(F32)[:, None] * freqs[None, :]


def rows_inner(left, right):
    return lax.dot_general(left, right, (((0,), (0,)), ((), ())), preferred_element_type=F32)


def cols_inner(left, right):
    return lax.dot_general(left, right, (((1,), (1,)), ((), ())), preferred_element_type=F32)


def dot(left, right):
    return jnp.dot(left, right, preferred_element_type=F32)


def norm_back(grad_normed, normed, inverse):
    return inverse * (grad_normed - normed * jnp.mean(grad_normed * normed, axis=-1, keepdims=True))


def ordered(own, other, place):
    first = jnp.where(place == 0, own, other)
    second = jnp.where(place == 0, other, own)
    return first, second


def spread4(parts, axis, place):
    def part(step):
        return lax.dynamic_index_in_dim(parts, (place + step) % 4, 0, keepdims=False)

    return [
        part(0),
        shift(part(1), axis, 4, 1),
        shift(part(3), axis, 4, 3),
        shift(part(2), axis, 4, 2),
    ]


def total4(pieces):
    return sum(piece.astype(F32) for piece in pieces).astype(BF)


def scatter2(parts, axis, place):
    keep = lax.dynamic_index_in_dim(parts, place, 0, keepdims=False)
    give = lax.dynamic_index_in_dim(parts, 1 - place, 0, keepdims=False)
    return (keep.astype(F32) + swap(give, axis).astype(F32)).astype(BF)


def after(value, *others):
    return lax.optimization_barrier((value,) + others)[0]


def quarter_kernel(ctx_ref, gate_ref, up_ref, down_ref, gu_out_ref, down_out_ref):
    gu_out_ref[...] = jnp.zeros_like(gu_out_ref)
    down_out_ref[...] = jnp.zeros_like(down_out_ref)
    for t in range(4):

        @pl.when(ctx_ref[0] == t)
        def _():
            down_out_ref[:38, :] = down_ref[38 * t : 38 * t + 38, :]
            for which, ref in enumerate((gate_ref, up_ref)):
                for run in range(32):
                    source, place, left = 152 * run + 38 * t, 40 * run, 38
                    while left:
                        size = min(left, CH - place % CH)
                        target = place // CH * 2 * CH + which * CH + place % CH
                        gu_out_ref[:, target : target + size] = ref[:, source : source + size]
                        source, place, left = source + size, place + size, left - size


def quarter(ctx, gate, up, down):
    smem = pl.BlockSpec(memory_space=pltpu.SMEM)
    vmem = pl.BlockSpec(memory_space=pltpu.VMEM)
    return pl.pallas_call(
        quarter_kernel,
        in_specs=[smem, vmem, vmem, vmem],
        out_shape=[
            jax.ShapeDtypeStruct((gate.shape[0], 2 * FFP), BF),
            jax.ShapeDtypeStruct((40, D), BF),
        ],
        compiler_params=pltpu.CompilerParams(vmem_limit_bytes=16 * 2**20),
        cost_estimate=pl.CostEstimate(flops=0, bytes_accessed=0, transcendentals=0),
        name="quarter",
    )(ctx, gate, up, down)


def tiles_down(part):
    return part.reshape(10, 8, 7, 128).transpose(2, 1, 0, 3).reshape(56, FFP)


PARTS = 4


def mlp_kernel(*refs):
    rows_refs, grads_refs = refs[:PARTS], refs[PARTS : 2 * PARTS]
    gu_ref, tiles_ref, inner_ref, gu_grad_ref, down_ref, wgrad_ref, turned_rows = refs[2 * PARTS :]
    step = pl.program_id(0)
    size = rows_refs[0].shape[0]

    @pl.when(step == 0)
    def _():
        for p in range(PARTS):
            turned_rows[:, p * size : (p + 1) * size] = jnp.transpose(rows_refs[p][...])

        for s in range(16):
            for pair in range(5):
                for lane in range(7):
                    rows = slice(56 * s + 8 * lane, 56 * s + 8 * lane + 8)
                    first = tiles_ref[rows, 256 * pair : 256 * pair + 128]
                    second = tiles_ref[rows, 256 * pair + 128 : 256 * pair + 256]
                    target = slice(80 * s + 16 * pair, 80 * s + 16 * pair + 16)
                    down_ref[target, 128 * lane : 128 * lane + 128] = jnp.concatenate(
                        [first, second], axis=0
                    )

    gate_w, up_w = gu_ref[:, :CH], gu_ref[:, CH:]
    down_w = down_ref[pl.ds(pl.multiple_of(step * CH, CH), CH), :]
    for p in range(PARTS):
        span = slice(p * size, (p + 1) * size)
        gate = dot(rows_refs[p][...], gate_w)
        up = dot(rows_refs[p][...], up_w)
        inner_grad = cols_inner(grads_refs[p][...], down_w)
        sigma = 0.5 + 0.5 * jnp.tanh(0.5 * gate)
        silu = gate * sigma
        slope = sigma + silu - silu * sigma
        inner_ref[span, :] = (silu * up).astype(BF)
        gu_grad_ref[span, :CH] = (inner_grad * up * slope).astype(BF)
        gu_grad_ref[span, CH:] = (inner_grad * silu).astype(BF)
    wgrad = dot(turned_rows[...], gu_grad_ref[...])
    wgrad_ref[...] = wgrad.astype(BF).reshape(wgrad_ref.shape)


def mlp(rows, grads, weights):
    size = rows[0].shape[0]
    count = PARTS * size
    whole = pl.BlockSpec((size, D), lambda j: (0, 0))
    return pl.pallas_call(
        mlp_kernel,
        grid=(CHUNKS,),
        in_specs=[
            *[whole] * (2 * PARTS),
            pl.BlockSpec((D, 2 * CH), lambda j: (0, j)),
            pl.BlockSpec((D, FFP), lambda j: (0, 2)),
        ],
        out_specs=[
            pl.BlockSpec((count, CH), lambda j: (0, j)),
            pl.BlockSpec((count, 2 * CH), lambda j: (0, j)),
            pl.BlockSpec((FFP, D), lambda j: (0, 0)),
            pl.BlockSpec((4, D // 4, 2 * CH), lambda j: (0, 0, j)),
        ],
        out_shape=[
            jax.ShapeDtypeStruct((count, FFP), BF),
            jax.ShapeDtypeStruct((count, 2 * FFP), BF),
            jax.ShapeDtypeStruct((FFP, D), BF),
            jax.ShapeDtypeStruct((4, D // 4, 2 * FFP), BF),
        ],
        scratch_shapes=[pltpu.VMEM((D, count), BF)],
        compiler_params=pltpu.CompilerParams(vmem_limit_bytes=VMEM_BYTES),
        cost_estimate=pl.CostEstimate(
            flops=10 * count * D * FFP, bytes_accessed=24 * 2**20, transcendentals=count * FFP
        ),
        name="mlp",
    )(*rows, *grads, weights, weights)


def mid_kernel(gu_grad_ref, gu_ref, keep_ref, give_ref):
    part = cols_inner(gu_grad_ref[...], gu_ref[...]).astype(BF)
    step = pl.program_id(0)

    @pl.when(step < PARTS // 2)
    def _():
        keep_ref[...] = part

    @pl.when(step >= PARTS // 2)
    def _():
        give_ref[...] = part


def mid(gu_grad, weights):
    count = gu_grad.shape[0]
    return pl.pallas_call(
        mid_kernel,
        grid=(PARTS,),
        in_specs=[
            pl.BlockSpec((count // PARTS, 2 * FFP), lambda j: (j, 0)),
            pl.BlockSpec((D, 2 * FFP), lambda j: (0, 0)),
        ],
        out_specs=[
            pl.BlockSpec((count // PARTS, D), lambda j: (jnp.minimum(j, PARTS // 2 - 1), 0)),
            pl.BlockSpec((count // PARTS, D), lambda j: (jnp.maximum(j - PARTS // 2, 0), 0)),
        ],
        out_shape=[jax.ShapeDtypeStruct((count // 2, D), BF)] * 2,
        compiler_params=pltpu.CompilerParams(vmem_limit_bytes=60 * 2**20),
        cost_estimate=pl.CostEstimate(
            flops=4 * count * D * FFP, bytes_accessed=12 * 2**20, transcendentals=0
        ),
        name="mid",
    )(gu_grad, weights)


def mlp_out_kernel(inner_ref, down_ref, keep_ref, give_ref):
    half = keep_ref.shape[0]
    keep_ref[...] = dot(inner_ref[:half, :], down_ref[...]).astype(BF)
    give_ref[...] = dot(inner_ref[half:, :], down_ref[...]).astype(BF)


def mlp_out(inner, down):
    count = inner.shape[0]
    return pl.pallas_call(
        mlp_out_kernel,
        out_shape=[jax.ShapeDtypeStruct((count // 2, D), BF)] * 2,
        compiler_params=pltpu.CompilerParams(vmem_limit_bytes=24 * 2**20),
        cost_estimate=pl.CostEstimate(flops=0, bytes_accessed=0, transcendentals=0),
        name="mlp_out",
    )(inner, down)


def down_wgrad_kernel(inner_ref, *refs):
    grads = jnp.concatenate([ref[...] for ref in refs[:PARTS]], axis=0)
    part = rows_inner(inner_ref[...], grads).astype(BF)
    for j in range(CHUNKS):

        @pl.when(pl.program_id(0) == j)
        def _():
            place = CH * j
            while place < CH * (j + 1):
                run, start = place // 80, place % 80
                size = min(80 - start, CH * (j + 1) - place)
                rows = part[place - CH * j : place - CH * j + size]
                refs[PARTS][run % 4, run // 4, start : start + size, :] = rows
                place += size


def down_wgrad(inner, grads):
    count = inner.shape[0]
    return pl.pallas_call(
        down_wgrad_kernel,
        grid=(CHUNKS,),
        in_specs=[
            pl.BlockSpec((count, CH), lambda j: (0, j)),
            *[pl.BlockSpec((count // PARTS, D), lambda j: (0, 0))] * PARTS,
        ],
        out_specs=pl.BlockSpec((4, 4, 80, D), lambda j: (0, 0, 0, 0)),
        out_shape=jax.ShapeDtypeStruct((4, 4, 80, D), BF),
        compiler_params=pltpu.CompilerParams(vmem_limit_bytes=24 * 2**20),
        cost_estimate=pl.CostEstimate(flops=0, bytes_accessed=0, transcendentals=0),
        name="down_wgrad",
    )(inner, *grads)


ORDER = (0, 7, 1, 6, 2, 5, 3, 4)
LENGTHS = {1: (0, 0), 8: (1, 0), 2: (2, 0), 7: (3, 0), 3: (0, 1), 6: (1, 1), 4: (2, 1), 5: (3, 1)}


def turned(value, cosine, sine):
    first, second = value[: HD // 2], value[HD // 2 :]
    return jnp.concatenate(
        [first * cosine - second * sine, second * cosine + first * sine], axis=0
    )


def project_kernel(
    core_ref,
    tok_ref,
    packed_ref,
    cos_ref,
    sin_ref,
    rows_ref,
    query_ref,
    kv_ref,
    gain,
    gain_two_ref,
    weight,
    out_ref,
    bias,
):
    for s in range(16):
        span = slice(56 * s, 56 * s + 56)
        weight[span, :] = packed_ref[s, :56, :PC]
        out_ref[s // 8, 56 * (s % 8) : 56 * (s % 8) + 56, :] = packed_ref[s, :56, PC:]
        gain[:, span] = packed_ref[s, 56:57, :56].astype(F32)
        gain_two_ref[:, span] = packed_ref[s, 57:58, :56].astype(F32)
    for group in range(2):

        @pl.when(core_ref[0] == group)
        def _():
            for head in range(REP):
                part = packed_ref[REP * group + head, 58:59, :HD]
                bias[:, HD * head : HD * (head + 1)] = part.astype(F32)
            bias[:, QC : QC + HD] = packed_ref[14 + group, 58:59, :HD].astype(F32)
            for run in range(8):
                part = packed_ref[8 * group + run, 59:60, :8]
                bias[:, QC + HD + 8 * run : QC + HD + 8 * run + 8] = part.astype(F32)

    inputs = tok_ref[...].astype(F32)
    inverse = lax.rsqrt(jnp.mean(inputs * inputs, axis=-1, keepdims=True) + EPSILON)
    rows = (inputs * inverse * gain[...]).astype(BF)
    rows_ref[...] = rows
    projected = dot(rows, weight[...]) + bias[...]
    for b in range(4):
        cosine, sine = cos_ref[b], sin_ref[b]
        block = projected[b * BLK : (b + 1) * BLK]
        for pair in range(4):
            both = jnp.transpose(block[:, 2 * HD * pair : 2 * HD * (pair + 1)])
            head = turned(both[:HD], cosine, sine).astype(BF)
            query_ref[b, :, 2 * pair * BLK : (2 * pair + 1) * BLK] = head
            other = turned(both[HD:], cosine, sine)
            if pair < 3:
                query_ref[b, :, (2 * pair + 1) * BLK : (2 * pair + 2) * BLK] = other.astype(BF)
            else:
                value = block[:, QC + HD :]
                kv_ref[b * BLK : (b + 1) * BLK, :] = jnp.concatenate(
                    [jnp.transpose(other), value], axis=1
                ).astype(BF)


def project(core, tok, packed, cosine, sine):
    smem = pl.BlockSpec(memory_space=pltpu.SMEM)
    vmem = pl.BlockSpec(memory_space=pltpu.VMEM)
    return pl.pallas_call(
        project_kernel,
        in_specs=[smem] + [vmem] * 4,
        out_shape=[
            jax.ShapeDtypeStruct((4 * BLK, D), BF),
            jax.ShapeDtypeStruct((4, HD, STACK), BF),
            jax.ShapeDtypeStruct((4 * BLK, 2 * HD), BF),
            jax.ShapeDtypeStruct((1, D), F32),
            jax.ShapeDtypeStruct((1, D), F32),
            jax.ShapeDtypeStruct((D, PC), BF),
            jax.ShapeDtypeStruct((2, QC, QC), BF),
        ],
        scratch_shapes=[pltpu.VMEM((1, PC), F32)],
        compiler_params=pltpu.CompilerParams(vmem_limit_bytes=32 * 2**20),
        cost_estimate=pl.CostEstimate(
            flops=2 * 4 * BLK * D * PC, bytes_accessed=6 * 2**20, transcendentals=0
        ),
        name="project",
    )(core, tok, packed, cosine, sine)


def split_kv(kv_ref, keys, values):
    for place, block in enumerate(ORDER):
        rows = kv_ref[place * BLK : (place + 1) * BLK, :]
        keys[block * BLK : (block + 1) * BLK, :] = rows[:, :HD]
        values[block * BLK : (block + 1) * BLK, :] = rows[:, HD:]


def masked_scores(keys, query, length):
    scores = dot(keys[: length * BLK, :], query) * HD ** (-0.5)
    key = lax.broadcasted_iota(jnp.int32, (BLK, STACK), 0)
    token = lax.rem(lax.broadcasted_iota(jnp.int32, (BLK, STACK), 1), BLK)
    last = jnp.where(key <= token, scores[(length - 1) * BLK :], -1e30)
    if length == 1:
        return last
    return jnp.concatenate([scores[: (length - 1) * BLK], last], axis=0)


def heads_out(stacked, ref, block):
    rows = slice(block * BLK, (block + 1) * BLK)
    for pair in range(3):
        first = stacked[:, 2 * pair * BLK : (2 * pair + 1) * BLK]
        second = stacked[:, (2 * pair + 1) * BLK : (2 * pair + 2) * BLK]
        both = jnp.transpose(jnp.concatenate([first, second], axis=0))
        ref[rows, 2 * HD * pair : 2 * HD * (pair + 1)] = both.astype(ref.dtype)
    ref[rows, 6 * HD :] = jnp.transpose(stacked[:, 6 * BLK :]).astype(ref.dtype)


def attend_kernel(chip_ref, query_ref, kv_ref, attn_ref, total_ref, keys, values):
    split_kv(kv_ref, keys, values)
    for length, (block, chip) in LENGTHS.items():

        @pl.when(chip_ref[0] == chip)
        def _():
            scores = masked_scores(keys, query_ref[block], length)
            top = jnp.max(scores, axis=0, keepdims=True)
            prob = jnp.exp(scores - top)
            total = jnp.sum(prob, axis=0, keepdims=True)
            total_ref[block] = top + jnp.log(total)
            attn = rows_inner(values[: length * BLK, :], prob.astype(BF)) / total
            heads_out(attn, attn_ref, block)


def attend(chip, query, kv):
    smem = pl.BlockSpec(memory_space=pltpu.SMEM)
    vmem = pl.BlockSpec(memory_space=pltpu.VMEM)
    return pl.pallas_call(
        attend_kernel,
        in_specs=[smem, vmem, vmem],
        out_shape=[
            jax.ShapeDtypeStruct((4 * BLK, QC), BF),
            jax.ShapeDtypeStruct((4, 1, STACK), F32),
        ],
        scratch_shapes=[pltpu.VMEM((8 * BLK, HD), BF), pltpu.VMEM((8 * BLK, HD), BF)],
        compiler_params=pltpu.CompilerParams(vmem_limit_bytes=32 * 2**20),
        cost_estimate=pl.CostEstimate(
            flops=2 * 18 * BLK * STACK * HD * 8, bytes_accessed=4 * 2**20, transcendentals=2**21
        ),
        name="attend",
    )(chip, query, kv)


def attend_back_kernel(
    chip_ref,
    query_ref,
    kv_ref,
    out_ref,
    total_ref,
    branch_ref,
    cos_ref,
    sin_ref,
    grad_ref,
    keep_ref,
    give_ref,
    keys,
    values,
    key_sum,
    value_sum,
    heads,
):
    split_kv(kv_ref, keys, values)
    key_sum[...] = jnp.zeros_like(key_sum)
    value_sum[...] = jnp.zeros_like(value_sum)
    attn_grad = cols_inner(branch_ref[...], out_ref[...])
    for b in range(4):
        part = attn_grad[b * BLK : (b + 1) * BLK]
        for pair in range(4):
            both = jnp.transpose(part[:, 2 * HD * pair : min(2 * HD * (pair + 1), QC)]).astype(BF)
            heads[b, :, 2 * pair * BLK : (2 * pair + 1) * BLK] = both[:HD]
            if pair < 3:
                heads[b, :, (2 * pair + 1) * BLK : (2 * pair + 2) * BLK] = both[HD:]
    for length, (block, chip) in LENGTHS.items():

        @pl.when(chip_ref[0] == chip)
        def _():
            span = length * BLK
            query = query_ref[block]
            grads = heads[block]
            prob = jnp.exp(masked_scores(keys, query, length) - total_ref[block])
            prob_grad = dot(values[:span, :], grads)
            weighted = jnp.sum(prob * prob_grad, axis=0, keepdims=True)
            score_grad = (prob * (prob_grad - weighted)).astype(BF)
            value_sum[:span, :] += cols_inner(prob.astype(BF), grads)
            key_sum[:span, :] += cols_inner(score_grad, query)
            query_grad = rows_inner(keys[:span, :], score_grad) * HD ** (-0.5)
            cosine = jnp.concatenate([cos_ref[block]] * REP, axis=1)
            sine = jnp.concatenate([sin_ref[block]] * REP, axis=1)
            heads_out(turned(query_grad, cosine, -sine), grad_ref, block)

    for place, block in enumerate(ORDER):
        span = slice(block * BLK, (block + 1) * BLK)
        both = jnp.concatenate([key_sum[span, :] * HD ** (-0.5), value_sum[span, :]], axis=1)
        rows = slice(place % 4 * BLK, (place % 4 + 1) * BLK)

        @pl.when(chip_ref[0] == place // 4)
        def _():
            keep_ref[rows, :] = both

        @pl.when(chip_ref[0] != place // 4)
        def _():
            give_ref[rows, :] = both.astype(BF)


def attend_back(chip, query, kv, out_half, total, branch_grad, cosine, sine):
    smem = pl.BlockSpec(memory_space=pltpu.SMEM)
    vmem = pl.BlockSpec(memory_space=pltpu.VMEM)
    return pl.pallas_call(
        attend_back_kernel,
        in_specs=[smem] + [vmem] * 7,
        out_shape=[
            jax.ShapeDtypeStruct((4 * BLK, QC), BF),
            jax.ShapeDtypeStruct((4 * BLK, 2 * HD), F32),
            jax.ShapeDtypeStruct((4 * BLK, 2 * HD), BF),
        ],
        scratch_shapes=[
            pltpu.VMEM((8 * BLK, HD), BF),
            pltpu.VMEM((8 * BLK, HD), BF),
            pltpu.VMEM((8 * BLK, HD), F32),
            pltpu.VMEM((8 * BLK, HD), F32),
            pltpu.VMEM((4, HD, STACK), BF),
        ],
        compiler_params=pltpu.CompilerParams(vmem_limit_bytes=40 * 2**20),
        cost_estimate=pl.CostEstimate(
            flops=2 * 18 * BLK * STACK * HD * 20, bytes_accessed=6 * 2**20, transcendentals=2**21
        ),
        name="attend_back",
    )(chip, query, kv, out_half, total, branch_grad, cosine, sine)


def project_back_kernel(
    core_ref,
    grad_ref,
    keep_ref,
    come_ref,
    rows_ref,
    tok_ref,
    weight_ref,
    gain_two_ref,
    out_keep_ref,
    out_come_ref,
    cos_ref,
    sin_ref,
    wgrad_ref,
    in_ref,
):
    kv_grad = keep_ref[...] + come_ref[...].astype(F32)
    keys = []
    for b in range(4):
        key = jnp.transpose(kv_grad[b * BLK : (b + 1) * BLK, :HD])
        keys.append(jnp.transpose(turned(key, cos_ref[b], -sin_ref[b])))
    key_back = jnp.concatenate(keys, axis=0)
    grads = jnp.concatenate(
        [grad_ref[...], key_back.astype(BF), kv_grad[:, HD:].astype(BF)], axis=1
    )
    wgrad = rows_inner(rows_ref[...], grads).astype(BF)
    in_part = cols_inner(grads, weight_ref[...])
    in_ref[...] = in_part.astype(BF)
    inputs = tok_ref[...].astype(F32)
    inverse = lax.rsqrt(jnp.mean(inputs * inputs, axis=-1, keepdims=True) + EPSILON)
    gain_one = jnp.sum(in_part * inputs * inverse, axis=0, keepdims=True)
    gain_two = gain_two_ref[...]
    bias = jnp.sum(grads.astype(F32), axis=0, keepdims=True)
    core = core_ref[0]
    wgrad_ref[:, 56:, :] = jnp.zeros((16, 8, PACK), BF)
    for group in range(2):

        @pl.when(core == group)
        def _():
            for s in range(8):
                span = slice(56 * s, 56 * s + 56)
                wgrad_ref[8 * group + s, :56, PC:] = out_keep_ref[span, :]
                wgrad_ref[8 * (1 - group) + s, :56, PC:] = out_come_ref[span, :]

    for s in range(16):
        wgrad_ref[s, :56, :PC] = wgrad[56 * s : 56 * s + 56]
        group, start = (s // 7, HD * (s % 7)) if s < 14 else (s - 14, QC)
        qk = jnp.where(core == group, bias[:, start : start + HD], 0.0)
        start = QC + HD + 8 * (s % 8)
        value = jnp.where(core == s // 8, bias[:, start : start + 8], 0.0)
        wgrad_ref[s, 56:57, :56] = gain_one[:, 56 * s : 56 * s + 56].astype(BF)
        wgrad_ref[s, 57:58, :56] = gain_two[:, 56 * s : 56 * s + 56].astype(BF)
        wgrad_ref[s, 58:59, :HD] = qk.astype(BF)
        wgrad_ref[s, 59:60, :8] = value.astype(BF)


def project_back(
    core, grad, keep, come, rows, tok, weight, gain_two, out_keep, out_come, cosine, sine
):
    smem = pl.BlockSpec(memory_space=pltpu.SMEM)
    vmem = pl.BlockSpec(memory_space=pltpu.VMEM)
    return pl.pallas_call(
        project_back_kernel,
        in_specs=[smem] + [vmem] * 11,
        out_shape=[
            jax.ShapeDtypeStruct((16, 64, PACK), BF),
            jax.ShapeDtypeStruct((4 * BLK, D), BF),
        ],
        compiler_params=pltpu.CompilerParams(vmem_limit_bytes=60 * 2**20),
        cost_estimate=pl.CostEstimate(
            flops=4 * 4 * BLK * D * PC, bytes_accessed=10 * 2**20, transcendentals=0
        ),
        name="project_back",
    )(core, grad, keep, come, rows, tok, weight, gain_two, out_keep, out_come, cosine, sine)


def sum4_kernel(parts_ref, out_ref):
    total = parts_ref[0].astype(F32)
    for s in range(1, 4):
        total += parts_ref[s].astype(F32)
    out_ref[...] = total.astype(BF)


def sum4(parts):
    _, count, width = parts.shape
    return pl.pallas_call(
        sum4_kernel,
        out_shape=jax.ShapeDtypeStruct((count, width), BF),
        compiler_params=pltpu.CompilerParams(vmem_limit_bytes=24 * 2**20),
        cost_estimate=pl.CostEstimate(flops=0, bytes_accessed=0, transcendentals=0),
        name="sum4",
    )(parts)


def small(kernel, shapes, *operands, name):
    vmem = pl.BlockSpec(memory_space=pltpu.VMEM)
    smem = pl.BlockSpec(memory_space=pltpu.SMEM)
    return pl.pallas_call(
        kernel,
        in_specs=[smem if value.dtype == jnp.int32 else vmem for value in operands],
        out_shape=shapes,
        compiler_params=pltpu.CompilerParams(vmem_limit_bytes=16 * 2**20),
        cost_estimate=pl.CostEstimate(flops=0, bytes_accessed=0, transcendentals=0),
        name=name,
    )(*operands)


def far_kernel(keep_ref, come_ref, out_ref):
    half = out_ref.shape[0]
    total = keep_ref[half:, :].astype(F32) + come_ref[half:, :].astype(F32)
    out_ref[...] = total.astype(BF)


def far_rows(keep, come):
    shape = jax.ShapeDtypeStruct((keep.shape[0] // 2, keep.shape[1]), BF)
    return small(far_kernel, shape, keep, come, name="far_rows")


def halves_kernel(place_ref, gu_ref, *refs):
    keep_ref, give_ref, total_ref = refs[4:]
    total_ref[...] = sum(ref[...].astype(F32) for ref in refs[:4])
    for place in range(2):

        @pl.when(place_ref[0] == place)
        def _():
            for ref, half in ((keep_ref, place), (give_ref, 1 - place)):
                ref[:, : 2 * FFP] = gu_ref[28 * half : 28 * half + 28, :]
                for piece in range(70):
                    row, lane = 40 * half + 4 * (piece // 7), 128 * (piece % 7)
                    part = total_ref[row : row + 4, lane : lane + 128].astype(BF)
                    row, lane = 4 * (piece // 10), 2 * FFP + 128 * (piece % 10)
                    ref[row : row + 4, lane : lane + 128] = part


def halves(place, gu, down_pieces):
    shape = jax.ShapeDtypeStruct((28, 3 * FFP), BF)
    vmem = pl.BlockSpec(memory_space=pltpu.VMEM)
    return pl.pallas_call(
        halves_kernel,
        in_specs=[pl.BlockSpec(memory_space=pltpu.SMEM)] + [vmem] * 5,
        out_shape=[shape, shape],
        scratch_shapes=[pltpu.VMEM((80, D), F32)],
        compiler_params=pltpu.CompilerParams(vmem_limit_bytes=24 * 2**20),
        cost_estimate=pl.CostEstimate(flops=0, bytes_accessed=0, transcendentals=0),
        name="halves",
    )(place, gu, *down_pieces)


def input_kernel(core_ref, grad_ref, parts_ref, come_ref, tok_ref, gain_ref, out_ref):
    size = come_ref.shape[0]
    for core in range(2):

        @pl.when(core_ref[0] == core)
        def _():
            part = parts_ref[core * size : (core + 1) * size, :].astype(F32)
            scaled = (part + come_ref[...].astype(F32)) * gain_ref[...]
            inputs = tok_ref[...].astype(F32)
            inverse = lax.rsqrt(jnp.mean(inputs * inputs, axis=-1, keepdims=True) + EPSILON)
            out_ref[...] = grad_ref[...] + norm_back(scaled, inputs * inverse, inverse)


def input_back(core, grad, parts, come, tok, gain):
    shape = jax.ShapeDtypeStruct(grad.shape, F32)
    return small(input_kernel, shape, core, grad, parts, come, tok, gain, name="input_back")


def part_sum_kernel(parts_ref, out_ref):
    total = parts_ref[0].astype(F32)
    for s in range(1, 16):
        total += parts_ref[s].astype(F32)
    total = total.astype(BF)
    for place in range(8):
        half = place % 2
        out_ref[place, :28, :] = total[28 * half : 28 * half + 28]
        out_ref[place, 28:, :] = jnp.zeros((4, PACK), BF)
        for row, size in enumerate((28, 28, 32, 4)):
            part = total[56 + row : 57 + row, size * half : size * (half + 1)]
            out_ref[place, 28 + row : 29 + row, :size] = part


def part_sum(parts):
    return pl.pallas_call(
        part_sum_kernel,
        out_shape=jax.ShapeDtypeStruct((8, 32, PACK), BF),
        compiler_params=pltpu.CompilerParams(vmem_limit_bytes=24 * 2**20),
        cost_estimate=pl.CostEstimate(flops=0, bytes_accessed=3 * 2**20, transcendentals=0),
        name="part_sum",
    )(parts)


def finish_kernel(parts_ref, qkv_ref, out_ref, *vec_refs):
    vectors = 0.0
    for group in range(2):
        total = 0.0
        for place in (0, 1, 4, 5):
            total += parts_ref[2 * group + place].astype(F32)
        rows = total[:28]
        vectors += total[28:, :128]
        qkv_ref[:, QC * group : QC * (group + 1)] = rows[:, :QC]
        qkv_ref[:, D + HD * group : D + HD * (group + 1)] = rows[:, QC : QC + HD]
        start = D + HD * (KVH + group)
        qkv_ref[:, start : start + HD] = rows[:, QC + HD : PC]
        out_ref[:, QC * group : QC * (group + 1)] = rows[:, PC:]
    for row, ref in enumerate(vec_refs):
        ref[...] = vectors[row : row + 1, : ref.shape[1]]


def finish(parts):
    return pl.pallas_call(
        finish_kernel,
        out_shape=[
            jax.ShapeDtypeStruct((28, D + 2 * KVH * HD), F32),
            jax.ShapeDtypeStruct((28, D), F32),
            *[jax.ShapeDtypeStruct((1, size), F32) for size in (28, 28, 32, 4)],
        ],
        compiler_params=pltpu.CompilerParams(vmem_limit_bytes=24 * 2**20),
        cost_estimate=pl.CostEstimate(flops=0, bytes_accessed=2**20, transcendentals=0),
        name="finish",
    )(parts)


def out_wgrad_kernel(core_ref, attn_ref, branch_ref, keep_ref, give_ref):
    wgrad = rows_inner(attn_ref[...], branch_ref[...]).astype(BF)
    for group in range(2):

        @pl.when(core_ref[0] == group)
        def _():
            keep_ref[...] = wgrad[:, QC * group : QC * (group + 1)]
            give_ref[...] = wgrad[:, QC * (1 - group) : QC * (2 - group)]


def out_wgrad(core, attn, branch_grad):
    smem = pl.BlockSpec(memory_space=pltpu.SMEM)
    vmem = pl.BlockSpec(memory_space=pltpu.VMEM)
    return pl.pallas_call(
        out_wgrad_kernel,
        in_specs=[smem, vmem, vmem],
        out_shape=[jax.ShapeDtypeStruct((QC, QC), BF)] * 2,
        compiler_params=pltpu.CompilerParams(vmem_limit_bytes=VMEM_BYTES),
        cost_estimate=pl.CostEstimate(flops=0, bytes_accessed=0, transcendentals=0),
        name="out_wgrad",
    )(core, attn, branch_grad)


def deal_kernel(parts_ref, gate_ref, up_ref, down_ref, rows_ref):
    for t in range(4):
        source_ref = parts_ref.at[t % 2 * 2 + t // 2]
        for which, ref in enumerate((gate_ref, up_ref)):
            for run in range(32):
                target, place, left = 152 * run + 38 * t, 40 * run, 38
                while left:
                    size = min(left, CH - place % CH)
                    source = place // CH * 2 * CH + which * CH + place % CH
                    part = source_ref[:, source : source + size]
                    ref[:, target : target + size] = part.astype(F32)
                    target, place, left = target + size, place + size, left - size
        for piece in range(70):
            row, lane = 4 * (piece // 10), 2 * FFP + 128 * (piece % 10)
            part = source_ref[row : row + 4, lane : lane + 128].astype(F32)
            row, lane = 4 * (piece // 7), 128 * (piece % 7)
            rows_ref[row : row + 4, lane : lane + 128] = part
        down_ref[38 * t : 38 * t + 38, :] = rows_ref[:38, :]


def deal(parts):
    return pl.pallas_call(
        deal_kernel,
        out_shape=[
            jax.ShapeDtypeStruct((28, FF), F32),
            jax.ShapeDtypeStruct((28, FF), F32),
            jax.ShapeDtypeStruct((152, D), F32),
        ],
        scratch_shapes=[pltpu.VMEM((40, D), F32)],
        compiler_params=pltpu.CompilerParams(vmem_limit_bytes=24 * 2**20),
        cost_estimate=pl.CostEstimate(flops=0, bytes_accessed=0, transcendentals=0),
        name="deal",
    )(parts)


def shards(
    tokens,
    attn_gain,
    qkv_weight,
    qk_bias,
    value_bias,
    out_weight,
    mlp_gain,
    gate_weight,
    up_weight,
    down_weight,
    cotangent,
):
    yl, c, z, x, yh = [lax.axis_index(name) for name in AXES]
    ctx = yl * 2 + c
    rows = 2 * BLK

    tok = tokens.reshape(rows, D)
    out_grad = cotangent.reshape(rows, D)
    chip = jnp.stack([yl])
    core = jnp.stack([c])

    def spare(vector):
        size = vector.shape[0]
        row = jnp.pad(vector, (0, PACK - size))
        return jnp.where(yh == 0, row, jnp.pad(vector, (size, PACK - 2 * size)))

    packed = jnp.concatenate(
        [
            lax.dynamic_slice_in_dim(qkv_weight, c * QC, QC, 1),
            lax.dynamic_slice_in_dim(qkv_weight, D + c * HD, HD, 1),
            lax.dynamic_slice_in_dim(qkv_weight, D + KVH * HD + c * HD, HD, 1),
            lax.dynamic_slice_in_dim(out_weight, c * QC, QC, 1),
        ],
        axis=1,
    )
    vec_rows = jnp.stack([spare(vector) for vector in (attn_gain, mlp_gain, qk_bias, value_bias)])
    packed = jnp.concatenate([packed, vec_rows], axis=0)
    packed, gate_weight, up_weight, down_weight = lax.optimization_barrier(
        (packed, gate_weight, up_weight, down_weight)
    )
    low, high = ordered(packed, swap(packed, "yh"), yh)
    packed = jnp.concatenate([low[:28], high[:28], low[28:] + high[28:]], axis=0)
    packed = jnp.broadcast_to(jnp.pad(packed, ((0, 4), (0, 0))), (16, 64, PACK))

    tok_two = lax.all_gather(tok, "c", axis=0, tiled=True)
    gu_part, down_part = quarter(jnp.stack([ctx]), gate_weight, up_weight, down_weight)
    gu_part = jnp.concatenate(ordered(gu_part, swap(gu_part, "yh"), yh), axis=0)
    down_part = jnp.concatenate(ordered(down_part, swap(down_part, "yh"), yh), axis=0)
    grads_far = swap(out_grad, "yl")
    mlp_part = jnp.concatenate([gu_part, tiles_down(down_part)], axis=1)
    places = jnp.stack([2 * yl, 7 - 2 * yl, 2 * yl + 1, 6 - 2 * yl])
    positions = places[:, None] * BLK + jnp.arange(BLK, dtype=jnp.int32)[None, :]
    freqs = THETA ** (-(jnp.arange(HD // 2, dtype=F32) * 2.0 / HD))
    turns = positions.astype(F32)[:, None, :] * freqs[None, :, None]
    cosine, sine = jnp.cos(turns), jnp.sin(turns)
    mlp_part, packed = lax.optimization_barrier((mlp_part, packed))
    packed = lax.all_to_all(packed, ("z", "x"), 0, 0, tiled=True)
    mlp_all = lax.all_gather(mlp_part, ("z", "x"), axis=0, tiled=True)

    normed_in, query, kv_own, gain_one, gain_two, qkv_half, out_cols = project(
        core, tok_two, packed, cosine, sine
    )
    kv_own, grads_far = lax.optimization_barrier((kv_own, grads_far))
    kv = lax.all_gather(kv_own, "yl", axis=0, tiled=True)

    attn, total = attend(chip, query, kv)
    out_give = lax.dynamic_index_in_dim(out_cols, 1 - c, 0, keepdims=False)
    out_keep = lax.dynamic_index_in_dim(out_cols, c, 0, keepdims=False)
    out_half = jnp.concatenate(ordered(out_keep, swap(out_give, "c"), c), axis=1)
    grads = [out_grad, grads_far, swap(out_grad, "c"), swap(grads_far, "c")]

    def own_rows(parts):
        return lax.dynamic_slice_in_dim(parts, c * rows, rows, 0)

    def chip_sum(parts):
        give = lax.dynamic_slice_in_dim(parts, (1 - c) * rows, rows, 0)
        return own_rows(parts).astype(F32) + swap(give, "c").astype(F32)

    attn_give = lax.dynamic_slice_in_dim(attn, (1 - c) * rows, rows, 0)
    branch_come = swap(dot(attn_give, out_half).astype(BF), "c")
    inputs = tok.astype(F32)
    hidden = inputs + dot(own_rows(attn), out_half) + branch_come.astype(F32)
    hidden, *grads = lax.optimization_barrier((hidden, *grads))

    inverse_two = lax.rsqrt(jnp.mean(hidden * hidden, axis=-1, keepdims=True) + EPSILON)
    normed_two = hidden * inverse_two
    normed_mid = (normed_two * gain_two).astype(BF)
    mid_far = swap(normed_mid, "yl")
    mids = [normed_mid, mid_far, swap(normed_mid, "c"), swap(mid_far, "c")]
    inner, gu_grad, down_t, gu_parts = mlp(mids, grads, mlp_all)
    gu_sum = lax.psum_scatter(gu_parts, "z", scatter_dimension=0, tiled=True)
    mid_keep, mid_give = mid(gu_grad, mlp_all)

    def group_sum(keep, come):
        far = keep[rows:].astype(F32) + come[rows:].astype(F32)
        away = swap(far.astype(BF), "yl")
        return keep[:rows].astype(F32) + come[:rows].astype(F32) + away.astype(F32)

    mid_come = swap(mid_give, "c")
    mid_grad = group_sum(mid_keep, mid_come)

    inner, mid_come = lax.optimization_barrier((inner, mid_come))
    down_parts = down_wgrad(inner, grads)
    mid_grad = after(mid_grad, down_parts)

    gain_two_grad = jnp.sum(mid_grad * normed_two, axis=0, keepdims=True)
    hidden_grad = out_grad.astype(F32) + norm_back(mid_grad * gain_two, normed_two, inverse_two)
    branch_grad = lax.all_gather(hidden_grad.astype(BF), "c", axis=0, tiled=True)
    down_pieces = lax.all_to_all(down_parts.reshape(4, 320, D), "x", 0, 0, tiled=True)
    query_grad, kv_keep, kv_give = attend_back(
        chip, query, kv, out_half, total, branch_grad, cosine, sine
    )
    kv_come = swap(kv_give, "yl")
    out_keep, out_give = out_wgrad(core, attn, after(branch_grad, kv_give))
    out_come = swap(out_give, "c")
    qkv_wgrad, in_parts = project_back(
        core,
        query_grad,
        kv_keep,
        kv_come,
        normed_in,
        tok_two,
        qkv_half,
        gain_two_grad,
        out_keep,
        out_come,
        cosine,
        sine,
    )

    gu_sum = after(gu_sum, kv_come).reshape(4, 56, 2 * FFP)
    gu_sum = lax.psum_scatter(gu_sum, "x", scatter_dimension=0, tiled=True)
    qkv_wparts = lax.all_to_all(qkv_wgrad, ("z", "x"), 0, 0, tiled=True)
    in_give = lax.dynamic_slice_in_dim(in_parts, (1 - c) * rows, rows, 0)
    in_come = swap(in_give, "c")
    down_pieces, in_come = lax.optimization_barrier((down_pieces, in_come))
    down_sum = sum4(down_pieces).reshape(4, 80, D)
    down_pieces = spread4(down_sum, "z", z)
    inner, down_sum = lax.optimization_barrier((inner, down_sum))
    out_keep, out_give = mlp_out(inner, down_t)
    out_come = swap(out_give, "c")
    out_far = far_rows(out_keep, out_come)
    input_grad = input_back(core, hidden_grad, in_parts, in_come, tok, gain_one)
    gu_sum, input_grad, out_far = lax.optimization_barrier((gu_sum, input_grad, out_far))
    keep, give = halves(jnp.stack([yh]), gu_sum.reshape(56, 2 * FFP), down_pieces)
    out_away = swap(out_far, "yl")
    qkv_wparts, give, out_away, input_grad = lax.optimization_barrier(
        (qkv_wparts, give, out_away, input_grad)
    )
    packed_sum = part_sum(qkv_wparts)
    come = after(swap(give, "yh"), packed_sum)
    mixed = hidden + out_keep[:rows].astype(F32) + out_come[:rows].astype(F32)
    mixed = (mixed + out_away.astype(F32)).astype(BF)
    packed_sum = lax.all_to_all(packed_sum, ("yl", "c", "yh"), 0, 0, tiled=True)

    mlp_sum = (keep.astype(F32) + come.astype(F32)).astype(BF)
    mlp_pair = jnp.stack(ordered(mlp_sum, swap(mlp_sum, "yl"), yl))
    mlp_pair = lax.all_gather(mlp_pair, "c", axis=0).reshape(4, 28, 3 * FFP)
    qkv_own, out_own, *vec_own = finish(packed_sum)
    mlp_pair, qkv_own, mixed = lax.optimization_barrier((mlp_pair, qkv_own, mixed))
    gate_own, up_own, down_own = deal(mlp_pair)

    return (
        mixed.reshape(tokens.shape),
        input_grad.reshape(tokens.shape),
        vec_own[0].reshape(28),
        qkv_own,
        vec_own[2].reshape(32),
        vec_own[3].reshape(4),
        out_own,
        vec_own[1].reshape(28),
        gate_own,
        up_own,
        down_own,
    )


def solution(mesh):
    devices = mesh.devices.reshape(2, 2, 4, 4, 2)
    split = Mesh(devices, AXES)
    ctx, fsdp = ("yl", "c"), ("z", "x", "yh")
    rows = P(fsdp, None, ctx, None, None)
    in_specs = (
        rows,
        P(fsdp),
        P(fsdp, None),
        P(fsdp),
        P(fsdp),
        P(fsdp, None),
        P(fsdp),
        P(fsdp, None),
        P(fsdp, None),
        P(fsdp, None),
        rows,
    )
    out_specs = (
        rows,
        rows,
        P(fsdp),
        P(fsdp, None),
        P(fsdp),
        P(fsdp),
        P(fsdp, None),
        P(fsdp),
        P(fsdp, None),
        P(fsdp, None),
        P(fsdp, None),
    )
    return jax.shard_map(
        shards, mesh=split, in_specs=in_specs, out_specs=out_specs, check_vma=False
    )
```
